32 devices in a mesh: dp: 16 (over z, y, x), tensor: 2 (over core).
Axes of the slice: x: 2, y: 2, z: 4, core: 2. Of those that a mesh axis runs over, the one named last changes fastest.
Arguments:
- tokens: bfloat16 [32, 197, 512], P('dp'), may hold values from -6 to 6
- routes: int32 [2, 32, 197, 2], P(None, 'dp'), may hold values from 0 to 3, all different within a row; in each aligned block of 197 rows (0 to 196, 197 to 393, ..., all dimensions but the last counted through in order) at most 128 rows name the same one
- norm1_gain: bfloat16 [2, 512], P(None, 'dp'), may hold values from 0.5 to 1.5
- norm1_bias: bfloat16 [2, 512], P(None, 'dp'), may hold values from -1 to 1
- qkv_weight: bfloat16 [2, 512, 3, 512], P(None, 'dp', None, 'tensor'), may hold values from -0.25 to 0.25
- qv_bias: bfloat16 [2, 2, 512], P(None, None, ('tensor', 'dp')), may hold values from -1 to 1
- output_weight: bfloat16 [2, 512, 512], P(None, 'tensor', 'dp'), may hold values from -2 to 2
- output_bias: bfloat16 [2, 512], P(None, 'dp'), may hold values from -1 to 1
- norm2_gain: bfloat16 [2, 512], P(None, 'dp'), may hold values from 0.5 to 1.5
- norm2_bias: bfloat16 [2, 512], P(None, 'dp'), may hold values from -1 to 1
- router_weight: bfloat16 [2, 512, 4], P(None, 'dp'), may hold values from -0.1875 to 0.1875
- expert_in: bfloat16 [2, 4, 512, 2048], P(None, None, 'dp', 'tensor'), may hold values from -0.25 to 0.25
- expert_in_bias: bfloat16 [2, 4, 2048], P(None, None, ('tensor', 'dp')), may hold values from -1 to 1
- expert_out: bfloat16 [2, 4, 2048, 512], P(None, None, 'tensor', 'dp'), may hold values from -0.375 to 0.375
- expert_out_bias: bfloat16 [2, 4, 512], P(None, None, 'dp'), may hold values from -1 to 1
- grad_out: bfloat16 [32, 197, 512], P('dp'), may hold values from -6 to 6
Outputs:
- output: float32 [32, 197, 512], P('dp')
- grad_tokens: float32 [32, 197, 512], P('dp')
- grad_norm1_gain: float32 [2, 512], P(None, 'dp')
- grad_norm1_bias: float32 [2, 512], P(None, 'dp')
- grad_qkv_weight: float32 [2, 512, 3, 512], P(None, 'dp', None, 'tensor')
- grad_qv_bias: float32 [2, 2, 512], P(None, None, ('tensor', 'dp'))
- grad_output_weight: float32 [2, 512, 512], P(None, 'tensor', 'dp')
- grad_output_bias: float32 [2, 512], P(None, 'dp')
- grad_norm2_gain: float32 [2, 512], P(None, 'dp')
- grad_norm2_bias: float32 [2, 512], P(None, 'dp')
- grad_router_weight: float32 [2, 512, 4], P(None, 'dp')
- grad_expert_in: float32 [2, 4, 512, 2048], P(None, None, 'dp', 'tensor')
- grad_expert_in_bias: float32 [2, 4, 2048], P(None, None, ('tensor', 'dp'))
- grad_expert_out: float32 [2, 4, 2048, 512], P(None, None, 'tensor', 'dp')
- grad_expert_out_bias: float32 [2, 4, 512], P(None, None, 'dp')
The draws below stay inside these ranges and needn't reach their ends.
Inputs may be any that keep to these rules, and one draw needn't show every extreme that they name: `routes`: in each aligned block of 197 rows of one layer (one micro-batch of one index of dp) no expert is named by more than 128 rows, and in some block one expert is named by exactly 128; a token's two experts differ.
All inputs are finite; a program needn't handle non-finite values.
Results may differ from the reference program's by a relative error of at most 0.025.
Values may be sent and summed in bfloat16 or wider, within the bound.
No kernel may reach another device: no remote copies, remote signals or barrier semaphores. Data moves between devices by JAX's collectives and lax.ppermute only.
A program may use at most 256 MiB of HBM per device.

```python
import math
import jax
import jax.numpy as jnp
import numpy as np
from jax import lax

D = 512
HEADS = 8
HD = 64
FF = 2048
SEQ = 197
EXPERTS = 4
LAYERS = 2
IMG_MB = 1
CAP = 128
IMAGES = 32


def raised(entries, key, source, target, blocks, factor):
    owner, partner = [(jnp.arange(entries.shape[axis_at]) // (entries.shape[axis_at] // blocks)).reshape([-1 if axis == axis_at else 1 for axis in range(entries.ndim)]) for axis_at in (source, target)]
    chosen = jax.random.permutation(key, blocks)[partner]
    strong = (owner == chosen) | (owner == (partner + blocks // 2) % blocks)
    return jnp.where(strong, factor * entries, entries)


def steps_of(key, extent, cuts, low, high):
    level = 1.0
    for position, shards_of in cuts:
        draws = jax.random.uniform(jax.random.fold_in(jax.random.fold_in(key, 6), position), (shards_of,), jnp.float32, low / len(cuts), high / len(cuts))
        level = level * jnp.repeat(jnp.exp(draws), extent[position] // shards_of).reshape((-1,) + (1,) * (len(extent) - 1 - position))
    return level


def deal_out(key, own, number, rows, count, top, limit, lean):
    order = jax.random.permutation(key, count)
    packed, ordinary = portions_of(count, rows * top, limit, lean, True), portions_of(count, rows * top, limit, lean, False)
    places = jnp.arange(count)

    def named(lengths, rotation):
        used = int((lengths > 0).sum())
        fixed = max(1, used // 4)
        passed = fixed + (places - fixed + rotation * (used - fixed)) % max(1, count - fixed)
        return jnp.zeros((count,), jnp.int32).at[order[jnp.where(places < fixed, places, passed)]].set(jnp.asarray(lengths, jnp.int32))

    lengths = jnp.where(number % 4 == 0, named(packed, number // 4), named(ordinary, number - number // 4 - 1))
    mixed = jax.random.permutation(jax.random.fold_in(own, 3), count)
    donor, receiver = mixed[0:count // 2 * 2:2], mixed[1:count // 2 * 2:2]
    margin = jnp.minimum(lengths[donor] - 1, limit - lengths[receiver]) // 2
    margin = jnp.where((donor == order[0]) | (receiver == order[0]) | (lengths[receiver] == 0), 0, jnp.maximum(margin, 0))
    passed = jax.random.randint(jax.random.fold_in(own, 4), (count // 2,), 0, 1 << 20) % (margin + 1)
    lengths = lengths.at[donor].add(-passed).at[receiver].add(passed)
    items = jnp.searchsorted(jnp.cumsum(lengths), jnp.arange(rows * top), side="right").astype(jnp.int32)
    grid = items.reshape(top, rows).T
    grid = grid[jax.random.permutation(jax.random.fold_in(own, 1), rows)]
    rotation = jax.random.randint(jax.random.fold_in(own, 2), (rows, 1), 0, top)
    return jnp.take_along_axis(grid, (jnp.arange(top)[None, :] + rotation) % top, axis=1)


def portions_of(count, total, bound, slope, full):
    portions = [(1 << 20) // math.isqrt(standing ** slope) + 1 for standing in range(1, count + 1)]
    largest = bound if full else min(bound, max(-(-total // count), total * portions[0] // sum(portions)))
    least = 1 if total - largest >= count - 1 else 0
    holding, rest = [largest] + [least] * (count - 1), total - largest - least * (count - 1)
    while rest > 0:
        movable = [i for i in range(1, count) if holding[i] < largest] or [i for i in range(1, count) if holding[i] < bound]
        whole, remaining = sum([portions[i] for i in movable]), rest
        for i in movable:
            extra = min(bound - holding[i], max(1, remaining * portions[i] // whole), rest)
            holding[i] = holding[i] + extra
            rest = rest - extra
    return np.array(holding)


def noise(stream_key, extent, scale, bound, shards=(), kind=jnp.bfloat16):
    loudness = steps_of(stream_key, extent, shards, -0.22, 0.18) if shards else 1.0
    array = jax.random.normal(stream_key, extent, jnp.float32) * scale * loudness
    return jnp.minimum(jnp.maximum(array, -bound), bound).astype(kind)


def heavy_noise(key, dims, deviation, bound, split, heavy, held_as=jnp.bfloat16):
    values = deviation * jax.random.normal(key, dims, jnp.float32)
    if split:
        values = values * steps_of(key, dims, split, -0.22, 0.18)
    return jnp.clip(raised(values, jax.random.fold_in(key, 3), *heavy), -bound, bound).astype(held_as)


def setup_inputs(seed: int = 0) -> dict:
    splits = jax.random.split(jax.random.key(seed), 17)
    tokens = noise(splits[0], (IMAGES, SEQ, D), 1.0, 6.0, ((0, 16),))
    routes_keys = jax.random.split(jax.random.fold_in(splits[1], 1), LAYERS * IMAGES * SEQ // (IMG_MB * SEQ))
    routes_turns = jax.random.permutation(jax.random.fold_in(splits[1], 3), LAYERS * IMAGES * SEQ // (IMG_MB * SEQ))
    routes = jax.vmap(lambda own, number: deal_out(jax.random.fold_in(splits[1], 2), own, number, IMG_MB * SEQ, EXPERTS, 2, CAP, 0))(routes_keys, routes_turns).reshape((LAYERS, IMAGES, SEQ, 2))
    norm1_gain = jnp.clip(1.0 + 0.1 * jax.random.normal(splits[2], (LAYERS, D), jnp.float32), 0.5, 1.5).astype(jnp.bfloat16)
    norm1_bias = noise(splits[3], (LAYERS, D), 0.2, 1.0, ((1, 16),))
    qkv_weight = noise(splits[4], (LAYERS, D, 3, HEADS * HD), D ** -0.5, 0.25, ((1, 16), (3, 2)))
    qv_bias = noise(splits[5], (LAYERS, 2, HEADS * HD), 0.2, 1.0, ((2, 32),))
    output_weight = noise(splits[6], (LAYERS, HEADS * HD, D), (max(1, HEADS * HD * 3 // SEQ)) ** -0.5, 2.0, ((1, 2), (2, 16)))
    output_bias = noise(splits[7], (LAYERS, D), 0.2, 1.0, ((1, 16),))
    norm2_gain = jnp.clip(1.0 + 0.1 * jax.random.normal(splits[8], (LAYERS, D), jnp.float32), 0.5, 1.5).astype(jnp.bfloat16)
    norm2_bias = noise(splits[9], (LAYERS, D), 0.2, 1.0, ((1, 16),))
    router_weight = noise(splits[10], (LAYERS, D, EXPERTS), (2 * D) ** -0.5, 0.1875, ((1, 16),))
    expert_in = noise(splits[11], (LAYERS, EXPERTS, D, FF), D ** -0.5, 0.25, ((2, 16), (3, 2)))
    expert_in_bias = noise(splits[12], (LAYERS, EXPERTS, FF), 0.2, 1.0, ((2, 32),))
    expert_out = noise(splits[13], (LAYERS, EXPERTS, FF, D), (FF // 8) ** -0.5, 0.375, ((2, 2), (3, 16)))
    expert_out_bias = noise(splits[14], (LAYERS, EXPERTS, D), 0.2, 1.0, ((2, 16),))
    grad_out = heavy_noise(splits[15], (IMAGES, SEQ, D), 1.0, 6.0, ((0, 16),), (0, 2, 16, 2.0))
    return {"tokens": tokens, "routes": routes, "norm1_gain": norm1_gain, "norm1_bias": norm1_bias, "qkv_weight": qkv_weight, "qv_bias": qv_bias, "output_weight": output_weight, "output_bias": output_bias, "norm2_gain": norm2_gain, "norm2_bias": norm2_bias, "router_weight": router_weight, "expert_in": expert_in, "expert_in_bias": expert_in_bias, "expert_out": expert_out, "expert_out_bias": expert_out_bias, "grad_out": grad_out}


EPSILON = 1e-06
HIGHEST = lax.Precision.HIGHEST

@jax.custom_vjp
def low(v):
    return lax.optimization_barrier(v.astype(jnp.bfloat16)).astype(jnp.float32)

@jax.custom_vjp
def low_back(v):
    return v

def low_keep(v):
    return (low(v), None)

def low_pass(kept, grad):
    return (grad,)

def back_keep(v):
    return (v, None)

def back_low(kept, grad):
    return (low(grad),)
low.defvjp(low_keep, low_pass)
low_back.defvjp(back_keep, back_low)

def layer_norm(token_rows, gain, shift):
    center = token_rows - lax.optimization_barrier(jnp.mean(token_rows, axis=-1, keepdims=True))
    spread = lax.optimization_barrier(jnp.mean(center * center, axis=-1, keepdims=True))
    return center * lax.rsqrt(spread + EPSILON) * gain + shift

def gelu_exact(values):
    return jax.nn.gelu(values, approximate=False)

def one_layer(current, route_group, weights):
    gain_one, bias_one, qkv_matrix, qv_shift, out_matrix, out_shift, gain_two, bias_two, router_matrix, in_matrix, in_shift, exp_matrix, exp_shift = weights
    image_count, seq_length, feature_count = current.shape
    token_rows = current.reshape(image_count * seq_length, feature_count)
    normed = low(layer_norm(token_rows, gain_one, bias_one))
    projected = jnp.einsum('rd,dti->rti', normed, qkv_matrix, precision=HIGHEST)
    head_count = qkv_matrix.shape[-1] // HD
    head_shape = (image_count, seq_length, head_count, HD)
    query_heads = low(low_back(projected[:, 0] + qv_shift[0])).reshape(head_shape)
    key_heads = low(low_back(projected[:, 1])).reshape(head_shape)
    value_heads = low(low_back(projected[:, 2] + qv_shift[1])).reshape(head_shape)
    scores = low_back(jnp.einsum('gqhc,gkhc->ghqk', query_heads, key_heads, precision=HIGHEST) * HD ** (-0.5))
    att_weights = low(jax.nn.softmax(scores, axis=-1))
    mixed_heads = jnp.einsum('ghqk,gkhc->gqhc', att_weights, value_heads, precision=HIGHEST)
    mixed_heads = low(low_back(mixed_heads)).reshape(image_count * seq_length, head_count * HD)
    attended = low_back(jnp.dot(mixed_heads, out_matrix, precision=HIGHEST) + out_shift)
    middle = token_rows + attended
    normed_two = low(layer_norm(middle, gain_two, bias_two))
    logits = low_back(jnp.dot(normed_two, router_matrix, precision=HIGHEST))
    gate_probs = jax.nn.softmax(logits, axis=-1)
    chosen = (route_group.reshape(-1, 2)[:, :, None] == jnp.arange(in_matrix.shape[0])).astype(jnp.float32)
    combine = lax.optimization_barrier(jnp.sum(chosen, axis=1)) * gate_probs
    expert_pre = low_back(jnp.einsum('rd,edf->erf', normed_two, in_matrix, precision=HIGHEST) + in_shift[:, None, :])
    hidden = low(gelu_exact(expert_pre))
    expert_rows = low_back(jnp.einsum('erf,efd->erd', hidden, exp_matrix, precision=HIGHEST) + exp_shift[:, None, :])
    output = middle + jnp.einsum('re,erd->rd', combine, expert_rows, precision=HIGHEST)
    return output.reshape(image_count, seq_length, feature_count)

def reference(tokens, routes, norm1_gain, norm1_bias, qkv_weight, qv_bias, output_weight, output_bias, norm2_gain, norm2_bias, router_weight, expert_in, expert_in_bias, expert_out, expert_out_bias, grad_out):
    params = tuple((array_in.astype(jnp.float32) for array_in in (norm1_gain, norm1_bias, qkv_weight, qv_bias, output_weight, output_bias, norm2_gain, norm2_bias, router_weight, expert_in, expert_in_bias, expert_out, expert_out_bias)))
    groups = tokens.shape[0] // IMG_MB
    blocks = tokens.astype(jnp.float32).reshape(groups, IMG_MB, SEQ, D)
    route_blocks = jnp.moveaxis(routes.reshape(LAYERS, groups, IMG_MB, SEQ, 2), 1, 0)

    def forward(params, blocks):

        def group_step(carried, group_item):
            current, route_group = group_item
            for layer_index in range(LAYERS):
                current = one_layer(current, route_group[layer_index], tuple((array_in[layer_index] for array_in in params)))
            return (carried, current)
        carried, result = lax.scan(jax.checkpoint(group_step), jnp.zeros((), jnp.float32), (blocks, route_blocks))
        return result
    result, pullback = jax.vjp(forward, params, blocks)
    gradients, grad_blocks = pullback(grad_out.astype(jnp.float32).reshape(groups, IMG_MB, SEQ, D))
    return (result.reshape(tokens.shape), grad_blocks.reshape(tokens.shape), gradients[0], gradients[1], gradients[2], gradients[3], gradients[4], gradients[5], gradients[6], gradients[7], gradients[8], gradients[9], gradients[10], gradients[11], gradients[12])
```

```python
import jax
import jax.numpy as jnp
from jax import lax
from jax.experimental import pallas as pl
from jax.experimental.pallas import tpu as pltpu
from jax.sharding import PartitionSpec as P

D = 512
HD = 64
HALF = 256
FFH = 1024
SEQ = 197
SP = 208
EXPERTS = 4
CAP = 128
SLOTS = EXPERTS * CAP
PLANE = 4
SMALL = 16
EPSILON = 1e-06
SCALE = HD ** (-0.5)
MIB = 2**20
F32 = jnp.float32
BF16 = jnp.bfloat16


def params(mib):
    return pltpu.CompilerParams(vmem_limit_bytes=mib * MIB)


def cost(flops, bytes_accessed, transcendentals=0):
    return pl.CostEstimate(
        flops=int(flops), bytes_accessed=int(bytes_accessed), transcendentals=int(transcendentals)
    )


def shape(dims, dtype):
    return jax.ShapeDtypeStruct(dims, dtype)


def mm(a, b):
    return lax.dot_general(a, b, (((1,), (0,)), ((), ())), preferred_element_type=F32)


def mm_t(a, b):
    return lax.dot_general(a, b, (((1,), (1,)), ((), ())), preferred_element_type=F32)


def mm_tn(a, b):
    return lax.dot_general(a, b, (((0,), (0,)), ((), ())), preferred_element_type=F32)


def normalise(rows):
    center = rows - jnp.mean(rows, axis=-1, keepdims=True)
    inverse = lax.rsqrt(jnp.mean(center * center, axis=-1, keepdims=True) + EPSILON)
    return center * inverse, inverse


def norm_back(grad, hat, inverse, gain):
    scaled = grad * gain
    return inverse * (
        scaled
        - jnp.mean(scaled, axis=-1, keepdims=True)
        - hat * jnp.mean(scaled * hat, axis=-1, keepdims=True)
    )


def small_row(small, row, part):
    return small[row : row + 1, part * D : (part + 1) * D]


def router_rows(small):
    return [small_row(small, 3 + e // 2, e % 2) for e in range(EXPERTS)]


def select_columns(targets, j):
    lanes = lax.broadcasted_iota(jnp.int32, (SP, SLOTS), 1)
    return jnp.where(lanes == targets[:, j : j + 1], 1.0, 0.0).astype(BF16)


def select_rows(target_rows, j):
    subs = lax.broadcasted_iota(jnp.int32, (SLOTS, SP), 0)
    return jnp.where(subs == target_rows[j : j + 1, :], 1.0, 0.0).astype(BF16)


def chosen_of(targets, j):
    lanes = lax.broadcasted_iota(jnp.int32, (SP, EXPERTS), 1)
    return jnp.where(lanes == targets[:, 2 + j : 3 + j], 1.0, 0.0)


def gates_of(probs, targets):
    return [jnp.sum(chosen_of(targets, j) * probs, axis=-1, keepdims=True) for j in range(2)]


def attention_forward(rows, halves, targets, target_rows, outs, grad_rows):
    middle_ref, normed_ref, normed2_ref, qkv_ref, mixed_ref, log_ref, probs_ref = outs[:7]
    send_refs = outs[7:]
    small = halves[0][D : D + SMALL, :].astype(F32)
    hat, _ = normalise(rows)
    normed = (hat * small_row(small, 0, 0) + small_row(small, 0, 1)).astype(BF16)
    normed_ref[...] = normed
    attended = jnp.zeros((SP, D), F32)
    key_ok = lax.broadcasted_iota(jnp.int32, (SP, SP), 1) < SEQ
    logs = []
    for half in range(2):
        qkv = mm(normed, halves[half][0:D, 0 : 3 * HALF])
        shift = halves[half][D : D + SMALL, :][2:3, D : 2 * D].astype(F32)
        query = (qkv[:, 0:HALF] + shift[:, 0:HALF]).astype(BF16)
        key = qkv[:, HALF : 2 * HALF].astype(BF16)
        value = (qkv[:, 2 * HALF : 3 * HALF] + shift[:, HALF : 2 * HALF]).astype(BF16)
        qkv_ref[half] = jnp.concatenate([query, key, value], axis=1)
        mixed = []
        for head in range(HALF // HD):
            cut = slice(head * HD, (head + 1) * HD)
            scores = jnp.where(key_ok, mm_t(query[:, cut], key[:, cut]) * SCALE, -1e30)
            top = jnp.max(scores, axis=-1, keepdims=True)
            weight = jnp.exp(scores - top)
            total = jnp.sum(weight, axis=-1, keepdims=True)
            logs.append(top + jnp.log(total))
            low = (weight * (1.0 / total)).astype(BF16)
            mixed.append(mm(low, value[:, cut]).astype(BF16))
        mixed = jnp.concatenate(mixed, axis=1)
        mixed_ref[half] = mixed
        attended = attended + mm_t(mixed, halves[half][0:D, 3 * HALF : 4 * HALF])
    log_ref[...] = jnp.concatenate(logs, axis=1)
    middle = rows + attended + small_row(small, 1, 0)
    middle_ref[...] = middle
    hat2, _ = normalise(middle)
    normed2 = (hat2 * small_row(small, 1, 1) + small_row(small, 2, 0)).astype(BF16)
    normed2_ref[...] = normed2
    router = jnp.concatenate(router_rows(small) + [jnp.zeros((4, D), F32)], axis=0).astype(BF16)
    logits = mm_t(normed2, router)[:, 0:EXPERTS]
    weight = jnp.exp(logits - jnp.max(logits, axis=-1, keepdims=True))
    probs = weight / jnp.sum(weight, axis=-1, keepdims=True)
    probs_ref[...] = probs
    picks = [select_rows(target_rows, j) for j in range(2)]
    sent = mm(picks[0] + picks[1], normed2).astype(BF16)
    if grad_rows is None:
        for k in range(PLANE):
            send_refs[k][...] = sent[k * CAP : (k + 1) * CAP]
    else:
        gates = gates_of(probs, targets)
        grads = (
            mm(picks[0], (gates[0] * grad_rows).astype(BF16))
            + mm(picks[1], (gates[1] * grad_rows).astype(BF16))
        ).astype(BF16)
        for k in range(PLANE):
            send_refs[k][0] = sent[k * CAP : (k + 1) * CAP]
            send_refs[k][1] = grads[k * CAP : (k + 1) * CAP]


def first_forward_kernel(rows_ref, own_ref, other_ref, targets_ref, target_rows_ref, *outs):
    attention_forward(
        rows_ref[...].astype(F32),
        (own_ref, other_ref),
        targets_ref[...],
        target_rows_ref[...],
        outs,
        None,
    )


def combine(middle, probs, targets, slot_rows):
    gates = gates_of(probs, targets)
    picked = [mm(select_columns(targets, j), slot_rows) for j in range(2)]
    return middle + gates[0] * picked[0] + gates[1] * picked[1], picked


def last_forward_kernel(
    middle_ref,
    probs_ref,
    prior_targets_ref,
    f0,
    f1,
    f2,
    f3,
    grad_ref,
    own_ref,
    other_ref,
    targets_ref,
    target_rows_ref,
    rows_ref,
    *outs,
):
    slot_rows = jnp.concatenate([f0[...], f1[...], f2[...], f3[...]], axis=0)
    rows, _ = combine(middle_ref[...], probs_ref[...], prior_targets_ref[...], slot_rows)
    rows_ref[...] = rows
    attention_forward(
        rows,
        (own_ref, other_ref),
        targets_ref[...],
        target_rows_ref[...],
        outs,
        grad_ref[...].astype(F32),
    )


def forward_outs(pair):
    block = (2, CAP, D) if pair else (CAP, D)
    return [
        shape((SP, D), F32),
        shape((SP, D), BF16),
        shape((SP, D), BF16),
        shape((2, SP, 3 * HALF), BF16),
        shape((2, SP, HALF), BF16),
        shape((SP, 8), F32),
        shape((SP, EXPERTS), F32),
    ] + [shape(block, BF16)] * PLANE


ATT_COST = cost(1.2e9, 6e6, 4e5)


def first_forward(rows, own, other, targets, target_rows):
    return pl.pallas_call(
        first_forward_kernel,
        out_shape=forward_outs(False),
        compiler_params=params(32),
        cost_estimate=ATT_COST,
        name="attention_first",
    )(rows, own, other, targets, target_rows)


def last_forward(
    middle, probs, prior_targets, slot_blocks, grad, own, other, targets, target_rows
):
    return pl.pallas_call(
        last_forward_kernel,
        out_shape=[shape((SP, D), F32)] + forward_outs(True),
        compiler_params=params(32),
        cost_estimate=ATT_COST,
        name="attention_last",
    )(middle, probs, prior_targets, *slot_blocks, grad, own, other, targets, target_rows)


def backward_kernel(final, *refs):
    (
        grad_ref,
        f0,
        f1,
        f2,
        f3,
        d0,
        d1,
        d2,
        d3,
        rows_ref,
        middle_ref,
        normed2_ref,
        qkv_ref,
        mixed_ref,
        log_ref,
        probs_ref,
        targets_ref,
        own_ref,
        other_ref,
    ) = refs[:19]
    rest = refs[19:]
    if final:
        prior_probs_ref, prior_targets_ref, prior_target_rows_ref = rest[:3]
        rest = rest[3:]
    grad_rows_ref, grad_qkv_ref, grad_att_ref, small_keep_ref, small_send_ref = rest[:5]
    rest = rest[5:]
    halves = (own_ref, other_ref)
    small = own_ref[D : D + SMALL, :].astype(F32)
    grad = grad_ref[...].astype(F32)
    targets = targets_ref[...]
    probs = probs_ref[...]
    middle = middle_ref[...]
    slot_rows = jnp.concatenate([f0[...], f1[...], f2[...], f3[...]], axis=0)
    picks = [select_columns(targets, j) for j in range(2)]
    picked = [mm(picks[j], slot_rows) for j in range(2)]
    if final:
        gates = gates_of(probs, targets)
        rest[0][...] = middle + gates[0] * picked[0] + gates[1] * picked[1]
    grad_probs = jnp.zeros((SP, EXPERTS), F32)
    for j in range(2):
        grad_probs = grad_probs + chosen_of(targets, j) * jnp.sum(
            grad * picked[j], axis=-1, keepdims=True
        )
    grad_logits = probs * (grad_probs - jnp.sum(probs * grad_probs, axis=-1, keepdims=True))
    grad_logits = grad_logits.astype(BF16).astype(F32)
    slot_grads = jnp.concatenate([d0[...], d1[...], d2[...], d3[...]], axis=0)
    grad_normed2 = mm(picks[0] + picks[1], slot_grads)
    normed2 = normed2_ref[...].astype(F32)
    routers = router_rows(small)
    grad_router = []
    for e in range(EXPERTS):
        column = grad_logits[:, e : e + 1]
        grad_normed2 = grad_normed2 + column * routers[e]
        grad_router.append(jnp.sum(column * normed2, axis=0, keepdims=True))
    hat2, inverse2 = normalise(middle)
    grad_gain2 = jnp.sum(grad_normed2 * hat2, axis=0, keepdims=True)
    grad_bias2 = jnp.sum(grad_normed2, axis=0, keepdims=True)
    grad_middle = grad + norm_back(grad_normed2, hat2, inverse2, small_row(small, 1, 1))
    grad_att = grad_middle.astype(BF16)
    grad_att_ref[...] = grad_att
    grad_shift = jnp.sum(grad_att.astype(F32), axis=0, keepdims=True)
    key_ok = lax.broadcasted_iota(jnp.int32, (SP, SP), 1) < SEQ
    grad_normed = jnp.zeros((SP, D), F32)
    qv_rows = []
    for half in range(2):
        grad_mixed = mm(grad_att, halves[half][0:D, 3 * HALF : 4 * HALF]).astype(BF16)
        query = qkv_ref[half, :, 0:HALF]
        key = qkv_ref[half, :, HALF : 2 * HALF]
        value = qkv_ref[half, :, 2 * HALF : 3 * HALF]
        grad_q, grad_k, grad_v = [], [], []
        for head in range(HALF // HD):
            cut = slice(head * HD, (head + 1) * HD)
            at = half * (HALF // HD) + head
            scores = mm_t(query[:, cut], key[:, cut]) * SCALE - log_ref[:, at : at + 1]
            weight = jnp.exp(jnp.where(key_ok, scores, -1e30))
            grad_v.append(mm_tn(weight.astype(BF16), grad_mixed[:, cut]).astype(BF16))
            grad_weight = mm_t(grad_mixed[:, cut], value[:, cut])
            mean = jnp.sum(weight * grad_weight, axis=-1, keepdims=True)
            grad_scores = (weight * (grad_weight - mean)).astype(BF16)
            grad_q.append((mm(grad_scores, key[:, cut]) * SCALE).astype(BF16))
            grad_k.append((mm_tn(grad_scores, query[:, cut]) * SCALE).astype(BF16))
        grad_qkv = jnp.concatenate(grad_q + grad_k + grad_v, axis=1)
        grad_qkv_ref[half] = grad_qkv
        grad_normed = grad_normed + mm_t(grad_qkv, halves[half][0:D, 0 : 3 * HALF])
        sums = jnp.sum(grad_qkv.astype(F32), axis=0, keepdims=True)
        qv_rows.append(jnp.concatenate([sums[:, 0:HALF], sums[:, 2 * HALF : 3 * HALF]], axis=1))
    hat, inverse = normalise(rows_ref[...].astype(F32))
    grad_gain = jnp.sum(grad_normed * hat, axis=0, keepdims=True)
    grad_bias = jnp.sum(grad_normed, axis=0, keepdims=True)
    grad_rows = grad_middle + norm_back(grad_normed, hat, inverse, small_row(small, 0, 0))
    grad_rows_ref[...] = grad_rows
    for half, ref in enumerate((small_keep_ref, small_send_ref)):
        left = [grad_gain, grad_shift, grad_bias2, grad_router[0], grad_router[2]]
        right = [grad_bias, grad_gain2, qv_rows[half], grad_router[1], grad_router[3]]
        ref[...] = jnp.concatenate(
            [
                jnp.concatenate(left + [jnp.zeros((SMALL - 5, D), F32)], axis=0),
                jnp.concatenate(right + [jnp.zeros((SMALL - 5, D), F32)], axis=0),
            ],
            axis=1,
        )
    if final:
        prior_gates = gates_of(prior_probs_ref[...], prior_targets_ref[...])
        prior_rows = prior_target_rows_ref[...]
        sent = (
            mm(select_rows(prior_rows, 0), (prior_gates[0] * grad_rows).astype(BF16))
            + mm(select_rows(prior_rows, 1), (prior_gates[1] * grad_rows).astype(BF16))
        ).astype(BF16)
        for k in range(PLANE):
            rest[1 + k][...] = sent[k * CAP : (k + 1) * CAP]


def backward(final, grad, slot_blocks, grad_blocks, kept, own, other, prior):
    outs = [
        shape((SP, D), F32),
        shape((2, SP, 3 * HALF), BF16),
        shape((SP, D), BF16),
        shape((SMALL, 2 * D), F32),
        shape((SMALL, 2 * D), F32),
    ]
    if final:
        outs += [shape((SP, D), F32)] + [shape((CAP, D), BF16)] * PLANE

    def kernel(*refs):
        backward_kernel(final, *refs)

    return pl.pallas_call(
        kernel,
        out_shape=outs,
        compiler_params=params(40),
        cost_estimate=cost(2.6e9, 8e6, 4e5),
        name="attention_back_last" if final else "attention_back_first",
    )(grad, *slot_blocks, *grad_blocks, *kept, own, other, *(prior or ()))


def attention_grads_kernel(
    normed_ref, grad_qkv_ref, grad_att_ref, mixed_ref, small_keep_ref, small_send_ref, keep_ref, send_ref
):
    normed = normed_ref[...]
    grad_att = grad_att_ref[...]
    for half in range(2):
        inner = mm_tn(normed, grad_qkv_ref[half])
        outer = mm_tn(grad_att, mixed_ref[half])
        if half == 0:
            keep_ref[0:D, 0 : 3 * HALF] = inner
            keep_ref[0:D, 3 * HALF : 4 * HALF] = outer
            keep_ref[D : D + SMALL, :] = small_keep_ref[...]
        else:
            send_ref[0:D, 0 : 3 * HALF] = inner.astype(BF16)
            send_ref[0:D, 3 * HALF : 4 * HALF] = outer.astype(BF16)
            send_ref[D : D + SMALL, :] = small_send_ref[...].astype(BF16)


def attention_grads(normed, grad_qkv, grad_att, mixed, small_keep, small_send):
    return pl.pallas_call(
        attention_grads_kernel,
        out_shape=[shape((D + SMALL, 2 * D), F32), shape((D + SMALL, 2 * D), BF16)],
        compiler_params=params(24),
        cost_estimate=cost(5e8, 5e6),
        name="attention_grads",
    )(normed, grad_qkv, grad_att, mixed, small_keep, small_send)


CHUNK = 512


def gelu_parts(values):
    tail = 0.5 * (1.0 + lax.erf(values * 0.7071067811865476))
    density = jnp.exp(-0.5 * values * values) * 0.3989422804014327
    return values * tail, tail + values * density


def expert_bias(small, role):
    out_shift = jnp.zeros((1, D), F32)
    in_shift = jnp.zeros((1, FFH), F32)
    for e in range(EXPERTS):
        at = jnp.where(role == e, 1.0, 0.0)
        out_shift = out_shift + at * small_row(small, 5 + e // 2, e % 2)
        in_shift = in_shift + at * small[7 + e : 8 + e, :]
    return out_shift, in_shift


def expert_kernel(both, role_ref, *refs):
    blocks, (own_ref, other_ref, small_own_ref, small_other_ref), outs = (
        refs[:PLANE],
        refs[PLANE : PLANE + 4],
        refs[PLANE + 4 :],
    )
    role = role_ref[0]
    hidden_ref, slope_ref = outs[:2]
    if both:
        inputs = jnp.concatenate([block[0] for block in blocks], axis=0)
        grads = jnp.concatenate([block[1] for block in blocks], axis=0)
        result = jnp.zeros((SLOTS, D), F32)
        result_grad = jnp.zeros((SLOTS, D), F32)
    else:
        inputs = jnp.concatenate([block[...] for block in blocks], axis=0)
        result = jnp.zeros((SLOTS, D), F32)
    out_shift = None
    for half, (ref, small_ref) in enumerate(
        ((own_ref, small_own_ref), (other_ref, small_other_ref))
    ):
        shift, in_shift = expert_bias(small_ref[D : D + SMALL, :].astype(F32), role)
        if half == 0:
            out_shift = shift
        for chunk in range(FFH // CHUNK):
            cut = slice(chunk * CHUNK, (chunk + 1) * CHUNK)
            columns = slice(half * FFH + chunk * CHUNK, half * FFH + (chunk + 1) * CHUNK)
            hidden, slope = gelu_parts(mm(inputs, ref[0, :, cut]) + in_shift[:, cut])
            hidden = hidden.astype(BF16)
            hidden_ref[:, columns] = hidden
            result = result + mm_t(hidden, ref[1, :, cut])
            if both:
                grad_pre = (mm(grads, ref[1, :, cut]) * slope).astype(BF16)
                slope_ref[:, columns] = grad_pre
                result_grad = result_grad + mm_t(grad_pre, ref[0, :, cut])
            else:
                slope_ref[:, columns] = slope.astype(BF16)
    result = (result + out_shift).astype(BF16)
    for k in range(PLANE):
        if both:
            outs[2 + k][0] = result[k * CAP : (k + 1) * CAP]
            outs[2 + k][1] = result_grad[k * CAP : (k + 1) * CAP].astype(BF16)
        else:
            outs[2 + k][...] = result[k * CAP : (k + 1) * CAP]


def smem():
    return pl.BlockSpec(memory_space=pltpu.SMEM)


def vmem():
    return pl.BlockSpec(memory_space=pltpu.VMEM)


def expert_pass(both, role, blocks, own, other, small_own, small_other):
    block = (2, CAP, D) if both else (CAP, D)

    def kernel(*refs):
        expert_kernel(both, *refs)

    return pl.pallas_call(
        kernel,
        out_shape=[shape((SLOTS, 2 * FFH), BF16)] * 2 + [shape(block, BF16)] * PLANE,
        in_specs=[smem()] + [vmem()] * (PLANE + 4),
        compiler_params=params(48),
        cost_estimate=cost(4.3e9 if both else 2.2e9, 1e7, 1e6),
        name="expert_both" if both else "expert_forward",
    )(role, *blocks, own, other, small_own, small_other)


def expert_back_kernel(*refs):
    blocks, (slope_ref, own_ref, other_ref, grad_pre_ref), outs = (
        refs[:PLANE],
        refs[PLANE : PLANE + 4],
        refs[PLANE + 4 :],
    )
    grads = jnp.concatenate([block[...] for block in blocks], axis=0)
    result = jnp.zeros((SLOTS, D), F32)
    for half, ref in enumerate((own_ref, other_ref)):
        for chunk in range(FFH // CHUNK):
            cut = slice(chunk * CHUNK, (chunk + 1) * CHUNK)
            columns = slice(half * FFH + chunk * CHUNK, half * FFH + (chunk + 1) * CHUNK)
            grad_pre = (mm(grads, ref[1, :, cut]) * slope_ref[:, columns].astype(F32)).astype(BF16)
            grad_pre_ref[:, columns] = grad_pre
            result = result + mm_t(grad_pre, ref[0, :, cut])
    for k in range(PLANE):
        outs[k][...] = result[k * CAP : (k + 1) * CAP].astype(BF16)


def expert_back(blocks, slope, own, other):
    return pl.pallas_call(
        expert_back_kernel,
        out_shape=[shape((SLOTS, 2 * FFH), BF16)] + [shape((CAP, D), BF16)] * PLANE,
        compiler_params=params(40),
        cost_estimate=cost(2.2e9, 1e7),
        name="expert_back",
    )(*blocks, slope, own, other)


def expert_grads_kernel(pair, *refs):
    if pair:
        blocks, (hidden_ref, grad_pre_ref, keep_ref, send_ref) = refs[:PLANE], refs[PLANE:]
        inputs = jnp.concatenate([block[0] for block in blocks], axis=0)
        grads = jnp.concatenate([block[1] for block in blocks], axis=0)
    else:
        blocks, (hidden_ref, grad_pre_ref, keep_ref, send_ref) = refs[: 2 * PLANE], refs[2 * PLANE :]
        inputs = jnp.concatenate([block[...] for block in blocks[:PLANE]], axis=0)
        grads = jnp.concatenate([block[...] for block in blocks[PLANE:]], axis=0)
    out_shift = jnp.sum(grads.astype(F32), axis=0, keepdims=True)
    out_shift = jnp.concatenate([out_shift, jnp.zeros((1, FFH - D), F32)], axis=1)
    for half, ref in enumerate((keep_ref, send_ref)):
        shifts = []
        for chunk in range(FFH // CHUNK):
            cut = slice(chunk * CHUNK, (chunk + 1) * CHUNK)
            columns = slice(half * FFH + chunk * CHUNK, half * FFH + (chunk + 1) * CHUNK)
            grad_pre = grad_pre_ref[:, columns]
            ref[0:D, cut] = mm_tn(inputs, grad_pre).astype(ref.dtype)
            ref[D : 2 * D, cut] = mm_tn(grads, hidden_ref[:, columns]).astype(ref.dtype)
            shifts.append(jnp.sum(grad_pre.astype(F32), axis=0, keepdims=True))
        tail = [out_shift, jnp.concatenate(shifts, axis=1), jnp.zeros((SMALL - 2, FFH), F32)]
        ref[2 * D : 2 * D + SMALL, :] = jnp.concatenate(tail, axis=0).astype(ref.dtype)


def expert_grads(pair, blocks, hidden, grad_pre):
    def kernel(*refs):
        expert_grads_kernel(pair, *refs)

    return pl.pallas_call(
        kernel,
        out_shape=[shape((2 * D + SMALL, FFH), F32), shape((2 * D + SMALL, FFH), BF16)],
        compiler_params=params(40),
        cost_estimate=cost(2.2e9, 1.2e7),
        name="expert_grads",
    )(*blocks, hidden, grad_pre)


def build(dp):
    depth = dp // PLANE
    rows_each = D // dp

    def swap(x, mask):
        return lax.ppermute(x, "dp", [(i, i ^ mask) for i in range(dp)])

    def swap_core(x):
        return lax.ppermute(x, "tensor", [(0, 1), (1, 0)])

    def by_index(pieces, me):
        stacked = jnp.stack(pieces)
        return jnp.take(stacked, me ^ jnp.arange(len(pieces)), axis=0)

    def relative(array, me, axis):
        return jnp.take(array, me ^ jnp.arange(array.shape[axis]), axis=axis)

    def total(pieces):
        return sum(piece.astype(F32) for piece in pieces)

    def local(
        tokens,
        routes,
        norm1_gain,
        norm1_bias,
        qkv_weight,
        qv_bias,
        output_weight,
        output_bias,
        norm2_gain,
        norm2_bias,
        router_weight,
        expert_in,
        expert_in_bias,
        expert_out,
        expert_out_bias,
        grad_out,
    ):
        layers = routes.shape[0]
        me = lax.axis_index("dp")
        core = lax.axis_index("tensor")
        role = me % PLANE
        level = me // PLANE

        features = jnp.concatenate(
            [
                norm1_gain[:, None],
                norm1_bias[:, None],
                output_bias[:, None],
                norm2_gain[:, None],
                norm2_bias[:, None],
                router_weight.transpose(0, 2, 1),
                expert_out_bias,
            ],
            axis=1,
        )

        def placed(values, width):
            extent = values.shape[-1]
            spot = (
                jnp.arange(extent)[:, None] + me * extent == jnp.arange(width)[None, :]
            ).astype(BF16)
            return jnp.dot(values, spot, preferred_element_type=F32).astype(BF16)

        wide = placed(features, D)
        shifts = placed(qv_bias, HALF).reshape(layers, 1, D)
        inner = placed(expert_in_bias, FFH)
        small = jnp.concatenate(
            [
                jnp.concatenate([wide[:, 0:5], shifts, wide[:, 5:13]], axis=1).reshape(
                    layers, 7, 2 * D
                ),
                inner,
                jnp.zeros((layers, SMALL - 11, 2 * D), BF16),
            ],
            axis=1,
        )
        attention_shard = jnp.concatenate(
            [
                qkv_weight.reshape(layers, rows_each, 3 * HALF),
                output_weight.transpose(0, 2, 1),
            ],
            axis=2,
        )
        attention_shard = jnp.concatenate([attention_shard, small], axis=1)
        expert_shard = jnp.stack([expert_in, expert_out.transpose(0, 1, 3, 2)], axis=2)
        expert_shard = relative(expert_shard, role, 1)

        choice = lax.dynamic_index_in_dim(routes, core, axis=1, keepdims=False)
        hot = (choice[..., None] == jnp.arange(EXPERTS)).astype(BF16)
        any_hot = hot[:, :, 0] + hot[:, :, 1]
        below = jnp.tril(jnp.ones((SEQ, SEQ), BF16), -1)
        slot = jnp.einsum("ts,lse->lte", below, any_hot, preferred_element_type=F32)
        slot = jnp.sum(hot.astype(F32) * slot[:, :, None], axis=-1).astype(jnp.int32)
        target = (choice ^ role) * CAP + slot
        columns = jnp.pad(
            jnp.concatenate([target, choice], axis=-1),
            ((0, 0), (0, SP - SEQ), (0, 0)),
            constant_values=-1,
        )
        target_rows = columns[:, :, 0:2].transpose(0, 2, 1)
        pad = ((0, SP - SEQ), (0, 0))
        rows = jnp.pad(lax.dynamic_index_in_dim(tokens, core, axis=0, keepdims=False), pad)
        grad = jnp.pad(lax.dynamic_index_in_dim(grad_out, core, axis=0, keepdims=False), pad)
        role_word = role.astype(jnp.int32).reshape(1)

        def gather_attention(shard):
            pieces = [shard] + [swap(shard, PLANE * j) for j in range(1, depth)]
            body = by_index([piece[:rows_each] for piece in pieces], level)
            tail = total([piece[rows_each:] for piece in pieces]).astype(BF16)
            message = jnp.concatenate([body.reshape(-1, 2 * D), tail], axis=0)
            pieces = [message] + [swap(message, k) for k in range(1, PLANE)]
            count = depth * rows_each
            body = by_index(
                [piece[:count].reshape(depth, rows_each, 2 * D) for piece in pieces], role
            )
            body = body.transpose(1, 0, 2, 3).reshape(D, 2 * D)
            tail = total([piece[count:] for piece in pieces]).astype(BF16)
            own = jnp.concatenate([body, tail], axis=0)
            return own, swap_core(own)

        def gather_expert(shard):
            pieces = [shard[0]] + [swap(shard[k], k) for k in range(1, PLANE)]
            body = by_index(pieces, role).transpose(1, 0, 2, 3)
            body = body.reshape(2, PLANE * rows_each, FFH)
            pieces = [body] + [swap(body, PLANE * j) for j in range(1, depth)]
            own = by_index(pieces, level).transpose(1, 0, 2, 3).reshape(2, D, FFH)
            return own, swap_core(own)

        attention = [gather_attention(attention_shard[layer]) for layer in range(layers)]
        expert = [gather_expert(expert_shard[layer]) for layer in range(layers)]

        def exchange(blocks):
            return [blocks[0]] + [swap(blocks[k], k) for k in range(1, PLANE)]

        kept0 = first_forward(rows, *attention[0], columns[0], target_rows[0])
        blocks0 = exchange(kept0[7:])
        middle0, normed0, normed2_0, qkv0, mixed0, log0, probs0 = kept0[:7]
        small0 = attention[0]
        hidden0, slope0, *results = expert_pass(
            False, role_word, blocks0, *expert[0], *small0
        )
        slots0 = exchange(results)

        rows1, *kept1 = last_forward(
            middle0, probs0, columns[0], slots0, grad, *attention[1], columns[1], target_rows[1]
        )
        blocks1 = exchange(kept1[7:])
        middle1, normed1, normed2_1, qkv1, mixed1, log1, probs1 = kept1[:7]
        hidden1, grad_pre1, *results = expert_pass(
            True, role_word, blocks1, *expert[1], *attention[1]
        )
        pairs1 = exchange(results)
        expert_sums1 = expert_grads(True, blocks1, hidden1, grad_pre1)
        back1 = backward(
            True,
            grad,
            [pair[0] for pair in pairs1],
            [pair[1] for pair in pairs1],
            (rows1, middle1, normed2_1, qkv1, mixed1, log1, probs1, columns[1]),
            *attention[1],
            (probs0, columns[0], target_rows[0]),
        )
        grad_rows1, grad_qkv1, grad_att1, keep1, send1, output = back1[:6]
        grads0 = exchange(back1[6:])
        attention_sums1 = attention_grads(normed1, grad_qkv1, grad_att1, mixed1, keep1, send1)

        grad_pre0, *results = expert_back(grads0, slope0, *expert[0])
        slot_grads0 = exchange(results)
        expert_sums0 = expert_grads(False, blocks0 + grads0, hidden0, grad_pre0)
        grad_rows0, grad_qkv0, grad_att0, keep0, send0 = backward(
            False,
            grad_rows1,
            slots0,
            slot_grads0,
            (rows, middle0, normed2_0, qkv0, mixed0, log0, probs0, columns[0]),
            *attention[0],
            None,
        )
        attention_sums0 = attention_grads(normed0, grad_qkv0, grad_att0, mixed0, keep0, send0)

        def scatter_expert(keep, send):
            whole = keep + swap_core(send).astype(F32)
            tail = whole[2 * D :]
            body = whole[: 2 * D].reshape(2, depth, PLANE * rows_each, FFH)
            body = relative(body, level, 1)
            low = body.astype(BF16)
            pieces = []
            for j in range(1, depth):
                message = jnp.concatenate(
                    [low[:, j].reshape(-1, FFH), tail.astype(BF16)], axis=0
                )
                pieces.append(swap(message, PLANE * j))
            count = 2 * PLANE * rows_each
            body = body[:, 0].reshape(count, FFH) + total([piece[:count] for piece in pieces])
            tail = tail + total([piece[count:] for piece in pieces])
            body = relative(body.reshape(2, PLANE, rows_each, FFH), role, 1)
            low = body.astype(BF16)
            low_tail = tail.astype(BF16)
            count = 2 * rows_each
            pieces = [jnp.concatenate([body[:, 0].reshape(count, FFH), tail], axis=0)]
            for k in range(1, PLANE):
                message = jnp.concatenate([low[:, k].reshape(count, FFH), low_tail], axis=0)
                pieces.append(swap(message, k).astype(F32))
            return by_index(pieces, role)

        def scatter_attention(keep, send):
            whole = keep + swap_core(send).astype(F32)
            tail = whole[D:]
            body = relative(whole[:D].reshape(depth, PLANE, rows_each, 2 * D), role, 1)
            count = depth * rows_each
            pieces = []
            for k in range(1, PLANE):
                message = jnp.concatenate([body[:, k].reshape(count, 2 * D), tail], axis=0)
                pieces.append(swap(message.astype(BF16), k))
            tail = tail + total([piece[count:] for piece in pieces])
            body = body[:, 0].reshape(count, 2 * D) + total([piece[:count] for piece in pieces])
            body = relative(body.reshape(depth, rows_each, 2 * D), level, 0)
            pieces = []
            for j in range(1, depth):
                message = jnp.concatenate([body[j], tail], axis=0)
                pieces.append(swap(message.astype(BF16), PLANE * j))
            return jnp.concatenate([body[0], tail], axis=0) + total(pieces)

        expert_owned = jnp.stack(
            [scatter_expert(*expert_sums0), scatter_expert(*expert_sums1)]
        )
        attention_owned = jnp.stack(
            [scatter_attention(*attention_sums0), scatter_attention(*attention_sums1)]
        )

        def shard(values, width):
            return lax.dynamic_slice_in_dim(values, me * width, width, axis=values.ndim - 1)

        count = rows_each
        tails = attention_owned[:, count:].reshape(layers, 2 * SMALL, D)
        wide = shard(tails, count)
        grad_qv = shard(tails[:, 5].reshape(layers, 2, HALF), HALF // dp)
        expert_tail = expert_owned[:, :, 2 * count :]

        def both(values):
            mine = values[:SEQ][None]
            others = swap_core(values)[:SEQ][None]
            first = jnp.where(core == 0, mine, others)
            second = jnp.where(core == 0, others, mine)
            return jnp.concatenate([first, second], axis=0)

        return (
            both(output),
            both(grad_rows0),
            wide[:, 0],
            wide[:, 1],
            attention_owned[:, :count, : 3 * HALF].reshape(layers, count, 3, HALF),
            grad_qv,
            attention_owned[:, :count, 3 * HALF :].transpose(0, 2, 1),
            wide[:, 2],
            wide[:, 3],
            wide[:, 4],
            wide[:, 6:10].transpose(0, 2, 1),
            expert_owned[:, :, :count],
            shard(expert_tail[:, :, 1], FFH // dp),
            expert_owned[:, :, count : 2 * count].transpose(0, 1, 3, 2),
            shard(expert_tail[:, :, 0, :D], count),
        )

    return local


def solution(mesh):
    weights = (
        P(None, "dp"),
        P(None, "dp"),
        P(None, "dp", None, "tensor"),
        P(None, None, ("tensor", "dp")),
        P(None, "tensor", "dp"),
        P(None, "dp"),
        P(None, "dp"),
        P(None, "dp"),
        P(None, "dp", None),
        P(None, None, "dp", "tensor"),
        P(None, None, ("tensor", "dp")),
        P(None, None, "tensor", "dp"),
        P(None, None, "dp"),
    )
    images = P("dp", None, None)
    return jax.shard_map(
        build(mesh.shape["dp"]),
        mesh=mesh,
        in_specs=(images, P(None, "dp", None, None)) + weights + (images,),
        out_specs=(images, images) + weights,
        check_vma=False,
    )
```

```python
import jax
import jax.numpy as jnp
from jax import lax
from jax.experimental import pallas as pl
from jax.experimental.pallas import tpu as pltpu
from jax.sharding import PartitionSpec as P

D = 512
HD = 64
HALF = 256
FFH = 1024
SEQ = 197
SP = 208
EXPERTS = 4
CAP = 128
SLOTS = EXPERTS * CAP
PLANE = 4
SMALL = 16
EPSILON = 1e-06
SCALE = HD ** (-0.5)
MIB = 2**20
VMEM_MIB = 32
F32 = jnp.float32
BF16 = jnp.bfloat16


def call(kernel, out_shape, operands, name, after, through, scalars):
    inputs, outputs = len(operands), len(out_shape)

    def body(*refs):
        first = inputs + len(after) + len(through)
        kernel(*refs[:inputs], *refs[first : first + outputs])

    anywhere = pl.BlockSpec(memory_space=pl.ANY)
    whole = pl.BlockSpec(memory_space=pltpu.VMEM)
    return pl.pallas_call(
        body,
        out_shape=list(out_shape) + [shape(array.shape, array.dtype) for array in through],
        in_specs=[pl.BlockSpec(memory_space=pltpu.SMEM)] * scalars
        + [whole] * (inputs - scalars)
        + [anywhere] * (len(after) + len(through)),
        out_specs=[whole] * outputs + [anywhere] * len(through),
        input_output_aliases={
            inputs + len(after) + i: outputs + i for i in range(len(through))
        },
        compiler_params=pltpu.CompilerParams(vmem_limit_bytes=VMEM_MIB * MIB),
        cost_estimate=pl.CostEstimate(flops=1, bytes_accessed=1, transcendentals=0),
        name=name,
    )(*operands, *after, *through)


def shape(dims, dtype):
    return jax.ShapeDtypeStruct(dims, dtype)


def far_shape(dims, dtype):
    return pltpu.HBM(dims, dtype)


def far(array):
    return pltpu.with_memory_space_constraint(array, pltpu.HBM)


def all_far(arrays):
    return [far(array) for array in arrays]


def mm(a, b):
    return lax.dot_general(a, b, (((1,), (0,)), ((), ())), preferred_element_type=F32)


def mm_t(a, b):
    return lax.dot_general(a, b, (((1,), (1,)), ((), ())), preferred_element_type=F32)


def mm_tn(a, b):
    return lax.dot_general(a, b, (((0,), (0,)), ((), ())), preferred_element_type=F32)


def normalise(rows):
    center = rows - jnp.mean(rows, axis=-1, keepdims=True)
    inverse = lax.rsqrt(jnp.mean(center * center, axis=-1, keepdims=True) + EPSILON)
    return center * inverse, inverse


def norm_back(grad, hat, inverse, gain):
    scaled = grad * gain
    return inverse * (
        scaled
        - jnp.mean(scaled, axis=-1, keepdims=True)
        - hat * jnp.mean(scaled * hat, axis=-1, keepdims=True)
    )


def small_row(small, row, part):
    return small[row : row + 1, part * D : (part + 1) * D]


def router_rows(small):
    return [small_row(small, 3 + e // 2, e % 2) for e in range(EXPERTS)]


def select_columns(targets, j):
    lanes = lax.broadcasted_iota(jnp.int32, (SP, SLOTS), 1)
    return jnp.where(lanes == targets[:, j : j + 1], 1.0, 0.0).astype(BF16)


def select_rows(target_rows, j):
    subs = lax.broadcasted_iota(jnp.int32, (SLOTS, SP), 0)
    return jnp.where(subs == target_rows[j : j + 1, :], 1.0, 0.0).astype(BF16)


def chosen_of(targets, j):
    lanes = lax.broadcasted_iota(jnp.int32, (SP, EXPERTS), 1)
    return jnp.where(lanes == targets[:, 2 + j : 3 + j], 1.0, 0.0)


def gates_of(probs, targets):
    return [jnp.sum(chosen_of(targets, j) * probs, axis=-1, keepdims=True) for j in range(2)]


def attention_forward(rows, halves, targets, target_rows, outs, grad_rows):
    middle_ref, normed_ref, normed2_ref, qkv_ref, mixed_ref, log_ref, probs_ref = outs[:7]
    small_ref, send_refs = outs[7], outs[8:]
    small_ref[0] = halves[0][D : D + SMALL, :]
    small_ref[1] = halves[1][D : D + SMALL, :]
    small = halves[0][D : D + SMALL, :].astype(F32)
    hat, _ = normalise(rows)
    normed = (hat * small_row(small, 0, 0) + small_row(small, 0, 1)).astype(BF16)
    normed_ref[...] = normed
    attended = jnp.zeros((SP, D), F32)
    key_ok = lax.broadcasted_iota(jnp.int32, (SP, SP), 1) < SEQ
    logs = []
    for half in range(2):
        qkv = mm(normed, halves[half][0:D, 0 : 3 * HALF])
        shift = halves[half][D : D + SMALL, :][2:3, D : 2 * D].astype(F32)
        query = (qkv[:, 0:HALF] + shift[:, 0:HALF]).astype(BF16)
        key = qkv[:, HALF : 2 * HALF].astype(BF16)
        value = (qkv[:, 2 * HALF : 3 * HALF] + shift[:, HALF : 2 * HALF]).astype(BF16)
        qkv_ref[half] = jnp.concatenate([query, key, value], axis=1)
        mixed = []
        for head in range(HALF // HD):
            cut = slice(head * HD, (head + 1) * HD)
            scores = jnp.where(key_ok, mm_t(query[:, cut], key[:, cut]) * SCALE, -1e30)
            top = jnp.max(scores, axis=-1, keepdims=True)
            weight = jnp.exp(scores - top)
            total = jnp.sum(weight, axis=-1, keepdims=True)
            logs.append(top + jnp.log(total))
            low = (weight * (1.0 / total)).astype(BF16)
            mixed.append(mm(low, value[:, cut]).astype(BF16))
        mixed = jnp.concatenate(mixed, axis=1)
        mixed_ref[half] = mixed
        attended = attended + mm_t(mixed, halves[half][0:D, 3 * HALF : 4 * HALF])
    log_ref[...] = jnp.concatenate(logs, axis=1)
    middle = rows + attended + small_row(small, 1, 0)
    middle_ref[...] = middle
    hat2, _ = normalise(middle)
    normed2 = (hat2 * small_row(small, 1, 1) + small_row(small, 2, 0)).astype(BF16)
    normed2_ref[...] = normed2
    router = jnp.concatenate(router_rows(small) + [jnp.zeros((4, D), F32)], axis=0).astype(BF16)
    logits = mm_t(normed2, router)[:, 0:EXPERTS]
    weight = jnp.exp(logits - jnp.max(logits, axis=-1, keepdims=True))
    probs = weight / jnp.sum(weight, axis=-1, keepdims=True)
    probs_ref[...] = probs
    picks = [select_rows(target_rows, j) for j in range(2)]
    sent = mm(picks[0] + picks[1], normed2).astype(BF16)
    if grad_rows is None:
        for k in range(PLANE):
            send_refs[k][...] = sent[k * CAP : (k + 1) * CAP]
    else:
        gates = gates_of(probs, targets)
        grads = (
            mm(picks[0], (gates[0] * grad_rows).astype(BF16))
            + mm(picks[1], (gates[1] * grad_rows).astype(BF16))
        ).astype(BF16)
        for k in range(PLANE):
            send_refs[k][0] = sent[k * CAP : (k + 1) * CAP]
            send_refs[k][1] = grads[k * CAP : (k + 1) * CAP]


def first_forward_kernel(rows_ref, own_ref, other_ref, targets_ref, target_rows_ref, *outs):
    attention_forward(
        rows_ref[...].astype(F32),
        (own_ref, other_ref),
        targets_ref[...],
        target_rows_ref[...],
        outs,
        None,
    )


def combine(middle, probs, targets, slot_rows):
    gates = gates_of(probs, targets)
    picked = [mm(select_columns(targets, j), slot_rows) for j in range(2)]
    return middle + gates[0] * picked[0] + gates[1] * picked[1], picked


def last_forward_kernel(
    middle_ref,
    probs_ref,
    prior_targets_ref,
    f0,
    f1,
    f2,
    f3,
    grad_ref,
    own_ref,
    other_ref,
    targets_ref,
    target_rows_ref,
    rows_ref,
    *outs,
):
    slot_rows = jnp.concatenate([f0[...], f1[...], f2[...], f3[...]], axis=0)
    rows, _ = combine(middle_ref[...], probs_ref[...], prior_targets_ref[...], slot_rows)
    rows_ref[...] = rows
    attention_forward(
        rows,
        (own_ref, other_ref),
        targets_ref[...],
        target_rows_ref[...],
        outs,
        grad_ref[...].astype(F32),
    )


def forward_outs(pair):
    block = (2, CAP, D) if pair else (CAP, D)
    return [
        far_shape((SP, D), F32),
        far_shape((SP, D), BF16),
        far_shape((SP, D), BF16),
        far_shape((2, SP, 3 * HALF), BF16),
        far_shape((2, SP, HALF), BF16),
        far_shape((SP, 8), F32),
        far_shape((SP, EXPERTS), F32),
        shape((2, SMALL, 2 * D), BF16),
    ] + [shape(block, BF16)] * PLANE


def backward_kernel(final, *refs):
    grad_ref, f0, f1, f2, f3 = refs[:5]
    refs = refs[5:]
    if not final:
        d0, d1, d2, d3 = refs[:4]
        refs = refs[4:]
    (
        rows_ref,
        middle_ref,
        normed2_ref,
        qkv_ref,
        mixed_ref,
        log_ref,
        probs_ref,
        targets_ref,
        own_ref,
        other_ref,
    ) = refs[:10]
    rest = refs[10:]
    if final:
        prior_probs_ref, prior_targets_ref, prior_target_rows_ref = rest[:3]
        rest = rest[3:]
    grad_rows_ref, grad_qkv_ref, grad_att_ref, small_keep_ref, small_send_ref = rest[:5]
    rest = rest[5:]
    halves = (own_ref, other_ref)
    small = own_ref[D : D + SMALL, :].astype(F32)
    grad = grad_ref[...].astype(F32)
    targets = targets_ref[...]
    probs = probs_ref[...]
    middle = middle_ref[...]
    if final:
        slot_rows = jnp.concatenate([f0[0], f1[0], f2[0], f3[0]], axis=0)
        slot_grads = jnp.concatenate([f0[1], f1[1], f2[1], f3[1]], axis=0)
    else:
        slot_rows = jnp.concatenate([f0[...], f1[...], f2[...], f3[...]], axis=0)
        slot_grads = jnp.concatenate([d0[...], d1[...], d2[...], d3[...]], axis=0)
    picks = [select_columns(targets, j) for j in range(2)]
    picked = [mm(picks[j], slot_rows) for j in range(2)]
    if final:
        gates = gates_of(probs, targets)
        rest[0][...] = middle + gates[0] * picked[0] + gates[1] * picked[1]
    grad_probs = jnp.zeros((SP, EXPERTS), F32)
    for j in range(2):
        grad_probs = grad_probs + chosen_of(targets, j) * jnp.sum(
            grad * picked[j], axis=-1, keepdims=True
        )
    grad_logits = probs * (grad_probs - jnp.sum(probs * grad_probs, axis=-1, keepdims=True))
    grad_logits = grad_logits.astype(BF16).astype(F32)
    grad_normed2 = mm(picks[0] + picks[1], slot_grads)
    normed2 = normed2_ref[...].astype(F32)
    routers = router_rows(small)
    grad_router = []
    for e in range(EXPERTS):
        column = grad_logits[:, e : e + 1]
        grad_normed2 = grad_normed2 + column * routers[e]
        grad_router.append(jnp.sum(column * normed2, axis=0, keepdims=True))
    hat2, inverse2 = normalise(middle)
    grad_gain2 = jnp.sum(grad_normed2 * hat2, axis=0, keepdims=True)
    grad_bias2 = jnp.sum(grad_normed2, axis=0, keepdims=True)
    grad_middle = grad + norm_back(grad_normed2, hat2, inverse2, small_row(small, 1, 1))
    grad_att = grad_middle.astype(BF16)
    grad_att_ref[...] = grad_att
    grad_shift = jnp.sum(grad_att.astype(F32), axis=0, keepdims=True)
    key_ok = lax.broadcasted_iota(jnp.int32, (SP, SP), 1) < SEQ
    grad_normed = jnp.zeros((SP, D), F32)
    qv_rows = []
    for half in range(2):
        grad_mixed = mm(grad_att, halves[half][0:D, 3 * HALF : 4 * HALF]).astype(BF16)
        query = qkv_ref[half, :, 0:HALF]
        key = qkv_ref[half, :, HALF : 2 * HALF]
        value = qkv_ref[half, :, 2 * HALF : 3 * HALF]
        grad_q, grad_k, grad_v = [], [], []
        for head in range(HALF // HD):
            cut = slice(head * HD, (head + 1) * HD)
            at = half * (HALF // HD) + head
            scores = mm_t(query[:, cut], key[:, cut]) * SCALE - log_ref[:, at : at + 1]
            weight = jnp.exp(jnp.where(key_ok, scores, -1e30))
            grad_v.append(mm_tn(weight.astype(BF16), grad_mixed[:, cut]).astype(BF16))
            grad_weight = mm_t(grad_mixed[:, cut], value[:, cut])
            mean = jnp.sum(weight * grad_weight, axis=-1, keepdims=True)
            grad_scores = (weight * (grad_weight - mean)).astype(BF16)
            grad_q.append((mm(grad_scores, key[:, cut]) * SCALE).astype(BF16))
            grad_k.append((mm_tn(grad_scores, query[:, cut]) * SCALE).astype(BF16))
        grad_qkv = jnp.concatenate(grad_q + grad_k + grad_v, axis=1)
        grad_qkv_ref[half] = grad_qkv
        grad_normed = grad_normed + mm_t(grad_qkv, halves[half][0:D, 0 : 3 * HALF])
        sums = jnp.sum(grad_qkv.astype(F32), axis=0, keepdims=True)
        qv_rows.append(jnp.concatenate([sums[:, 0:HALF], sums[:, 2 * HALF : 3 * HALF]], axis=1))
    hat, inverse = normalise(rows_ref[...].astype(F32))
    grad_gain = jnp.sum(grad_normed * hat, axis=0, keepdims=True)
    grad_bias = jnp.sum(grad_normed, axis=0, keepdims=True)
    grad_rows = grad_middle + norm_back(grad_normed, hat, inverse, small_row(small, 0, 0))
    grad_rows_ref[...] = grad_rows
    for half, ref in enumerate((small_keep_ref, small_send_ref)):
        left = [grad_gain, grad_shift, grad_bias2, grad_router[0], grad_router[2]]
        right = [grad_bias, grad_gain2, qv_rows[half], grad_router[1], grad_router[3]]
        ref[...] = jnp.concatenate(
            [
                jnp.concatenate(left + [jnp.zeros((SMALL - 5, D), F32)], axis=0),
                jnp.concatenate(right + [jnp.zeros((SMALL - 5, D), F32)], axis=0),
            ],
            axis=1,
        )
    if final:
        prior_gates = gates_of(prior_probs_ref[...], prior_targets_ref[...])
        prior_rows = prior_target_rows_ref[...]
        sent = (
            mm(select_rows(prior_rows, 0), (prior_gates[0] * grad_rows).astype(BF16))
            + mm(select_rows(prior_rows, 1), (prior_gates[1] * grad_rows).astype(BF16))
        ).astype(BF16)
        for k in range(PLANE):
            rest[1 + k][...] = sent[k * CAP : (k + 1) * CAP]


def backward_last_kernel(*refs):
    backward_kernel(True, *refs)


def backward_first_kernel(*refs):
    backward_kernel(False, *refs)


def backward_outs(final):
    keep = far_shape if final else shape
    outs = [
        keep((SP, D), F32),
        shape((2, SP, 3 * HALF), BF16),
        shape((SP, D), BF16),
        keep((SMALL, 2 * D), F32),
        keep((SMALL, 2 * D), F32),
    ]
    if final:
        outs += [shape((SP, D), F32)] + [shape((CAP, D), BF16)] * PLANE
    return outs


def attention_grads_kernel(normed_ref, grad_qkv_ref, grad_att_ref, mixed_ref, *outs):
    normed = normed_ref[...]
    grad_att = grad_att_ref[...]
    for half, ref in enumerate(outs):
        ref[0:D, 0 : 3 * HALF] = mm_tn(normed, grad_qkv_ref[half]).astype(ref.dtype)
        ref[0:D, 3 * HALF : 4 * HALF] = mm_tn(grad_att, mixed_ref[half]).astype(ref.dtype)


PARTS = (slice(0, 384), slice(384, 768), slice(768, 1024))


def attention_grads_small_kernel(*refs):
    normed = refs[0][...]
    grad_qkv_ref, grad_att, mixed_ref, small = refs[1], refs[2][...], refs[3], refs[4:8]
    keep_ref, sends = refs[8], refs[9:]
    tails = [
        jnp.concatenate([small[half][0:8, :], small[2 + half][0:8, :]], axis=0)
        for half in range(2)
    ]
    keep_ref[0:D, 0 : 3 * HALF] = mm_tn(normed, grad_qkv_ref[0])
    keep_ref[0:D, 3 * HALF : 4 * HALF] = mm_tn(grad_att, mixed_ref[0])
    keep_ref[D : D + SMALL, :] = tails[0]
    for ref, cut in zip(sends, PARTS):
        if cut.stop <= 3 * HALF:
            ref[0:D, :] = mm_tn(normed, grad_qkv_ref[1, :, cut]).astype(BF16)
        else:
            ref[0:D, :] = mm_tn(grad_att, mixed_ref[1]).astype(BF16)
        ref[D : D + SMALL, :] = tails[1][:, cut].astype(BF16)


ATTENTION_SUMS = [far_shape((D + SMALL, 2 * D), F32)] + [
    shape((D + SMALL, cut.stop - cut.start), BF16) for cut in PARTS
]


CHUNK = 512


def gelu_parts(values):
    tail = 0.5 * (1.0 + lax.erf(values * 0.7071067811865476))
    density = jnp.exp(-0.5 * values * values) * 0.3989422804014327
    return values * tail, tail + values * density


def expert_bias(small, role):
    out_shift = jnp.zeros((1, D), F32)
    in_shift = jnp.zeros((1, FFH), F32)
    for e in range(EXPERTS):
        at = jnp.where(role == e, 1.0, 0.0)
        out_shift = out_shift + at * small_row(small, 5 + e // 2, e % 2)
        in_shift = in_shift + at * small[7 + e : 8 + e, :]
    return out_shift, in_shift


def expert_kernel(both, place_ref, *refs):
    blocks, (own_ref, other_ref, small_ref), outs = (
        refs[:PLANE],
        refs[PLANE : PLANE + 3],
        refs[PLANE + 3 :],
    )
    role = place_ref[1]
    hidden_ref, slope_ref = outs[:2]
    if both:
        inputs = jnp.concatenate([block[0] for block in blocks], axis=0)
        grads = jnp.concatenate([block[1] for block in blocks], axis=0)
        result = jnp.zeros((SLOTS, D), F32)
        result_grad = jnp.zeros((SLOTS, D), F32)
    else:
        inputs = jnp.concatenate([block[...] for block in blocks], axis=0)
        result = jnp.zeros((SLOTS, D), F32)
    out_shift = None
    for half, ref in enumerate((own_ref, other_ref)):
        shift, in_shift = expert_bias(small_ref[half].astype(F32), role)
        if half == 0:
            out_shift = shift
        for chunk in range(FFH // CHUNK):
            cut = slice(chunk * CHUNK, (chunk + 1) * CHUNK)
            columns = slice(half * FFH + chunk * CHUNK, half * FFH + (chunk + 1) * CHUNK)
            hidden, slope = gelu_parts(mm(inputs, ref[0, :, cut]) + in_shift[:, cut])
            hidden = hidden.astype(BF16)
            hidden_ref[:, columns] = hidden
            result = result + mm_t(hidden, ref[1, :, cut])
            if both:
                grad_pre = (mm(grads, ref[1, :, cut]) * slope).astype(BF16)
                slope_ref[:, columns] = grad_pre
                result_grad = result_grad + mm_t(grad_pre, ref[0, :, cut])
            else:
                slope_ref[:, columns] = slope.astype(BF16)
    result = (result + out_shift).astype(BF16)
    for k in range(PLANE):
        if both:
            outs[2 + k][0] = result[k * CAP : (k + 1) * CAP]
            outs[2 + k][1] = result_grad[k * CAP : (k + 1) * CAP].astype(BF16)
        else:
            outs[2 + k][...] = result[k * CAP : (k + 1) * CAP]


def expert_forward_kernel(*refs):
    expert_kernel(False, *refs)


def expert_both_kernel(*refs):
    expert_kernel(True, *refs)


def expert_outs(both):
    block = (2, CAP, D) if both else (CAP, D)
    kept = shape if both else far_shape
    return [kept((SLOTS, 2 * FFH), BF16)] * 2 + [shape(block, BF16)] * PLANE


def expert_back_kernel(*refs):
    blocks, (slope_ref, own_ref, other_ref, grad_pre_ref), outs = (
        refs[:PLANE],
        refs[PLANE : PLANE + 4],
        refs[PLANE + 4 :],
    )
    grads = jnp.concatenate([block[...] for block in blocks], axis=0)
    result = jnp.zeros((SLOTS, D), F32)
    for half, ref in enumerate((own_ref, other_ref)):
        for chunk in range(FFH // CHUNK):
            cut = slice(chunk * CHUNK, (chunk + 1) * CHUNK)
            columns = slice(half * FFH + chunk * CHUNK, half * FFH + (chunk + 1) * CHUNK)
            grad_pre = (mm(grads, ref[1, :, cut]) * slope_ref[:, columns].astype(F32)).astype(BF16)
            grad_pre_ref[:, columns] = grad_pre
            result = result + mm_t(grad_pre, ref[0, :, cut])
    for k in range(PLANE):
        outs[k][...] = result[k * CAP : (k + 1) * CAP].astype(BF16)


EXPERT_BACK = [shape((SLOTS, 2 * FFH), BF16)] + [shape((CAP, D), BF16)] * PLANE


def expert_grads_kernel(pair, *refs):
    if pair:
        blocks, (hidden_ref, grad_pre_ref, keep_ref, send_ref) = refs[:PLANE], refs[PLANE:]
        inputs = jnp.concatenate([block[0] for block in blocks], axis=0)
        grads = jnp.concatenate([block[1] for block in blocks], axis=0)
    else:
        blocks, (hidden_ref, grad_pre_ref, keep_ref, send_ref) = refs[: 2 * PLANE], refs[2 * PLANE :]
        inputs = jnp.concatenate([block[...] for block in blocks[:PLANE]], axis=0)
        grads = jnp.concatenate([block[...] for block in blocks[PLANE:]], axis=0)
    out_shift = jnp.sum(grads.astype(F32), axis=0, keepdims=True)
    out_shift = jnp.concatenate([out_shift, jnp.zeros((1, FFH - D), F32)], axis=1)
    for half, ref in enumerate((keep_ref, send_ref)):
        shifts = []
        for chunk in range(FFH // CHUNK):
            cut = slice(chunk * CHUNK, (chunk + 1) * CHUNK)
            columns = slice(half * FFH + chunk * CHUNK, half * FFH + (chunk + 1) * CHUNK)
            grad_pre = grad_pre_ref[:, columns]
            ref[0:D, cut] = mm_tn(inputs, grad_pre).astype(ref.dtype)
            ref[D : 2 * D, cut] = mm_tn(grads, hidden_ref[:, columns]).astype(ref.dtype)
            shifts.append(jnp.sum(grad_pre.astype(F32), axis=0, keepdims=True))
        tail = [out_shift, jnp.concatenate(shifts, axis=1), jnp.zeros((SMALL - 2, FFH), F32)]
        ref[2 * D : 2 * D + SMALL, :] = jnp.concatenate(tail, axis=0).astype(ref.dtype)


def expert_grads_pair_kernel(*refs):
    expert_grads_kernel(True, *refs)


def expert_grads_single_kernel(*refs):
    expert_grads_kernel(False, *refs)


EXPERT_SUMS = [shape((2 * D + SMALL, FFH), F32), shape((2 * D + SMALL, FFH), BF16)]


def spot_of(level, role):
    return role + PLANE * level


def rows_at(index, size, base=0):
    return pl.ds(base + pl.multiple_of(index * size, size), size)


def one_hot(me, extent, width, dtype=BF16):
    row = lax.broadcasted_iota(jnp.int32, (extent, width), 0)
    column = lax.broadcasted_iota(jnp.int32, (extent, width), 1)
    return jnp.where(row + me * extent == column, 1.0, 0.0).astype(dtype)


def pack_shard(layer, rows, me, refs, shard_ref):
    (gain1, bias1, shift, gain2, bias2, router, out_bias, qv, in_bias, qkv, output) = refs
    vectors = [ref[layer : layer + 1, :].astype(F32) for ref in (gain1, bias1, shift, gain2, bias2)]
    vectors = jnp.concatenate(vectors + [out_bias[layer].astype(F32)], axis=0)
    place = one_hot(me, rows, D)
    wide = mm(vectors.astype(BF16), place)
    router = mm(router[layer], place)
    shifts = mm(qv[layer], one_hot(me, qv.shape[2], HALF))
    shifts = jnp.concatenate([shifts[0:1], shifts[1:2]], axis=1)
    inner = mm(in_bias[layer], one_hot(me, in_bias.shape[2], FFH))
    left = [wide[0:1], wide[2:3], wide[4:5], router[0:1], router[2:3], wide[5:6], wide[7:8]]
    right = [wide[1:2], wide[3:4], shifts, router[1:2], router[3:4], wide[6:7], wide[8:9]]
    small = jnp.concatenate(
        [jnp.concatenate(left, axis=0), jnp.concatenate(right, axis=0)], axis=1
    )
    small = jnp.concatenate([small, inner, jnp.zeros((SMALL - 11, 2 * D), F32)], axis=0)
    shard_ref[rows : rows + SMALL, :] = small.astype(BF16)
    for part in range(3):
        shard_ref[0:rows, part * HALF : (part + 1) * HALF] = qkv[layer, part]
    shard_ref[0:rows, 3 * HALF : 4 * HALF] = output[layer]


def pack_kernel(rows, place_ref, *refs):
    first_ref, last_ref = refs[13:15]
    role = place_ref[1]
    expert_in, expert_out = refs[11:13]
    for layer in range(2):
        for k, ref in enumerate(refs[15 + layer * PLANE : 15 + (layer + 1) * PLANE]):
            ref[0:rows, :] = expert_in[layer, role ^ k]
            ref[rows : 2 * rows, :] = expert_out[layer, role ^ k]
    pack_shard(0, rows, place_ref[0], refs[:11], first_ref)
    pack_shard(1, rows, place_ref[0], refs[:11], last_ref)


def stack_attention_kernel(rows, place_ref, *refs):
    pieces, out_ref = refs[:-1], refs[-1]
    high = place_ref[3]
    tail = jnp.zeros((SMALL, 2 * D), F32)
    for j, piece in enumerate(pieces):
        out_ref[rows_at(high ^ j, rows), :] = piece[0:rows, :]
        tail = tail + piece[rows : rows + SMALL, :].astype(F32)
    out_ref[len(pieces) * rows : len(pieces) * rows + SMALL, :] = tail.astype(BF16)


def join_attention_kernel(rows, depth, place_ref, *refs):
    pieces, out_ref = refs[:-1], refs[-1]
    low = place_ref[4]
    tail = jnp.zeros((SMALL, 2 * D), F32)
    for k, piece in enumerate(pieces):
        for high in range(depth):
            out_ref[rows_at(high * 4 + (low ^ k), rows), :] = piece[
                high * rows : (high + 1) * rows, :
            ]
        tail = tail + piece[depth * rows : depth * rows + SMALL, :].astype(F32)
    out_ref[D : D + SMALL, :] = tail.astype(BF16)


def join_gathered_kernel(rows, pieces_ref, out_ref):
    tail = jnp.zeros((SMALL, 2 * D), F32)
    for at in range(D // rows):
        piece = pieces_ref.at[at]
        out_ref[at * rows : (at + 1) * rows, :] = piece[0:rows, :]
        tail = tail + piece[rows : rows + SMALL, :].astype(F32)
    out_ref[D : D + SMALL, :] = tail.astype(BF16)


def join_plane_kernel(rows, place_ref, *refs):
    pieces, outs = refs[:PLANE], refs[PLANE:]
    for k, piece in enumerate(pieces):
        for out_ref in outs:
            out_ref[rows_at(place_ref[1] ^ k, 2 * rows), :] = piece[...]


def join_levels_kernel(rows, place_ref, *refs):
    pieces, out_ref = refs[:-1], refs[-1]
    for j, piece in enumerate(pieces):
        for role in range(PLANE):
            at = rows_at(spot_of(place_ref[2] ^ j, role), rows)
            for part in range(2):
                first = (2 * role + part) * rows
                out_ref[part, at, :] = piece[first : first + rows, :]


def split_levels_kernel(
    rows, depth, keep_ref, got_ref, att_keep_ref, att_got_ref, out_ref
):
    block = PLANE * rows
    low = slice(2 * D, 2 * D + SMALL)
    first = 2 * block + SMALL
    tail = (keep_ref[low, :].astype(F32) + got_ref[low, :].astype(F32)).astype(BF16)
    for level in range(depth):
        for part in range(2):
            at = slice(part * D + level * block, part * D + (level + 1) * block)
            out_ref[level, part * block : (part + 1) * block, :] = (
                keep_ref[at, :].astype(F32) + got_ref[at, :].astype(F32)
            ).astype(BF16)
        out_ref[level, 2 * block : first, :] = tail
        at = slice(level * block, (level + 1) * block)
        out_ref[level, first : first + block, :] = (
            att_keep_ref[at, :].astype(F32) + att_got_ref[at, :].astype(F32)
        ).astype(BF16)


def spread_last_kernel(rows, place_ref, got_ref, *outs):
    block = PLANE * rows
    first = 2 * rows + SMALL
    for k, out in enumerate(outs):
        role = place_ref[1] ^ k
        for part in range(2):
            out[part * rows : (part + 1) * rows, :] = got_ref[
                rows_at(role, rows, part * block), :
            ]
        out[2 * rows : first, :] = got_ref[2 * block : 2 * block + SMALL, :]
        out[first : first + rows, :] = got_ref[rows_at(role, rows, 2 * block + SMALL), :]


def split_expert_kernel(rows, place_ref, keep_ref, got_ref, own_ref, far_ref, near_ref, next_ref):
    block = PLANE * rows
    tail = keep_ref[2 * D : 2 * D + SMALL, :] + got_ref[2 * D : 2 * D + SMALL, :].astype(F32)
    for j, ref in ((3, far_ref), (1, near_ref), (2, next_ref), (0, own_ref)):
        for part in range(2):
            for role in range(PLANE):
                at = rows_at(spot_of(place_ref[2] ^ j, role), rows, part * D)
                first = part * block + role * rows
                ref[first : first + rows, :] = (
                    keep_ref[at, :] + got_ref[at, :].astype(F32)
                ).astype(ref.dtype)
        if j != 1:
            ref[2 * block : 2 * block + SMALL, :] = tail.astype(ref.dtype)


def add_kernel(own_ref, got_ref, out_ref):
    out_ref[...] = (own_ref[...].astype(F32) + got_ref[...].astype(F32)).astype(BF16)


def spread_expert_kernel(rows, place_ref, own_ref, far_ref, near_ref, next_ref, *outs):
    role = place_ref[1]
    block = PLANE * rows
    base = 2 * block
    tail = own_ref[base : base + SMALL, :] + far_ref[base : base + SMALL, :].astype(F32)
    tail = tail + next_ref[base : base + SMALL, :].astype(F32)
    for k, out in enumerate(outs):
        for part in range(2):
            at = rows_at(role ^ k, rows, part * block)
            out[part * rows : (part + 1) * rows, :] = (
                own_ref[at, :] + near_ref[at, :].astype(F32) + next_ref[at, :].astype(F32)
            ).astype(BF16)
        out[2 * rows : 2 * rows + SMALL, :] = tail.astype(BF16)


def split_attention_kernel(rows, depth, place_ref, keep_ref, *refs):
    gots, outs = refs[: len(PARTS)], refs[len(PARTS) :]
    low = place_ref[4]
    for got_ref, cut in zip(gots, PARTS):
        tail = keep_ref[D : D + SMALL, cut] + got_ref[D : D + SMALL, :].astype(F32)
        for k, out in enumerate(outs):
            for high in range(depth):
                at = rows_at(high * 4 + (low ^ k), rows)
                out[high * rows : (high + 1) * rows, cut] = (
                    keep_ref[at, cut] + got_ref[at, :].astype(F32)
                ).astype(out.dtype)
            out[depth * rows : depth * rows + SMALL, cut] = tail.astype(out.dtype)


def spread_attention_kernel(rows, depth, place_ref, *refs):
    pieces, (keep_ref, send_ref) = refs[:PLANE], refs[PLANE:]
    high = place_ref[3]
    base = depth * rows

    def summed(at):
        total = pieces[0][at, :]
        for piece in pieces[1:]:
            total = total + piece[at, :].astype(F32)
        return total

    tail = summed(slice(base, base + SMALL))
    for ref, flip in ((keep_ref, 0), (send_ref, 1)):
        for at in range(2):
            ref[at * rows : (at + 1) * rows, :] = summed(
                rows_at(high ^ (flip + 2 * at), rows)
            ).astype(ref.dtype)
        ref[2 * rows : 2 * rows + SMALL, :] = tail.astype(ref.dtype)


def halve_attention_kernel(rows, own_ref, got_ref, keep_ref, send_ref):
    total = own_ref[...] + got_ref[...].astype(F32)
    tail = total[2 * rows : 2 * rows + SMALL]
    for ref, at in ((keep_ref, 0), (send_ref, rows)):
        ref[0:rows, :] = total[at : at + rows].astype(ref.dtype)
        ref[rows : rows + SMALL, :] = tail.astype(ref.dtype)


def exact(a, b):
    return lax.dot_general(
        a, b, (((1,), (1,)), ((), ())), precision=lax.Precision.HIGHEST, preferred_element_type=F32
    )


def own_attention(rows, me, first, tail, last, outs):
    gain1, bias1, qkv, qv, output, shift, gain2, bias2, router = outs
    for layer, body in enumerate((first, last)):
        for part in range(3):
            qkv[layer, part] = body[:, part * HALF : (part + 1) * HALF]
        output[layer] = body[:, 3 * HALF : 4 * HALF]
        small = tail[8 * layer : 8 * layer + 8]
        left = exact(small[:, 0:D], one_hot(me, rows, D, F32))
        right = exact(small[:, D : 2 * D], one_hot(me, rows, D, F32))
        for ref, values, row in (
            (gain1, left, 0),
            (bias1, right, 0),
            (shift, left, 1),
            (gain2, right, 1),
            (bias2, left, 2),
        ):
            ref[layer : layer + 1, :] = values[row : row + 1]
        for e in range(EXPERTS):
            values = (left, right)[e % 2]
            router[layer, e : e + 1, :] = values[3 + e // 2 : 4 + e // 2]
        width = qv.shape[2]
        for part in range(2):
            values = exact(
                small[:, D + part * HALF : D + (part + 1) * HALF], one_hot(me, width, HALF, F32)
            )
            qv[layer, part : part + 1, :] = values[2:3]


def own_attention_kernel(rows, place_ref, *refs):
    pieces, lasts, outs = refs[:2], refs[2 : 2 + PLANE], refs[2 + PLANE :]
    last = jnp.zeros((rows, 2 * D), F32)
    for ref in lasts:
        last = last + ref[2 * rows + SMALL : 3 * rows + SMALL, :].astype(F32)
    total = pieces[0][...]
    for piece in pieces[1:]:
        total = total + piece[...].astype(F32)
    own_attention(
        rows,
        place_ref[0],
        total[0:rows],
        total[rows : rows + SMALL],
        last,
        outs,
    )


def own_experts_kernel(rows, place_ref, *refs):
    pieces = refs[: 2 * PLANE]
    inner_ref, in_bias_ref, outer_ref, out_bias_ref = refs[2 * PLANE :]
    me, role = place_ref[0], place_ref[1]
    in_place = one_hot(me, in_bias_ref.shape[2], FFH)
    out_place = one_hot(me, rows, D)
    for layer in range(2):
        for k in range(PLANE):
            piece = pieces[layer * PLANE + k]
            expert = role ^ k
            inner_ref[layer, expert] = piece[0:rows, :].astype(F32)
            outer_ref[layer, expert] = piece[rows : 2 * rows, :].astype(F32)
            tail = piece[2 * rows : 2 * rows + SMALL, :]
            out_bias_ref[layer, pl.ds(expert, 1), :] = mm_t(tail[:, 0:D], out_place)[0:1]
            in_bias_ref[layer, pl.ds(expert, 1), :] = mm_t(tail, in_place)[1:2]


class Order:
    def __init__(self, place):
        self.last = ()
        self.place = place

    def run(self, kernel, out_shape, operands, name, fixed=(), place=True, through=()):
        def body(*refs):
            kernel(*fixed, *refs)

        if place:
            operands = (self.place, *operands)
        outs = list(call(body, out_shape, operands, name, self.last, through, int(place)))
        sized = outs[: len(out_shape)]
        self.last = (min(sized, key=lambda out: out.size * out.dtype.itemsize),)
        return outs

    def gate(self, through):
        def kernel(place_ref, out_ref):
            out_ref[...] = jnp.zeros_like(out_ref)

        return self.run(kernel, [shape((8, 128), F32)], (), "gate", through=through)[1:]

    def main(self, kernel, out_shape, operands, name, through=(), place=False):
        outs = self.run(kernel, out_shape, operands, name, (), place, through)
        count = len(out_shape)
        return outs[:count], outs[count:]


class Moves:
    def __init__(self, dp, order, me, role, level):
        self.dp, self.order = dp, order
        self.me, self.role, self.level = me, role, level
        self.depth, self.rows = dp // PLANE, D // dp

    def swap(self, x, mask):
        return lax.ppermute(x, "dp", [(i, i ^ mask) for i in range(self.dp)])

    def swap_core(self, x):
        return lax.ppermute(x, "tensor", [(0, 1), (1, 0)])

    def to_role(self, x, k):
        return self.swap(x, spot_of(0, k))

    def to_level(self, x, j):
        return self.swap(x, spot_of(j, 0))

    def exchange(self, blocks):
        return [blocks[0]] + [self.to_role(blocks[k], k) for k in range(1, PLANE)]


class FastMoves(Moves):
    def one(self, *args, **kwargs):
        return self.order.run(*args, **kwargs)[0]

    def begin(self, weights):
        rows = self.rows
        outs = [shape((rows + SMALL, 2 * D), BF16)] * 2
        outs += [shape((2 * rows, FFH), BF16)] * (2 * PLANE)
        first, last, *sends = self.order.run(
            pack_kernel, outs, all_far(weights), "pack", (rows,)
        )
        exp0 = self.exchange(sends[:PLANE])
        att0 = [first] + [self.swap(first, 4 * j) for j in range(1, self.depth)]
        return att0, exp0, lax.all_gather(last, "dp"), sends[PLANE:]

    def groups(self, index):
        firsts = {}
        for level in range(self.depth):
            for role in range(PLANE):
                key = level if index == 0 else role
                firsts.setdefault(key, []).append(spot_of(level, role))
        return list(firsts.values())

    def plane0(self, pieces):
        out = [shape((2 * PLANE * self.rows, FFH), BF16)]
        own = self.one(join_plane_kernel, out, pieces, "join_plane", (self.rows,))
        return [own, self.to_level(own, 1), self.to_level(own, 2)]

    def stack0(self, pieces):
        out = [shape((self.depth * self.rows + SMALL, 2 * D), BF16)]
        message = self.one(stack_attention_kernel, out, pieces, "stack_attention", (self.rows,))
        return [message] + [self.swap(message, k) for k in range(1, 4)]

    def join0(self, pieces, exp0, exp1):
        out = [far_shape((D + SMALL, 2 * D), BF16)]
        fixed = (self.rows, self.depth)
        own, near, next_, *sends = self.order.run(
            join_attention_kernel,
            out,
            pieces,
            "join_attention",
            fixed,
            through=[*exp0[1:3], *exp1[1:]],
        )
        exp0 = [exp0[0], near, next_, self.to_level(next_, 1)]
        return (own, self.swap_core(own)), exp0, self.exchange([exp1[0], *sends])

    def plane1(self, pieces):
        out = [shape((2 * PLANE * self.rows, FFH), BF16)] * 2
        return self.order.run(join_plane_kernel, out, pieces, "join_plane", (self.rows,))

    def forward(self, piece):
        return self.to_level(piece, 1)

    def join_last(self, gathered):
        out = [far_shape((D + SMALL, 2 * D), BF16)]
        own = self.one(
            join_gathered_kernel, out, (gathered,), "join_gathered", (self.rows,), False
        )
        return own, self.swap_core(own)

    def join_levels(self, pieces, through=()):
        out = [far_shape((2, D, FFH), BF16)]
        own, *through = self.order.run(
            join_levels_kernel, out, all_far(pieces), "join_levels", (self.rows,), through=through
        )
        return (own, self.swap_core(own)), through

    def last_attention_1(self, operands):
        (keep, send), _ = self.order.main(
            attention_grads_kernel,
            [shape((D, 2 * D), BF16)] * 2,
            operands,
            "attention_grads1",
        )
        return keep, self.swap_core(send)

    def last_expert_1(self, operands):
        (keep, send), _ = self.order.main(
            expert_grads_pair_kernel, EXPERT_SUMS, operands, "expert_grads1"
        )
        return keep, self.swap_core(send)

    def last_sums_1(self, expert, attention):
        count = 3 * PLANE * self.rows + SMALL
        out = [shape((self.depth, count, FFH), BF16)]
        sums = self.one(
            split_levels_kernel,
            out,
            (far(expert[0]), *expert[1:], *attention),
            "split_levels",
            (self.rows, self.depth),
            False,
        )
        return lax.psum_scatter(
            sums, "dp", scatter_dimension=0, axis_index_groups=self.groups(1)
        )

    def last_sums_2(self, got):
        outs = [shape((3 * self.rows + SMALL, FFH), BF16)] * PLANE
        pieces = self.exchange(
            self.order.run(spread_last_kernel, outs, (got,), "spread_last", (self.rows,))
        )
        return pieces, pieces

    def expert_sum_2(self, keep, got, through=()):
        count = 2 * PLANE * self.rows
        outs = [
            far_shape((count + SMALL, FFH), F32),
            shape((count + SMALL, FFH), BF16),
            shape((count, FFH), BF16),
            far_shape((count + SMALL, FFH), BF16),
        ]
        own, third, near, next_, *through = self.order.run(
            split_expert_kernel, outs, (keep, got), "split_expert", (self.rows,), through=through
        )
        return [own, self.to_level(third, 1), self.to_level(near, 1), next_], through

    def expert_sum_3(self, state):
        own, third, near, next_ = state
        message = self.one(
            add_kernel,
            [shape(third.shape, BF16)],
            (far(next_), far(third)),
            "add_expert",
            place=False,
        )
        return [own, third, near, self.to_level(message, 2)]

    def expert_sum_4(self, state, through=()):
        outs = [shape((2 * self.rows + SMALL, FFH), BF16)] * PLANE
        blocks = self.order.run(
            spread_expert_kernel,
            outs,
            all_far(state),
            "spread_expert",
            (self.rows,),
            through=through,
        )
        return self.exchange(blocks[:PLANE]), blocks[PLANE:]

    def attention_sum_1(self, keep, sends):
        return keep, [self.swap_core(send) for send in sends]

    def attention_sum_2(self, state, through):
        dims = (self.depth * self.rows + SMALL, 2 * D)
        outs = [far_shape(dims, F32)] + [shape(dims, BF16)] * 3
        fixed = (self.rows, self.depth)
        operands = (far(state[0]), *state[1])
        blocks = self.order.run(
            split_attention_kernel, outs, operands, "split_attention", fixed, through=through
        )
        return [blocks[0]] + [self.swap(blocks[k], k) for k in range(1, 4)], blocks[4:]

    def attention_sum_3(self, pieces, through=()):
        outs = [
            shape((2 * self.rows + SMALL, 2 * D), F32),
            shape((2 * self.rows + SMALL, 2 * D), BF16),
        ]
        fixed = (self.rows, self.depth)
        operands = (far(pieces[0]), *pieces[1:])
        keep, send, *through = self.order.run(
            spread_attention_kernel, outs, operands, "spread_attention", fixed, through=through
        )
        return (keep, self.swap(send, 4)), through

    def attention_sum_4(self, state):
        outs = [
            shape((self.rows + SMALL, 2 * D), F32),
            shape((self.rows + SMALL, 2 * D), BF16),
        ]
        keep, send = self.order.run(
            halve_attention_kernel, outs, state, "halve_attention", (self.rows,), False
        )
        return keep, self.swap(send, 8)

    def own_attention(self, pieces, last):
        rows, dp = self.rows, self.dp
        outs = [
            shape((2, rows), F32),
            shape((2, rows), F32),
            shape((2, 3, rows, HALF), F32),
            shape((2, 2, HALF // dp), F32),
            shape((2, rows, HALF), F32),
            shape((2, rows), F32),
            shape((2, rows), F32),
            shape((2, rows), F32),
            shape((2, EXPERTS, rows), F32),
        ]
        return self.order.run(
            own_attention_kernel, outs, (*pieces, *last), "own_attention", (rows,)
        )

    def own_experts(self, first, last):
        rows = self.rows
        outs = [
            shape((2, EXPERTS, rows, FFH), F32),
            shape((2, EXPERTS, FFH // self.dp), F32),
            shape((2, EXPERTS, rows, FFH), F32),
            shape((2, EXPERTS, rows), F32),
        ]
        return self.order.run(own_experts_kernel, outs, (*first, *last), "own_experts", (rows,))


class PlainMoves(Moves):
    def by_index(self, pieces, me):
        return jnp.take(jnp.stack(pieces), me ^ jnp.arange(len(pieces)), axis=0)

    def relative(self, array, me, axis):
        return jnp.take(array, me ^ jnp.arange(array.shape[axis]), axis=axis)

    def spots(self):
        return [spot_of(j, k) for j in range(self.depth) for k in range(PLANE)]

    def total(self, pieces):
        return sum(piece.astype(F32) for piece in pieces)

    def pack(self, layer, weights):
        (
            norm1_gain,
            norm1_bias,
            output_bias,
            norm2_gain,
            norm2_bias,
            router_weight,
            expert_out_bias,
            qv_bias,
            expert_in_bias,
            qkv_weight,
            output_weight,
            expert_in,
            expert_out,
        ) = [weight[layer] for weight in weights]
        vectors = (norm1_gain, norm1_bias, output_bias, norm2_gain, norm2_bias)

        def placed(values, width):
            extent = values.shape[-1]
            column = jnp.arange(extent)[:, None] + self.me * extent
            spot = (column == jnp.arange(width)[None, :]).astype(BF16)
            return jnp.dot(values, spot, preferred_element_type=F32).astype(BF16)

        wide = placed(jnp.stack(vectors), D)
        router = placed(router_weight, D)
        shifts = placed(qv_bias, HALF).reshape(1, D)
        outer = placed(expert_out_bias, D)
        small = jnp.concatenate([wide, shifts, router, outer], axis=0).reshape(7, 2 * D)
        inner = placed(expert_in_bias, FFH)
        body = jnp.concatenate([*qkv_weight, output_weight], axis=1)
        blank = jnp.zeros((SMALL - 11, 2 * D), BF16)
        shard = jnp.concatenate([body, small, inner, blank], axis=0)
        experts = jnp.stack([expert_in, expert_out], axis=1)
        return shard, list(self.relative(experts, self.role, 0))

    def begin(self, weights):
        shard0, sends0 = self.pack(0, weights)
        shard1, sends1 = self.pack(1, weights)
        return shard0, [jnp.stack(sends0)], shard1, [jnp.stack(sends1)]

    def plane0(self, pieces):
        return pieces * 3

    def plane1(self, pieces):
        return pieces * 2

    def stack0(self, shard):
        return shard

    def join0(self, shard, exp0, exp1):
        return self.join_last(shard), exp0, exp1

    def forward(self, piece):
        return piece

    def join_last(self, shard):
        gathered = lax.all_gather(shard, "dp")
        body = gathered[:, : self.rows].reshape(D, 2 * D)
        tail = jnp.sum(gathered[:, self.rows :].astype(F32), axis=0).astype(BF16)
        own = jnp.concatenate([body, tail], axis=0)
        return own, self.swap_core(own)

    def join_levels(self, pieces, through=()):
        body = self.by_index(self.exchange(list(pieces[0])), self.role)
        pieces = [body] + [self.to_level(body, j) for j in range(1, self.depth)]
        stacked = self.by_index(pieces, self.level).reshape(self.dp, 2, self.rows, FFH)
        order = sorted(range(self.dp), key=lambda at: self.spots()[at])
        own = stacked[jnp.array(order)].transpose(1, 0, 2, 3).reshape(2, D, FFH)
        return (own, self.swap_core(own)), through

    def expert_sum_2(self, keep, got, through=()):
        return [keep, got, got, got], through

    def expert_sum_3(self, state):
        return state

    def expert_sum_4(self, state, through=()):
        return self.sum_expert(*state[:2]), through

    def sum_expert(self, keep, got):
        rows, depth = self.rows, self.depth
        whole = keep.astype(F32) + got.astype(F32)
        tail = whole[2 * D :]
        body = whole[: 2 * D].reshape(2, self.dp, rows, FFH)[:, jnp.array(self.spots())]
        body = self.relative(body.reshape(2, depth, PLANE * rows, FFH), self.level, 1)
        low, low_tail = body.astype(BF16), tail.astype(BF16)
        count = 2 * PLANE * rows
        pieces = []
        for j in range(1, depth):
            message = jnp.concatenate([low[:, j].reshape(count, FFH), low_tail], axis=0)
            pieces.append(self.to_level(message, j))
        body = body[:, 0].reshape(count, FFH) + self.total([piece[:count] for piece in pieces])
        tail = tail + self.total([piece[count:] for piece in pieces])
        body = self.relative(body.reshape(2, PLANE, rows, FFH), self.role, 1).astype(BF16)
        tail = tail.astype(BF16)
        count = 2 * rows
        blocks = [
            jnp.concatenate([body[:, k].reshape(count, FFH), tail], axis=0) for k in range(PLANE)
        ]
        return self.exchange(blocks)

    def attention_sum_1(self, keep, sends):
        return keep, jnp.concatenate(sends, axis=1)

    def attention_sum_2(self, state, through):
        return state, through

    def attention_sum_3(self, state, through=()):
        return state, through

    def attention_sum_4(self, state):
        keep, send = state
        whole = keep + self.swap_core(send).astype(F32)
        body = lax.psum_scatter(whole[:D], "dp", scatter_dimension=0, tiled=True)
        return jnp.concatenate([body, lax.psum(whole[D:], "dp")], axis=0)

    def last_attention_1(self, operands):
        (keep, send), _ = self.order.main(
            attention_grads_kernel,
            [shape((D, 2 * D), F32), shape((D, 2 * D), BF16)],
            operands,
            "attention_grads1",
        )
        return keep, self.swap_core(send)

    def last_expert_1(self, operands):
        (keep, send), _ = self.order.main(
            expert_grads_pair_kernel, EXPERT_SUMS, operands, "expert_grads1"
        )
        return keep, self.swap_core(send)

    def last_sums_1(self, expert, attention):
        whole = attention[0] + attention[1].astype(F32)
        return expert, lax.psum_scatter(whole, "dp", scatter_dimension=0, tiled=True)

    def last_sums_2(self, state):
        return self.sum_expert(*state[0]), state[1]

    def own_attention(self, total, last):
        rows = self.rows
        body = jnp.stack([total[:rows], last])
        tail = total[rows:].reshape(2, 16, D)

        def owned(values, width):
            return lax.dynamic_slice_in_dim(
                values, self.me * width, width, axis=values.ndim - 1
            )

        wide = owned(tail, rows)
        qkv = body[:, :, : 3 * HALF].reshape(2, rows, 3, HALF).transpose(0, 2, 1, 3)
        qv = owned(tail[:, 5].reshape(2, 2, HALF), HALF // self.dp)
        vectors = [wide[:, row] for row in range(5)]
        return (
            *vectors[:2],
            qkv,
            qv,
            body[:, :, 3 * HALF :],
            *vectors[2:],
            wide[:, 6:10],
        )

    def own_experts(self, first, last):
        rows = self.rows
        owned = jnp.stack([self.by_index(first, self.role), self.by_index(last, self.role)])
        owned = owned.astype(F32)
        tail = owned[:, :, 2 * rows :]
        width = FFH // self.dp
        in_bias = lax.dynamic_slice_in_dim(tail[:, :, 1], self.me * width, width, axis=2)
        out_bias = lax.dynamic_slice_in_dim(tail[:, :, 0], self.me * rows, rows, axis=2)
        return owned[:, :, :rows], in_bias, owned[:, :, rows : 2 * rows], out_bias


def build(dp):
    def local(
        tokens,
        routes,
        norm1_gain,
        norm1_bias,
        qkv_weight,
        qv_bias,
        output_weight,
        output_bias,
        norm2_gain,
        norm2_bias,
        router_weight,
        expert_in,
        expert_in_bias,
        expert_out,
        expert_out_bias,
        grad_out,
    ):
        me = lax.axis_index("dp").astype(jnp.int32)
        core = lax.axis_index("tensor")
        role, level = me % PLANE, me // PLANE
        order = Order(
            jnp.stack([me, role, level, me // 4, me % 4, core.astype(jnp.int32)])
        )
        moves = (FastMoves if dp == 16 else PlainMoves)(dp, order, me, role, level)
        weights = (
            norm1_gain,
            norm1_bias,
            output_bias,
            norm2_gain,
            norm2_bias,
            router_weight.transpose(0, 2, 1),
            expert_out_bias,
            qv_bias,
            expert_in_bias,
            qkv_weight.transpose(0, 2, 1, 3),
            output_weight.transpose(0, 2, 1),
            expert_in,
            expert_out.transpose(0, 1, 3, 2),
        )

        att0, exp0, gathered1, exp1 = moves.begin(weights)

        choice = lax.dynamic_index_in_dim(routes, core, axis=1, keepdims=False)
        hot = (choice[..., None] == jnp.arange(EXPERTS)).astype(BF16)
        any_hot = hot[:, :, 0] + hot[:, :, 1]
        below = jnp.tril(jnp.ones((SEQ, SEQ), BF16), -1)
        slot = jnp.einsum("ts,lse->lte", below, any_hot, preferred_element_type=F32)
        slot = jnp.sum(hot.astype(F32) * slot[:, :, None], axis=-1).astype(jnp.int32)
        target = (choice ^ role) * CAP + slot
        columns = jnp.pad(
            jnp.concatenate([target, choice], axis=-1),
            ((0, 0), (0, SP - SEQ), (0, 0)),
            constant_values=-1,
        )
        target_rows = columns[:, :, 0:2].transpose(0, 2, 1)

        def image(values):
            values = lax.dynamic_index_in_dim(values, core, axis=0, keepdims=False)
            return jnp.pad(values, ((0, SP - SEQ), (0, 0)))

        rows, grad = image(tokens), image(grad_out)

        exp0 = moves.plane0(exp0)
        att0 = moves.stack0(att0)
        attention0, exp0, exp1 = moves.join0(att0, exp0, exp1)

        kept0, exp1[1:] = order.main(
            first_forward_kernel,
            forward_outs(False),
            (rows, *all_far(attention0), columns[0], target_rows[0]),
            "attention_first",
            exp1[1:],
        )
        middle0, normed0, normed2_0, qkv0, mixed0, log0, probs0, small0 = kept0[:8]
        blocks0 = moves.exchange(kept0[8:])
        exp1, early1 = moves.plane1(exp1)
        next1 = moves.to_level(early1, 2)
        expert0, _ = moves.join_levels(exp0)
        (hidden0, slope0, *results), (exp1,) = order.main(
            expert_forward_kernel,
            expert_outs(False),
            all_far((*blocks0, *expert0)) + [small0],
            "expert_forward",
            [exp1],
            place=True,
        )
        slots0 = moves.exchange(results)
        near1 = moves.to_level(exp1, 1)
        next1, *slots0[1:] = order.gate([next1, *slots0[1:]])
        exp1 = [exp1, near1, next1, moves.forward(next1)]
        attention1 = moves.join_last(gathered1)

        (rows1, *kept1), _ = order.main(
            last_forward_kernel,
            [far_shape((SP, D), F32)] + forward_outs(True),
            (
                *all_far((middle0, probs0)),
                columns[0],
                *all_far(slots0),
                grad,
                *all_far(attention1),
                columns[1],
                target_rows[1],
            ),
            "attention_last",
        )
        middle1, normed1, normed2_1, qkv1, mixed1, log1, probs1, small1 = kept1[:8]
        blocks1 = moves.exchange(kept1[8:])
        expert1, _ = moves.join_levels(exp1)
        (hidden1, grad_pre1, *results), _ = order.main(
            expert_both_kernel,
            expert_outs(True),
            (*all_far(blocks1), *expert1, small1),
            "expert_both",
            place=True,
        )
        pairs1 = moves.exchange(results)
        sums1 = moves.last_expert_1((*all_far(blocks1), hidden1, grad_pre1))
        back1, _ = order.main(
            backward_last_kernel,
            backward_outs(True),
            (
                grad,
                *pairs1,
                *all_far((rows1, middle1, normed2_1, qkv1, mixed1, log1, probs1)),
                columns[1],
                *all_far(attention1),
                far(probs0),
                columns[0],
                target_rows[0],
            ),
            "attention_back_last",
        )
        grad_rows1, grad_qkv1, grad_att1, keep1, send1, output = back1[:6]
        grads0 = moves.exchange(back1[6:])
        att_owned1 = moves.last_attention_1((far(normed1), grad_qkv1, grad_att1, far(mixed1)))

        (grad_pre0, *results), _ = order.main(
            expert_back_kernel, EXPERT_BACK, all_far((*grads0, slope0, *expert0)), "expert_back"
        )
        sums1 = moves.last_sums_1(sums1, att_owned1)
        slot_grads0 = moves.exchange(results)
        sums0, _ = order.main(
            expert_grads_single_kernel,
            EXPERT_SUMS,
            all_far((*blocks0, *grads0, hidden0)) + [grad_pre0],
            "expert_grads0",
        )
        sums0, slot_grads0[1:] = moves.expert_sum_2(
            sums0[0], moves.swap_core(sums0[1]), slot_grads0[1:]
        )
        (grad_rows0, grad_qkv0, grad_att0, keep0, send0), _ = order.main(
            backward_first_kernel,
            backward_outs(False),
            (
                far(grad_rows1),
                *all_far(slots0),
                *slot_grads0,
                rows,
                *all_far((middle0, normed2_0, qkv0, mixed0, log0, probs0)),
                columns[0],
                *all_far(attention0),
            ),
            "attention_back_first",
        )
        att_sums0, _ = order.main(
            attention_grads_small_kernel,
            ATTENTION_SUMS,
            (
                far(normed0),
                grad_qkv0,
                grad_att0,
                far(mixed0),
                keep0,
                send0,
                far(keep1),
                far(send1),
            ),
            "attention_grads0",
        )

        att_sums0 = moves.attention_sum_1(att_sums0[0], att_sums0[1:])
        sums0 = moves.expert_sum_3(sums0)
        att_sums0, (grad_rows0, output) = moves.attention_sum_2(att_sums0, [grad_rows0, output])
        att_sums0, _ = moves.attention_sum_3(att_sums0)
        sums1, att_owned1 = moves.last_sums_2(sums1)
        sums0, _ = moves.expert_sum_4(sums0)
        att_sums0 = moves.attention_sum_4(att_sums0)
        output_got, rows_got = moves.swap_core(output), moves.swap_core(grad_rows0)
        gain1, bias1, qkv, qv, out, shift, gain2, bias2, router = moves.own_attention(
            att_sums0, att_owned1
        )
        inner, in_bias, outer, out_bias = moves.own_experts(sums0, sums1)

        def both(values, others):
            first = jnp.where(core == 0, values, others)[:SEQ]
            second = jnp.where(core == 0, others, values)[:SEQ]
            return jnp.stack([first, second], axis=1).transpose(1, 0, 2)

        return (
            both(output, output_got),
            both(grad_rows0, rows_got),
            gain1,
            bias1,
            qkv.transpose(0, 2, 1, 3),
            qv,
            out.transpose(0, 2, 1),
            shift,
            gain2,
            bias2,
            router.transpose(0, 2, 1),
            inner,
            in_bias,
            outer.transpose(0, 1, 3, 2),
            out_bias,
        )

    return local


def solution(mesh):
    weights = (
        P(None, "dp"),
        P(None, "dp"),
        P(None, "dp", None, "tensor"),
        P(None, None, ("tensor", "dp")),
        P(None, "tensor", "dp"),
        P(None, "dp"),
        P(None, "dp"),
        P(None, "dp"),
        P(None, "dp", None),
        P(None, None, "dp", "tensor"),
        P(None, None, ("tensor", "dp")),
        P(None, None, "tensor", "dp"),
        P(None, None, "dp"),
    )
    images = P("dp", None, None)
    return jax.shard_map(
        build(mesh.shape["dp"]),
        mesh=mesh,
        in_specs=(images, P(None, "dp", None, None)) + weights + (images,),
        out_specs=(images, images) + weights,
        check_vma=False,
    )
```

```python
import jax
import jax.numpy as jnp
from jax import lax
from jax.experimental import pallas as pl
from jax.experimental.pallas import tpu as pltpu
from jax.sharding import PartitionSpec as P

D = 512
HD = 64
HALF = 256
FFH = 1024
SEQ = 197
SP = 208
EXPERTS = 4
CAP = 128
SLOTS = EXPERTS * CAP
PLANE = 4
SMALL = 16
EPSILON = 1e-06
SCALE = HD ** (-0.5)
MIB = 2**20
VMEM_MIB = 32
F32 = jnp.float32
BF16 = jnp.bfloat16


def call(kernel, out_shape, operands, name, after, through, scalars):
    inputs, outputs = len(operands), len(out_shape)

    def body(*refs):
        first = inputs + len(after) + len(through)
        kernel(*refs[:inputs], *refs[first : first + outputs])

    anywhere = pl.BlockSpec(memory_space=pl.ANY)
    whole = pl.BlockSpec(memory_space=pltpu.VMEM)
    return pl.pallas_call(
        body,
        out_shape=list(out_shape) + [shape(array.shape, array.dtype) for array in through],
        in_specs=[pl.BlockSpec(memory_space=pltpu.SMEM)] * scalars
        + [whole] * (inputs - scalars)
        + [anywhere] * (len(after) + len(through)),
        out_specs=[whole] * outputs + [anywhere] * len(through),
        input_output_aliases={
            inputs + len(after) + i: outputs + i for i in range(len(through))
        },
        compiler_params=pltpu.CompilerParams(vmem_limit_bytes=VMEM_MIB * MIB),
        cost_estimate=pl.CostEstimate(flops=1, bytes_accessed=1, transcendentals=0),
        name=name,
    )(*operands, *after, *through)


def shape(dims, dtype):
    return jax.ShapeDtypeStruct(dims, dtype)


def far_shape(dims, dtype):
    return pltpu.HBM(dims, dtype)


def far(array):
    return pltpu.with_memory_space_constraint(array, pltpu.HBM)


def all_far(arrays):
    return [far(array) for array in arrays]


def mm(a, b):
    return lax.dot_general(a, b, (((1,), (0,)), ((), ())), preferred_element_type=F32)


def mm_t(a, b):
    return lax.dot_general(a, b, (((1,), (1,)), ((), ())), preferred_element_type=F32)


def mm_tn(a, b):
    return lax.dot_general(a, b, (((0,), (0,)), ((), ())), preferred_element_type=F32)


def normalise(rows):
    center = rows - jnp.mean(rows, axis=-1, keepdims=True)
    inverse = lax.rsqrt(jnp.mean(center * center, axis=-1, keepdims=True) + EPSILON)
    return center * inverse, inverse


def norm_back(grad, hat, inverse, gain):
    scaled = grad * gain
    return inverse * (
        scaled
        - jnp.mean(scaled, axis=-1, keepdims=True)
        - hat * jnp.mean(scaled * hat, axis=-1, keepdims=True)
    )


def small_row(small, row, part):
    return small[row : row + 1, part * D : (part + 1) * D]


def router_rows(small):
    return [small_row(small, 3 + e // 2, e % 2) for e in range(EXPERTS)]


def select_columns(targets, j):
    lanes = lax.broadcasted_iota(jnp.int32, (SP, SLOTS), 1)
    return jnp.where(lanes == targets[:, j : j + 1], 1.0, 0.0).astype(BF16)


def select_rows(target_rows, j):
    subs = lax.broadcasted_iota(jnp.int32, (SLOTS, SP), 0)
    return jnp.where(subs == target_rows[j : j + 1, :], 1.0, 0.0).astype(BF16)


def chosen_of(targets, j):
    lanes = lax.broadcasted_iota(jnp.int32, (SP, EXPERTS), 1)
    return jnp.where(lanes == targets[:, 2 + j : 3 + j], 1.0, 0.0)


def gates_of(probs, targets):
    return [jnp.sum(chosen_of(targets, j) * probs, axis=-1, keepdims=True) for j in range(2)]


def attention_forward(rows, halves, targets, target_rows, outs, grad_rows):
    middle_ref, normed_ref, normed2_ref, qkv_ref, mixed_ref, log_ref, probs_ref = outs[:7]
    small_ref, send_refs = outs[7], outs[8:]
    small_ref[0] = halves[0][D : D + SMALL, :]
    small_ref[1] = halves[1][D : D + SMALL, :]
    small = halves[0][D : D + SMALL, :].astype(F32)
    hat, _ = normalise(rows)
    normed = (hat * small_row(small, 0, 0) + small_row(small, 0, 1)).astype(BF16)
    normed_ref[...] = normed
    attended = jnp.zeros((SP, D), F32)
    key_ok = lax.broadcasted_iota(jnp.int32, (SP, SP), 1) < SEQ
    logs = []
    for half in range(2):
        qkv = mm(normed, halves[half][0:D, 0 : 3 * HALF])
        shift = halves[half][D : D + SMALL, :][2:3, D : 2 * D].astype(F32)
        query = (qkv[:, 0:HALF] + shift[:, 0:HALF]).astype(BF16)
        key = qkv[:, HALF : 2 * HALF].astype(BF16)
        value = (qkv[:, 2 * HALF : 3 * HALF] + shift[:, HALF : 2 * HALF]).astype(BF16)
        qkv_ref[half] = jnp.concatenate([query, key, value], axis=1)
        mixed = []
        for head in range(HALF // HD):
            cut = slice(head * HD, (head + 1) * HD)
            scores = jnp.where(key_ok, mm_t(query[:, cut], key[:, cut]) * SCALE, -1e30)
            top = jnp.max(scores, axis=-1, keepdims=True)
            weight = jnp.exp(scores - top)
            total = jnp.sum(weight, axis=-1, keepdims=True)
            logs.append(top + jnp.log(total))
            low = (weight * (1.0 / total)).astype(BF16)
            mixed.append(mm(low, value[:, cut]).astype(BF16))
        mixed = jnp.concatenate(mixed, axis=1)
        mixed_ref[half] = mixed
        attended = attended + mm_t(mixed, halves[half][0:D, 3 * HALF : 4 * HALF])
    log_ref[...] = jnp.concatenate(logs, axis=1)
    middle = rows + attended + small_row(small, 1, 0)
    middle_ref[...] = middle
    hat2, _ = normalise(middle)
    normed2 = (hat2 * small_row(small, 1, 1) + small_row(small, 2, 0)).astype(BF16)
    normed2_ref[...] = normed2
    router = jnp.concatenate(router_rows(small) + [jnp.zeros((4, D), F32)], axis=0).astype(BF16)
    logits = mm_t(normed2, router)[:, 0:EXPERTS]
    weight = jnp.exp(logits - jnp.max(logits, axis=-1, keepdims=True))
    probs = weight / jnp.sum(weight, axis=-1, keepdims=True)
    probs_ref[...] = probs
    picks = [select_rows(target_rows, j) for j in range(2)]
    sent = mm(picks[0] + picks[1], normed2).astype(BF16)
    if grad_rows is None:
        for k in range(PLANE):
            send_refs[k][...] = sent[k * CAP : (k + 1) * CAP]
    else:
        gates = gates_of(probs, targets)
        grads = (
            mm(picks[0], (gates[0] * grad_rows).astype(BF16))
            + mm(picks[1], (gates[1] * grad_rows).astype(BF16))
        ).astype(BF16)
        for k in range(PLANE):
            send_refs[k][0] = sent[k * CAP : (k + 1) * CAP]
            send_refs[k][1] = grads[k * CAP : (k + 1) * CAP]


def first_forward_kernel(rows_ref, own_ref, other_ref, targets_ref, target_rows_ref, *outs):
    attention_forward(
        rows_ref[...].astype(F32),
        (own_ref, other_ref),
        targets_ref[...],
        target_rows_ref[...],
        outs,
        None,
    )


def combine(middle, probs, targets, slot_rows):
    gates = gates_of(probs, targets)
    picked = [mm(select_columns(targets, j), slot_rows) for j in range(2)]
    return middle + gates[0] * picked[0] + gates[1] * picked[1], picked


def last_forward_kernel(
    middle_ref,
    probs_ref,
    prior_targets_ref,
    f0,
    f1,
    f2,
    f3,
    grad_ref,
    own_ref,
    left_ref,
    right_ref,
    targets_ref,
    target_rows_ref,
    rows_ref,
    *outs,
):
    slot_rows = jnp.concatenate([f0[...], f1[...], f2[...], f3[...]], axis=0)
    rows, _ = combine(middle_ref[...], probs_ref[...], prior_targets_ref[...], slot_rows)
    rows_ref[...] = rows
    attention_forward(
        rows,
        (own_ref, jnp.concatenate([left_ref[...], right_ref[...]], axis=1)),
        targets_ref[...],
        target_rows_ref[...],
        outs,
        grad_ref[...].astype(F32),
    )


def forward_outs(pair):
    block = (2, CAP, D) if pair else (CAP, D)
    return [
        far_shape((SP, D), F32),
        far_shape((SP, D), BF16),
        far_shape((SP, D), BF16),
        far_shape((2, SP, 3 * HALF), BF16),
        far_shape((2, SP, HALF), BF16),
        far_shape((SP, 8), F32),
        far_shape((SP, EXPERTS), F32),
        shape((2, SMALL, 2 * D), BF16),
    ] + [shape(block, BF16)] * PLANE


def backward_kernel(final, *refs):
    grad_ref, f0, f1, f2, f3 = refs[:5]
    refs = refs[5:]
    if not final:
        d0, d1, d2, d3 = refs[:4]
        refs = refs[4:]
    (
        rows_ref,
        middle_ref,
        normed2_ref,
        qkv_ref,
        mixed_ref,
        log_ref,
        probs_ref,
        targets_ref,
        own_ref,
        other,
    ) = refs[:10]
    rest = refs[10:]
    if final:
        other = jnp.concatenate([other[...], rest[0][...]], axis=1)
        rest = rest[1:]
        prior_probs_ref, prior_targets_ref, prior_target_rows_ref = rest[:3]
        rest = rest[3:]
    grad_rows_ref, grad_qkv_ref, grad_att_ref, small_keep_ref, small_send_ref = rest[:5]
    rest = rest[5:]
    halves = (own_ref, other)
    small = own_ref[D : D + SMALL, :].astype(F32)
    grad = grad_ref[...].astype(F32)
    targets = targets_ref[...]
    probs = probs_ref[...]
    middle = middle_ref[...]
    if final:
        slot_rows = jnp.concatenate([f0[0], f1[0], f2[0], f3[0]], axis=0)
        slot_grads = jnp.concatenate([f0[1], f1[1], f2[1], f3[1]], axis=0)
    else:
        slot_rows = jnp.concatenate([f0[...], f1[...], f2[...], f3[...]], axis=0)
        slot_grads = jnp.concatenate([d0[...], d1[...], d2[...], d3[...]], axis=0)
    picks = [select_columns(targets, j) for j in range(2)]
    picked = [mm(picks[j], slot_rows) for j in range(2)]
    if final:
        gates = gates_of(probs, targets)
        rest[0][...] = middle + gates[0] * picked[0] + gates[1] * picked[1]
    grad_probs = jnp.zeros((SP, EXPERTS), F32)
    for j in range(2):
        grad_probs = grad_probs + chosen_of(targets, j) * jnp.sum(
            grad * picked[j], axis=-1, keepdims=True
        )
    grad_logits = probs * (grad_probs - jnp.sum(probs * grad_probs, axis=-1, keepdims=True))
    grad_logits = grad_logits.astype(BF16).astype(F32)
    grad_normed2 = mm(picks[0] + picks[1], slot_grads)
    normed2 = normed2_ref[...].astype(F32)
    routers = router_rows(small)
    grad_router = []
    for e in range(EXPERTS):
        column = grad_logits[:, e : e + 1]
        grad_normed2 = grad_normed2 + column * routers[e]
        grad_router.append(jnp.sum(column * normed2, axis=0, keepdims=True))
    hat2, inverse2 = normalise(middle)
    grad_gain2 = jnp.sum(grad_normed2 * hat2, axis=0, keepdims=True)
    grad_bias2 = jnp.sum(grad_normed2, axis=0, keepdims=True)
    grad_middle = grad + norm_back(grad_normed2, hat2, inverse2, small_row(small, 1, 1))
    grad_att = grad_middle.astype(BF16)
    grad_att_ref[...] = grad_att
    grad_shift = jnp.sum(grad_att.astype(F32), axis=0, keepdims=True)
    key_ok = lax.broadcasted_iota(jnp.int32, (SP, SP), 1) < SEQ
    grad_normed = jnp.zeros((SP, D), F32)
    qv_rows = []
    for half in range(2):
        grad_mixed = mm(grad_att, halves[half][0:D, 3 * HALF : 4 * HALF]).astype(BF16)
        query = qkv_ref[half, :, 0:HALF]
        key = qkv_ref[half, :, HALF : 2 * HALF]
        value = qkv_ref[half, :, 2 * HALF : 3 * HALF]
        grad_q, grad_k, grad_v = [], [], []
        for head in range(HALF // HD):
            cut = slice(head * HD, (head + 1) * HD)
            at = half * (HALF // HD) + head
            scores = mm_t(query[:, cut], key[:, cut]) * SCALE - log_ref[:, at : at + 1]
            weight = jnp.exp(jnp.where(key_ok, scores, -1e30))
            grad_v.append(mm_tn(weight.astype(BF16), grad_mixed[:, cut]).astype(BF16))
            grad_weight = mm_t(grad_mixed[:, cut], value[:, cut])
            mean = jnp.sum(weight * grad_weight, axis=-1, keepdims=True)
            grad_scores = (weight * (grad_weight - mean)).astype(BF16)
            grad_q.append((mm(grad_scores, key[:, cut]) * SCALE).astype(BF16))
            grad_k.append((mm_tn(grad_scores, query[:, cut]) * SCALE).astype(BF16))
        grad_qkv = jnp.concatenate(grad_q + grad_k + grad_v, axis=1)
        grad_qkv_ref[half] = grad_qkv
        grad_normed = grad_normed + mm_t(grad_qkv, halves[half][0:D, 0 : 3 * HALF])
        sums = jnp.sum(grad_qkv.astype(F32), axis=0, keepdims=True)
        qv_rows.append(jnp.concatenate([sums[:, 0:HALF], sums[:, 2 * HALF : 3 * HALF]], axis=1))
    hat, inverse = normalise(rows_ref[...].astype(F32))
    grad_gain = jnp.sum(grad_normed * hat, axis=0, keepdims=True)
    grad_bias = jnp.sum(grad_normed, axis=0, keepdims=True)
    grad_rows = grad_middle + norm_back(grad_normed, hat, inverse, small_row(small, 0, 0))
    grad_rows_ref[...] = grad_rows
    for half, ref in enumerate((small_keep_ref, small_send_ref)):
        left = [grad_gain, grad_shift, grad_bias2, grad_router[0], grad_router[2]]
        right = [grad_bias, grad_gain2, qv_rows[half], grad_router[1], grad_router[3]]
        ref[...] = jnp.concatenate(
            [
                jnp.concatenate(left + [jnp.zeros((SMALL - 5, D), F32)], axis=0),
                jnp.concatenate(right + [jnp.zeros((SMALL - 5, D), F32)], axis=0),
            ],
            axis=1,
        )
    if final:
        prior_gates = gates_of(prior_probs_ref[...], prior_targets_ref[...])
        prior_rows = prior_target_rows_ref[...]
        sent = (
            mm(select_rows(prior_rows, 0), (prior_gates[0] * grad_rows).astype(BF16))
            + mm(select_rows(prior_rows, 1), (prior_gates[1] * grad_rows).astype(BF16))
        ).astype(BF16)
        for k in range(PLANE):
            rest[1 + k][...] = sent[k * CAP : (k + 1) * CAP]


def backward_last_kernel(*refs):
    backward_kernel(True, *refs)


def backward_first_kernel(*refs):
    backward_kernel(False, *refs)


def backward_outs(final):
    keep = far_shape if final else shape
    outs = [
        keep((SP, D), F32),
        shape((2, SP, 3 * HALF), BF16),
        shape((SP, D), BF16),
        keep((SMALL, 2 * D), F32),
        keep((SMALL, 2 * D), F32),
    ]
    if final:
        outs += [shape((SP, D), F32)] + [shape((CAP, D), BF16)] * PLANE
    return outs


def attention_grads_kernel(normed_ref, grad_qkv_ref, grad_att_ref, mixed_ref, *outs):
    normed = normed_ref[...]
    grad_att = grad_att_ref[...]
    for half, ref in enumerate(outs):
        ref[0:D, 0 : 3 * HALF] = mm_tn(normed, grad_qkv_ref[half]).astype(ref.dtype)
        ref[0:D, 3 * HALF : 4 * HALF] = mm_tn(grad_att, mixed_ref[half]).astype(ref.dtype)


PARTS = (slice(0, 384), slice(384, 768), slice(768, 1024))


def attention_grads_small_kernel(*refs):
    normed = refs[0][...]
    grad_qkv_ref, grad_att, mixed_ref, small = refs[1], refs[2][...], refs[3], refs[4:8]
    keep_ref, sends = refs[8], refs[9:]
    tails = [
        jnp.concatenate([small[half][0:8, :], small[2 + half][0:8, :]], axis=0)
        for half in range(2)
    ]
    keep_ref[0:D, 0 : 3 * HALF] = mm_tn(normed, grad_qkv_ref[0])
    keep_ref[0:D, 3 * HALF : 4 * HALF] = mm_tn(grad_att, mixed_ref[0])
    keep_ref[D : D + SMALL, :] = tails[0]
    for ref, cut in zip(sends, PARTS):
        if cut.stop <= 3 * HALF:
            ref[0:D, :] = mm_tn(normed, grad_qkv_ref[1, :, cut]).astype(BF16)
        else:
            ref[0:D, :] = mm_tn(grad_att, mixed_ref[1]).astype(BF16)
        ref[D : D + SMALL, :] = tails[1][:, cut].astype(BF16)


ATTENTION_SUMS = [far_shape((D + SMALL, 2 * D), F32)] + [
    shape((D + SMALL, cut.stop - cut.start), BF16) for cut in PARTS
]


CHUNK = 512


def gelu_parts(values):
    tail = 0.5 * (1.0 + lax.erf(values * 0.7071067811865476))
    density = jnp.exp(-0.5 * values * values) * 0.3989422804014327
    return values * tail, tail + values * density


def expert_bias(small, role):
    out_shift = jnp.zeros((1, D), F32)
    in_shift = jnp.zeros((1, FFH), F32)
    for e in range(EXPERTS):
        at = jnp.where(role == e, 1.0, 0.0)
        out_shift = out_shift + at * small_row(small, 5 + e // 2, e % 2)
        in_shift = in_shift + at * small[7 + e : 8 + e, :]
    return out_shift, in_shift


def expert_kernel(both, place_ref, *refs):
    blocks, (own_ref, other_ref, small_ref), outs = (
        refs[:PLANE],
        refs[PLANE : PLANE + 3],
        refs[PLANE + 3 :],
    )
    role = place_ref[1]
    hidden_ref, slope_ref = outs[:2]
    if both:
        inputs = jnp.concatenate([block[0] for block in blocks], axis=0)
        grads = jnp.concatenate([block[1] for block in blocks], axis=0)
        result = jnp.zeros((SLOTS, D), F32)
        result_grad = jnp.zeros((SLOTS, D), F32)
    else:
        inputs = jnp.concatenate([block[...] for block in blocks], axis=0)
        result = jnp.zeros((SLOTS, D), F32)
    out_shift = None
    for half, ref in enumerate((own_ref, other_ref)):
        shift, in_shift = expert_bias(small_ref[half].astype(F32), role)
        if half == 0:
            out_shift = shift
        for chunk in range(FFH // CHUNK):
            cut = slice(chunk * CHUNK, (chunk + 1) * CHUNK)
            columns = slice(half * FFH + chunk * CHUNK, half * FFH + (chunk + 1) * CHUNK)
            hidden, slope = gelu_parts(mm(inputs, ref[0, :, cut]) + in_shift[:, cut])
            hidden = hidden.astype(BF16)
            hidden_ref[:, columns] = hidden
            result = result + mm_t(hidden, ref[1, :, cut])
            if both:
                grad_pre = (mm(grads, ref[1, :, cut]) * slope).astype(BF16)
                slope_ref[:, columns] = grad_pre
                result_grad = result_grad + mm_t(grad_pre, ref[0, :, cut])
            else:
                slope_ref[:, columns] = slope.astype(BF16)
    result = (result + out_shift).astype(BF16)
    for k in range(PLANE):
        if both:
            outs[2 + k][0] = result[k * CAP : (k + 1) * CAP]
            outs[2 + k][1] = result_grad[k * CAP : (k + 1) * CAP].astype(BF16)
        else:
            outs[2 + k][...] = result[k * CAP : (k + 1) * CAP]


def expert_forward_kernel(*refs):
    expert_kernel(False, *refs)


def expert_both_kernel(*refs):
    expert_kernel(True, *refs)


def expert_outs(both):
    block = (2, CAP, D) if both else (CAP, D)
    kept = shape if both else far_shape
    return [kept((SLOTS, 2 * FFH), BF16)] * 2 + [shape(block, BF16)] * PLANE


def expert_back_kernel(*refs):
    blocks, (slope_ref, own_ref, other_ref, grad_pre_ref), outs = (
        refs[:PLANE],
        refs[PLANE : PLANE + 4],
        refs[PLANE + 4 :],
    )
    grads = jnp.concatenate([block[...] for block in blocks], axis=0)
    result = jnp.zeros((SLOTS, D), F32)
    for half, ref in enumerate((own_ref, other_ref)):
        for chunk in range(FFH // CHUNK):
            cut = slice(chunk * CHUNK, (chunk + 1) * CHUNK)
            columns = slice(half * FFH + chunk * CHUNK, half * FFH + (chunk + 1) * CHUNK)
            grad_pre = (mm(grads, ref[1, :, cut]) * slope_ref[:, columns].astype(F32)).astype(BF16)
            grad_pre_ref[:, columns] = grad_pre
            result = result + mm_t(grad_pre, ref[0, :, cut])
    for k in range(PLANE):
        outs[k][...] = result[k * CAP : (k + 1) * CAP].astype(BF16)


EXPERT_BACK = [shape((SLOTS, 2 * FFH), BF16)] + [shape((CAP, D), BF16)] * PLANE


def expert_grads_kernel(pair, *refs):
    if pair:
        blocks, (hidden_ref, grad_pre_ref, keep_ref, send_ref) = refs[:PLANE], refs[PLANE:]
        inputs = jnp.concatenate([block[0] for block in blocks], axis=0)
        grads = jnp.concatenate([block[1] for block in blocks], axis=0)
    else:
        blocks, (hidden_ref, grad_pre_ref, keep_ref, send_ref) = refs[: 2 * PLANE], refs[2 * PLANE :]
        inputs = jnp.concatenate([block[...] for block in blocks[:PLANE]], axis=0)
        grads = jnp.concatenate([block[...] for block in blocks[PLANE:]], axis=0)
    out_shift = jnp.sum(grads.astype(F32), axis=0, keepdims=True)
    out_shift = jnp.concatenate([out_shift, jnp.zeros((1, FFH - D), F32)], axis=1)
    for half, ref in enumerate((keep_ref, send_ref)):
        shifts = []
        for chunk in range(FFH // CHUNK):
            cut = slice(chunk * CHUNK, (chunk + 1) * CHUNK)
            columns = slice(half * FFH + chunk * CHUNK, half * FFH + (chunk + 1) * CHUNK)
            grad_pre = grad_pre_ref[:, columns]
            ref[0:D, cut] = mm_tn(inputs, grad_pre).astype(ref.dtype)
            ref[D : 2 * D, cut] = mm_tn(grads, hidden_ref[:, columns]).astype(ref.dtype)
            shifts.append(jnp.sum(grad_pre.astype(F32), axis=0, keepdims=True))
        tail = [out_shift, jnp.concatenate(shifts, axis=1), jnp.zeros((SMALL - 2, FFH), F32)]
        ref[2 * D : 2 * D + SMALL, :] = jnp.concatenate(tail, axis=0).astype(ref.dtype)


def expert_grads_pair_kernel(*refs):
    expert_grads_kernel(True, *refs)


def expert_grads_single_kernel(*refs):
    expert_grads_kernel(False, *refs)


EXPERT_SUMS = [far_shape((2 * D + SMALL, FFH), BF16), shape((2 * D + SMALL, FFH), BF16)]


def spot_of(level, role):
    return role + PLANE * level


def rows_at(index, size, base=0):
    return pl.ds(base + pl.multiple_of(index * size, size), size)


def one_hot(me, extent, width, dtype=BF16):
    row = lax.broadcasted_iota(jnp.int32, (extent, width), 0)
    column = lax.broadcasted_iota(jnp.int32, (extent, width), 1)
    return jnp.where(row + me * extent == column, 1.0, 0.0).astype(dtype)


def pack_shard(layer, rows, me, refs, shard_ref):
    (gain1, bias1, shift, gain2, bias2, router, out_bias, qv, in_bias, qkv, output) = refs
    vectors = [ref[layer : layer + 1, :].astype(F32) for ref in (gain1, bias1, shift, gain2, bias2)]
    vectors = jnp.concatenate(vectors + [out_bias[layer].astype(F32)], axis=0)
    place = one_hot(me, rows, D)
    wide = mm(vectors.astype(BF16), place)
    router = mm(router[layer], place)
    shifts = mm(qv[layer], one_hot(me, qv.shape[2], HALF))
    shifts = jnp.concatenate([shifts[0:1], shifts[1:2]], axis=1)
    inner = mm(in_bias[layer], one_hot(me, in_bias.shape[2], FFH))
    left = [wide[0:1], wide[2:3], wide[4:5], router[0:1], router[2:3], wide[5:6], wide[7:8]]
    right = [wide[1:2], wide[3:4], shifts, router[1:2], router[3:4], wide[6:7], wide[8:9]]
    small = jnp.concatenate(
        [jnp.concatenate(left, axis=0), jnp.concatenate(right, axis=0)], axis=1
    )
    small = jnp.concatenate([small, inner, jnp.zeros((SMALL - 11, 2 * D), F32)], axis=0)
    shard_ref[rows : rows + SMALL, :] = small.astype(BF16)
    for part in range(3):
        shard_ref[0:rows, part * HALF : (part + 1) * HALF] = qkv[layer, part]
    shard_ref[0:rows, 3 * HALF : 4 * HALF] = output[layer]


def pack_kernel(rows, place_ref, *refs):
    first_ref, last_ref = refs[13:15]
    role = place_ref[1]
    expert_in, expert_out = refs[11:13]
    for layer in range(2):
        for k, ref in enumerate(refs[15 + layer * PLANE : 15 + (layer + 1) * PLANE]):
            ref[0:rows, :] = expert_in[layer, role ^ k]
            ref[rows : 2 * rows, :] = expert_out[layer, role ^ k]
    pack_shard(0, rows, place_ref[0], refs[:11], first_ref)
    pack_shard(1, rows, place_ref[0], refs[:11], last_ref)
    last_ref[rows + SMALL : rows + 2 * SMALL, :] = jnp.zeros((SMALL, 2 * D), BF16)


def stack_attention_kernel(rows, place_ref, *refs):
    pieces, out_ref = refs[:-1], refs[-1]
    high = place_ref[3]
    tail = jnp.zeros((SMALL, 2 * D), F32)
    for j, piece in enumerate(pieces):
        out_ref[rows_at(high ^ j, rows), :] = piece[0:rows, :]
        tail = tail + piece[rows : rows + SMALL, :].astype(F32)
    out_ref[len(pieces) * rows : len(pieces) * rows + SMALL, :] = tail.astype(BF16)


def join_attention_kernel(rows, depth, place_ref, *refs):
    pieces, out_ref = refs[:-1], refs[-1]
    low = place_ref[4]
    tail = jnp.zeros((SMALL, 2 * D), F32)
    for k, piece in enumerate(pieces):
        for high in range(depth):
            out_ref[rows_at(high * 4 + (low ^ k), rows), :] = piece[
                high * rows : (high + 1) * rows, :
            ]
        tail = tail + piece[depth * rows : depth * rows + SMALL, :].astype(F32)
    out_ref[D : D + SMALL, :] = tail.astype(BF16)


def join_gathered_kernel(rows, pieces_ref, out_ref, *sends):
    tail = jnp.zeros((SMALL, 2 * D), F32)
    for at in range(D // rows):
        piece = pieces_ref[at, 0:rows, :]
        out_ref[at * rows : (at + 1) * rows, :] = piece
        for half, ref in enumerate(sends):
            ref[at * rows : (at + 1) * rows, :] = piece[:, half * D : (half + 1) * D]
        tail = tail + pieces_ref[at, rows : rows + SMALL, :].astype(F32)
    out_ref[D : D + SMALL, :] = tail.astype(BF16)
    for half, ref in enumerate(sends):
        ref[D : D + SMALL, :] = tail[:, half * D : (half + 1) * D].astype(BF16)


def join_plane_kernel(rows, place_ref, *refs):
    pieces, outs = refs[:PLANE], refs[PLANE:]
    count = 2 * PLANE * rows
    for out_ref in outs:
        for k, piece in enumerate(pieces):
            out_ref[rows_at(place_ref[1] ^ k, 2 * rows), :] = piece[...]
        if out_ref.shape[0] > count:
            out_ref[count : count + SMALL, :] = jnp.zeros((SMALL, FFH), BF16)


def join_levels_kernel(rows, place_ref, *refs):
    pieces, outs = refs[:-2], refs[-2:]
    for j, piece in enumerate(pieces):
        for role in range(PLANE):
            at = rows_at(spot_of(place_ref[2] ^ j, role), rows)
            for part in range(2):
                first = (2 * role + part) * rows
                for out_ref in outs:
                    out_ref[part, at, :] = piece[first : first + rows, :]


def split_levels_kernel(rows, depth, keep_ref, got_ref, out_ref):
    block = PLANE * rows
    low = slice(2 * D, 2 * D + SMALL)
    tail = (keep_ref[low, :].astype(F32) + got_ref[low, :].astype(F32)).astype(BF16)
    for level in range(depth):
        for part in range(2):
            at = slice(part * D + level * block, part * D + (level + 1) * block)
            out_ref[level, part * block : (part + 1) * block, :] = (
                keep_ref[at, :].astype(F32) + got_ref[at, :].astype(F32)
            ).astype(BF16)
        out_ref[level, 2 * block : 2 * block + SMALL, :] = tail


def split_roles_kernel(rows, depth, keep_ref, got_ref, out_ref):
    for role in range(PLANE):
        for level in range(depth):
            first = spot_of(level, role) * rows
            at = slice(first, first + rows)
            out_ref[role, level * rows : (level + 1) * rows, :] = (
                keep_ref[at, :].astype(F32) + got_ref[at, :].astype(F32)
            ).astype(BF16)


def split_expert_kernel(rows, place_ref, keep_ref, got_ref, own_ref, far_ref, near_ref, next_ref):
    block = PLANE * rows
    low = slice(2 * D, 2 * D + SMALL)
    tail = keep_ref[low, :].astype(F32) + got_ref[low, :].astype(F32)
    for j, ref in ((3, far_ref), (1, near_ref), (2, next_ref), (0, own_ref)):
        for part in range(2):
            for role in range(PLANE):
                at = rows_at(spot_of(place_ref[2] ^ j, role), rows, part * D)
                first = part * block + role * rows
                ref[first : first + rows, :] = (
                    keep_ref[at, :].astype(F32) + got_ref[at, :].astype(F32)
                ).astype(ref.dtype)
        if j != 1:
            ref[2 * block : 2 * block + SMALL, :] = tail.astype(ref.dtype)


def add_kernel(own_ref, got_ref, out_ref):
    out_ref[...] = (own_ref[...].astype(F32) + got_ref[...].astype(F32)).astype(BF16)


def spread_expert_kernel(
    rows, place_ref, own_ref, far_ref, near_ref, next_ref, last_ref, *outs
):
    block = PLANE * rows
    base = 2 * block
    each = 2 * rows + SMALL
    tail = own_ref[base : base + SMALL, :] + far_ref[base : base + SMALL, :].astype(F32)
    tail = tail + next_ref[base : base + SMALL, :].astype(F32)
    for k, out in enumerate(outs):
        for part in range(2):
            at = rows_at(place_ref[1] ^ k, rows, part * block)
            first = part * rows
            out[first : first + rows, :] = (
                own_ref[at, :] + near_ref[at, :].astype(F32) + next_ref[at, :].astype(F32)
            ).astype(BF16)
            out[each + first : each + first + rows, :] = last_ref[at, :]
        out[2 * rows : each, :] = tail.astype(BF16)
        out[each + 2 * rows : 2 * each, :] = last_ref[base : base + SMALL, :]


def split_attention_kernel(rows, depth, place_ref, keep_ref, *refs):
    gots, outs = refs[: len(PARTS)], refs[len(PARTS) :]
    low = place_ref[4]
    for got_ref, cut in zip(gots, PARTS):
        tail = keep_ref[D : D + SMALL, cut] + got_ref[D : D + SMALL, :].astype(F32)
        for k, out in enumerate(outs):
            for high in range(depth):
                at = rows_at(high * 4 + (low ^ k), rows)
                out[high * rows : (high + 1) * rows, cut] = (
                    keep_ref[at, cut] + got_ref[at, :].astype(F32)
                ).astype(out.dtype)
            out[depth * rows : depth * rows + SMALL, cut] = tail.astype(out.dtype)


def spread_attention_kernel(rows, depth, place_ref, *refs):
    pieces, last_ref, (keep_ref, send_ref) = refs[:PLANE], refs[PLANE], refs[PLANE + 1 :]
    high = place_ref[3]
    base = depth * rows

    def summed(at):
        total = pieces[0][at, :]
        for piece in pieces[1:]:
            total = total + piece[at, :].astype(F32)
        return total

    tail = summed(slice(base, base + SMALL))
    for ref, flip in ((keep_ref, 0), (send_ref, 1)):
        for at in range(2):
            index = rows_at(high ^ (flip + 2 * at), rows)
            first = 2 * at * rows
            ref[first : first + rows, :] = summed(index).astype(ref.dtype)
            ref[first + rows : first + 2 * rows, :] = last_ref[index, :].astype(ref.dtype)
        ref[4 * rows : 4 * rows + SMALL, :] = tail.astype(ref.dtype)


def halve_attention_kernel(rows, own_ref, got_ref, keep_ref, send_ref):
    total = own_ref[...] + got_ref[...].astype(F32)
    tail = total[4 * rows : 4 * rows + SMALL]
    for ref, at in ((keep_ref, 0), (send_ref, 2 * rows)):
        ref[0 : 2 * rows, :] = total[at : at + 2 * rows].astype(ref.dtype)
        ref[2 * rows : 2 * rows + SMALL, :] = tail.astype(ref.dtype)


def exact(a, b):
    return lax.dot_general(
        a, b, (((1,), (1,)), ((), ())), precision=lax.Precision.HIGHEST, preferred_element_type=F32
    )


def own_attention(rows, me, first, tail, last, outs):
    gain1, bias1, qkv, qv, output, shift, gain2, bias2, router = outs
    for layer, body in enumerate((first, last)):
        for part in range(3):
            qkv[layer, part] = body[:, part * HALF : (part + 1) * HALF]
        output[layer] = body[:, 3 * HALF : 4 * HALF]
        small = tail[8 * layer : 8 * layer + 8]
        left = exact(small[:, 0:D], one_hot(me, rows, D, F32))
        right = exact(small[:, D : 2 * D], one_hot(me, rows, D, F32))
        for ref, values, row in (
            (gain1, left, 0),
            (bias1, right, 0),
            (shift, left, 1),
            (gain2, right, 1),
            (bias2, left, 2),
        ):
            ref[layer : layer + 1, :] = values[row : row + 1]
        for e in range(EXPERTS):
            values = (left, right)[e % 2]
            router[layer, e : e + 1, :] = values[3 + e // 2 : 4 + e // 2]
        width = qv.shape[2]
        for part in range(2):
            values = exact(
                small[:, D + part * HALF : D + (part + 1) * HALF], one_hot(me, width, HALF, F32)
            )
            qv[layer, part : part + 1, :] = values[2:3]


def own_attention_kernel(rows, place_ref, own_ref, got_ref, *outs):
    total = own_ref[...] + got_ref[...].astype(F32)
    tail = total[2 * rows : 2 * rows + SMALL]
    own_attention(rows, place_ref[0], total[0:rows], tail, total[rows : 2 * rows], outs)


def own_experts_kernel(rows, place_ref, *refs):
    pieces = refs[:PLANE]
    inner_ref, in_bias_ref, outer_ref, out_bias_ref = refs[PLANE:]
    each = 2 * rows + SMALL
    me, role = place_ref[0], place_ref[1]
    in_place = one_hot(me, in_bias_ref.shape[2], FFH)
    out_place = one_hot(me, rows, D)
    for layer in range(2):
        for k in range(PLANE):
            piece = pieces[k].at[layer * each : (layer + 1) * each]
            expert = role ^ k
            inner_ref[layer, expert] = piece[0:rows, :].astype(F32)
            outer_ref[layer, expert] = piece[rows : 2 * rows, :].astype(F32)
            tail = piece[2 * rows : 2 * rows + SMALL, :]
            out_bias_ref[layer, pl.ds(expert, 1), :] = mm_t(tail[:, 0:D], out_place)[0:1]
            in_bias_ref[layer, pl.ds(expert, 1), :] = mm_t(tail, in_place)[1:2]


class Order:
    def __init__(self, place):
        self.last = ()
        self.place = place

    def run(self, kernel, out_shape, operands, name, fixed=(), place=True, through=()):
        count = len(out_shape)
        fars = [at for at in range(count) if not isinstance(out_shape[at], jax.ShapeDtypeStruct)]
        if not fars:
            out_shape = [*out_shape, shape((8, 128), F32)]

        def body(*refs):
            if fars:
                kernel(*fixed, *refs)
            else:
                kernel(*fixed, *refs[:-1])
                refs[-1][...] = jnp.zeros((8, 128), F32)

        if place:
            operands = (self.place, *operands)
        outs = list(call(body, out_shape, operands, name, self.last, through, int(place)))
        if fars:
            sized = [outs[at] for at in fars]
            token = far(min(sized, key=lambda out: out.size * out.dtype.itemsize))
        else:
            token = outs.pop(count)
        self.last = (token,)
        return outs

    def gate(self, through):
        def kernel(place_ref, out_ref):
            out_ref[...] = jnp.zeros_like(out_ref)

        return self.run(kernel, [shape((8, 128), F32)], (), "gate", through=through)[1:]

    def main(self, kernel, out_shape, operands, name, through=(), place=False):
        outs = self.run(kernel, out_shape, operands, name, (), place, through)
        count = len(out_shape)
        return outs[:count], outs[count:]


class Moves:
    def __init__(self, dp, order, me, role, level):
        self.dp, self.order = dp, order
        self.me, self.role, self.level = me, role, level
        self.depth, self.rows = dp // PLANE, D // dp

    def swap(self, x, mask):
        return lax.ppermute(x, "dp", [(i, i ^ mask) for i in range(self.dp)])

    def swap_core(self, x):
        return lax.ppermute(x, "tensor", [(0, 1), (1, 0)])

    def kept(self, x):
        return far(x)

    def to_role(self, x, k):
        return self.swap(x, spot_of(0, k))

    def to_level(self, x, j):
        return self.swap(x, spot_of(j, 0))

    def exchange(self, blocks):
        return [blocks[0]] + [self.to_role(blocks[k], k) for k in range(1, PLANE)]


class FastMoves(Moves):
    def one(self, *args, **kwargs):
        return self.order.run(*args, **kwargs)[0]

    def begin(self, weights):
        rows = self.rows
        outs = [shape((rows + SMALL, 2 * D), BF16), shape((rows + 2 * SMALL, 2 * D), BF16)]
        outs += [shape((2 * rows, FFH), BF16)] * (2 * PLANE)
        first, last, *sends = self.order.run(
            pack_kernel, outs, all_far(weights), "pack", (rows,)
        )
        exp0 = self.exchange(sends[:PLANE])
        att0 = [first] + [self.swap(first, 4 * j) for j in range(1, self.depth)]
        return att0, exp0, lax.all_gather(last, "dp"), sends[PLANE:]

    def groups(self, index):
        firsts = {}
        for level in range(self.depth):
            for role in range(PLANE):
                key = level if index == 0 else role
                firsts.setdefault(key, []).append(spot_of(level, role))
        return list(firsts.values())

    def plane0(self, pieces):
        out = [shape((2 * PLANE * self.rows, FFH), BF16)]
        own = self.one(join_plane_kernel, out, pieces, "join_plane", (self.rows,))
        return [own, self.to_level(own, 1), self.to_level(own, 2)]

    def stack0(self, pieces):
        out = [shape((self.depth * self.rows + SMALL, 2 * D), BF16)]
        message = self.one(stack_attention_kernel, out, pieces, "stack_attention", (self.rows,))
        return [message] + [self.swap(message, k) for k in range(1, 4)]

    def join0(self, pieces, exp0, exp1, given):
        out = [far_shape((D + SMALL, 2 * D), BF16)]
        fixed = (self.rows, self.depth)
        own, near, next_, *rest = self.order.run(
            join_attention_kernel,
            out,
            pieces,
            "join_attention",
            fixed,
            through=[*exp0[1:3], *exp1[1:], *given],
        )
        sends, given = rest[: PLANE - 1], rest[PLANE - 1 :]
        exp0 = [exp0[0], near, next_, self.to_level(next_, 1)]
        return (own, self.swap_core(own)), exp0, self.exchange([exp1[0], *sends]), given

    def plane1(self, pieces):
        count = 2 * PLANE * self.rows
        out = [shape((count + SMALL, FFH), BF16), shape((count, FFH), BF16)]
        return self.order.run(join_plane_kernel, out, pieces, "join_plane", (self.rows,))

    def forward(self, piece):
        return self.to_level(piece, 1)

    def join_last(self, gathered):
        out = [far_shape((D + SMALL, 2 * D), BF16)] + [shape((D + SMALL, D), BF16)] * 2
        own, left, right = self.order.run(
            join_gathered_kernel, out, (far(gathered),), "join_gathered", (self.rows,), False
        )
        return own, self.swap_core(left), self.swap_core(right)

    def join_levels(self, pieces, through=()):
        out = [far_shape((2, D, FFH), BF16), shape((2, D, FFH), BF16)]
        own, send, *through = self.order.run(
            join_levels_kernel, out, all_far(pieces), "join_levels", (self.rows,), through=through
        )
        return (own, self.swap_core(send)), through

    def last_attention_1(self, operands):
        (keep, send), _ = self.order.main(
            attention_grads_kernel,
            [shape((D, 2 * D), BF16)] * 2,
            operands,
            "attention_grads1",
        )
        return keep, self.swap_core(send)

    def last_expert_1(self, operands):
        (keep, send), _ = self.order.main(
            expert_grads_pair_kernel, EXPERT_SUMS, operands, "expert_grads1"
        )
        return keep, self.swap_core(send)

    def last_sums_1(self, keep, got):
        out = [shape((self.depth, 2 * PLANE * self.rows + SMALL, FFH), BF16)]
        fixed = (self.rows, self.depth)
        sums = self.one(split_levels_kernel, out, (far(keep), far(got)), "split_levels", fixed, False)
        return lax.psum_scatter(
            sums, "dp", scatter_dimension=0, axis_index_groups=self.groups(1)
        )

    def last_attention_2(self, keep, got):
        out = [shape((PLANE, self.depth * self.rows, 2 * D), BF16)]
        fixed = (self.rows, self.depth)
        sums = self.one(split_roles_kernel, out, (keep, got), "split_roles", fixed, False)
        return lax.psum_scatter(
            sums, "dp", scatter_dimension=0, axis_index_groups=self.groups(0)
        )

    def expert_sum_2(self, keep, got, through=()):
        count = 2 * PLANE * self.rows
        outs = [
            far_shape((count + SMALL, FFH), F32),
            shape((count + SMALL, FFH), BF16),
            shape((count, FFH), BF16),
            far_shape((count + SMALL, FFH), BF16),
        ]
        own, third, near, next_, *through = self.order.run(
            split_expert_kernel, outs, (far(keep), got), "split_expert", (self.rows,), through=through
        )
        return [own, self.to_level(third, 1), self.to_level(near, 1), next_], through

    def expert_sum_3(self, state):
        own, third, near, next_ = state
        message = self.one(
            add_kernel,
            [shape(third.shape, BF16)],
            (far(next_), far(third)),
            "add_expert",
            place=False,
        )
        return [own, third, near, self.to_level(message, 2)]

    def expert_sum_4(self, state, last, through=()):
        outs = [shape((2 * (2 * self.rows + SMALL), FFH), BF16)] * PLANE
        state = (*state, last.reshape(2 * PLANE * self.rows + SMALL, FFH))
        blocks = self.order.run(
            spread_expert_kernel,
            outs,
            all_far(state),
            "spread_expert",
            (self.rows,),
            through=through,
        )
        return self.exchange(blocks[:PLANE]), blocks[PLANE:]

    def attention_sum_1(self, keep, sends):
        return keep, [self.swap_core(send) for send in sends]

    def attention_sum_2(self, state, through):
        dims = (self.depth * self.rows + SMALL, 2 * D)
        outs = [far_shape(dims, F32)] + [shape(dims, BF16)] * 3
        fixed = (self.rows, self.depth)
        operands = (far(state[0]), *state[1])
        blocks = self.order.run(
            split_attention_kernel, outs, operands, "split_attention", fixed, through=through
        )
        return [blocks[0]] + [self.swap(blocks[k], k) for k in range(1, 4)], blocks[4:]

    def attention_sum_3(self, pieces, last, through=()):
        outs = [
            shape((4 * self.rows + SMALL, 2 * D), F32),
            shape((4 * self.rows + SMALL, 2 * D), BF16),
        ]
        fixed = (self.rows, self.depth)
        operands = all_far((*pieces, last.reshape(self.depth * self.rows, 2 * D)))
        keep, send, *through = self.order.run(
            spread_attention_kernel, outs, operands, "spread_attention", fixed, through=through
        )
        return (keep, self.swap(send, 4)), through

    def attention_sum_4(self, state):
        outs = [
            shape((2 * self.rows + SMALL, 2 * D), F32),
            shape((2 * self.rows + SMALL, 2 * D), BF16),
        ]
        keep, send = self.order.run(
            halve_attention_kernel, outs, state, "halve_attention", (self.rows,), False
        )
        return keep, self.swap(send, 8)

    def own_attention(self, pieces):
        rows, dp = self.rows, self.dp
        outs = [
            shape((2, rows), F32),
            shape((2, rows), F32),
            shape((2, 3, rows, HALF), F32),
            shape((2, 2, HALF // dp), F32),
            shape((2, rows, HALF), F32),
            shape((2, rows), F32),
            shape((2, rows), F32),
            shape((2, rows), F32),
            shape((2, EXPERTS, rows), F32),
        ]
        return self.order.run(
            own_attention_kernel, outs, pieces, "own_attention", (rows,)
        )

    def own_experts(self, pieces):
        rows = self.rows
        outs = [
            shape((2, EXPERTS, rows, FFH), F32),
            shape((2, EXPERTS, FFH // self.dp), F32),
            shape((2, EXPERTS, rows, FFH), F32),
            shape((2, EXPERTS, rows), F32),
        ]
        return self.order.run(own_experts_kernel, outs, pieces, "own_experts", (rows,))


class PlainMoves(Moves):
    def kept(self, x):
        return x

    def by_index(self, pieces, me):
        return jnp.take(jnp.stack(pieces), me ^ jnp.arange(len(pieces)), axis=0)

    def relative(self, array, me, axis):
        return jnp.take(array, me ^ jnp.arange(array.shape[axis]), axis=axis)

    def spots(self):
        return [spot_of(j, k) for j in range(self.depth) for k in range(PLANE)]

    def total(self, pieces):
        return sum(piece.astype(F32) for piece in pieces)

    def pack(self, layer, weights):
        (
            norm1_gain,
            norm1_bias,
            output_bias,
            norm2_gain,
            norm2_bias,
            router_weight,
            expert_out_bias,
            qv_bias,
            expert_in_bias,
            qkv_weight,
            output_weight,
            expert_in,
            expert_out,
        ) = [weight[layer] for weight in weights]
        vectors = (norm1_gain, norm1_bias, output_bias, norm2_gain, norm2_bias)

        def placed(values, width):
            extent = values.shape[-1]
            column = jnp.arange(extent)[:, None] + self.me * extent
            spot = (column == jnp.arange(width)[None, :]).astype(BF16)
            return jnp.dot(values, spot, preferred_element_type=F32).astype(BF16)

        wide = placed(jnp.stack(vectors), D)
        router = placed(router_weight, D)
        shifts = placed(qv_bias, HALF).reshape(1, D)
        outer = placed(expert_out_bias, D)
        small = jnp.concatenate([wide, shifts, router, outer], axis=0).reshape(7, 2 * D)
        inner = placed(expert_in_bias, FFH)
        body = jnp.concatenate([*qkv_weight, output_weight], axis=1)
        blank = jnp.zeros((SMALL - 11, 2 * D), BF16)
        shard = jnp.concatenate([body, small, inner, blank], axis=0)
        experts = jnp.stack([expert_in, expert_out], axis=1)
        return shard, list(self.relative(experts, self.role, 0))

    def begin(self, weights):
        shard0, sends0 = self.pack(0, weights)
        shard1, sends1 = self.pack(1, weights)
        return shard0, [jnp.stack(sends0)], shard1, [jnp.stack(sends1)]

    def plane0(self, pieces):
        return pieces * 3

    def plane1(self, pieces):
        return pieces * 2

    def stack0(self, shard):
        return shard

    def join0(self, shard, exp0, exp1, given):
        own, left, right = self.join_last(shard)
        return (own, jnp.concatenate([left, right], axis=1)), exp0, exp1, given

    def forward(self, piece):
        return piece

    def join_last(self, shard):
        gathered = lax.all_gather(shard, "dp")
        body = gathered[:, : self.rows].reshape(D, 2 * D)
        tail = jnp.sum(gathered[:, self.rows :].astype(F32), axis=0).astype(BF16)
        own = jnp.concatenate([body, tail], axis=0)
        other = self.swap_core(own)
        return own, other[:, :D], other[:, D:]

    def join_levels(self, pieces, through=()):
        body = self.by_index(self.exchange(list(pieces[0])), self.role)
        pieces = [body] + [self.to_level(body, j) for j in range(1, self.depth)]
        stacked = self.by_index(pieces, self.level).reshape(self.dp, 2, self.rows, FFH)
        order = sorted(range(self.dp), key=lambda at: self.spots()[at])
        own = stacked[jnp.array(order)].transpose(1, 0, 2, 3).reshape(2, D, FFH)
        return (own, self.swap_core(own)), through

    def expert_sum_2(self, keep, got, through=()):
        return [keep, got, got, got], through

    def expert_sum_3(self, state):
        return state

    def expert_sum_4(self, state, last, through=()):
        return (self.sum_expert(*state[:2]), self.sum_expert(*last)), through

    def sum_expert(self, keep, got):
        rows, depth = self.rows, self.depth
        whole = keep.astype(F32) + got.astype(F32)
        tail = whole[2 * D :]
        body = whole[: 2 * D].reshape(2, self.dp, rows, FFH)[:, jnp.array(self.spots())]
        body = self.relative(body.reshape(2, depth, PLANE * rows, FFH), self.level, 1)
        low, low_tail = body.astype(BF16), tail.astype(BF16)
        count = 2 * PLANE * rows
        pieces = []
        for j in range(1, depth):
            message = jnp.concatenate([low[:, j].reshape(count, FFH), low_tail], axis=0)
            pieces.append(self.to_level(message, j))
        body = body[:, 0].reshape(count, FFH) + self.total([piece[:count] for piece in pieces])
        tail = tail + self.total([piece[count:] for piece in pieces])
        body = self.relative(body.reshape(2, PLANE, rows, FFH), self.role, 1).astype(BF16)
        tail = tail.astype(BF16)
        count = 2 * rows
        blocks = [
            jnp.concatenate([body[:, k].reshape(count, FFH), tail], axis=0) for k in range(PLANE)
        ]
        return self.exchange(blocks)

    def attention_sum_1(self, keep, sends):
        return keep, jnp.concatenate(sends, axis=1)

    def attention_sum_2(self, state, through):
        return state, through

    def attention_sum_3(self, state, last, through=()):
        return (state, last), through

    def attention_sum_4(self, state):
        (keep, send), last = state
        whole = keep + self.swap_core(send).astype(F32)
        body = lax.psum_scatter(whole[:D], "dp", scatter_dimension=0, tiled=True)
        return jnp.concatenate([body, lax.psum(whole[D:], "dp")], axis=0), last

    def last_attention_1(self, operands):
        (keep, send), _ = self.order.main(
            attention_grads_kernel,
            [shape((D, 2 * D), F32), shape((D, 2 * D), BF16)],
            operands,
            "attention_grads1",
        )
        return keep, self.swap_core(send)

    def last_expert_1(self, operands):
        (keep, send), _ = self.order.main(
            expert_grads_pair_kernel, EXPERT_SUMS, operands, "expert_grads1"
        )
        return keep, self.swap_core(send)

    def last_sums_1(self, keep, got):
        return keep, got

    def last_attention_2(self, keep, got):
        whole = keep + got.astype(F32)
        return lax.psum_scatter(whole, "dp", scatter_dimension=0, tiled=True)

    def own_attention(self, state):
        total, last = state
        rows = self.rows
        body = jnp.stack([total[:rows], last])
        tail = total[rows:].reshape(2, 16, D)

        def owned(values, width):
            return lax.dynamic_slice_in_dim(
                values, self.me * width, width, axis=values.ndim - 1
            )

        wide = owned(tail, rows)
        qkv = body[:, :, : 3 * HALF].reshape(2, rows, 3, HALF).transpose(0, 2, 1, 3)
        qv = owned(tail[:, 5].reshape(2, 2, HALF), HALF // self.dp)
        vectors = [wide[:, row] for row in range(5)]
        return (
            *vectors[:2],
            qkv,
            qv,
            body[:, :, 3 * HALF :],
            *vectors[2:],
            wide[:, 6:10],
        )

    def own_experts(self, state):
        first, last = state
        rows = self.rows
        owned = jnp.stack([self.by_index(first, self.role), self.by_index(last, self.role)])
        owned = owned.astype(F32)
        tail = owned[:, :, 2 * rows :]
        width = FFH // self.dp
        in_bias = lax.dynamic_slice_in_dim(tail[:, :, 1], self.me * width, width, axis=2)
        out_bias = lax.dynamic_slice_in_dim(tail[:, :, 0], self.me * rows, rows, axis=2)
        return owned[:, :, :rows], in_bias, owned[:, :, rows : 2 * rows], out_bias


def build(dp):
    def local(
        tokens,
        routes,
        norm1_gain,
        norm1_bias,
        qkv_weight,
        qv_bias,
        output_weight,
        output_bias,
        norm2_gain,
        norm2_bias,
        router_weight,
        expert_in,
        expert_in_bias,
        expert_out,
        expert_out_bias,
        grad_out,
    ):
        me = lax.axis_index("dp").astype(jnp.int32)
        core = lax.axis_index("tensor")
        role, level = me % PLANE, me // PLANE
        order = Order(
            jnp.stack([me, role, level, me // 4, me % 4, core.astype(jnp.int32)])
        )
        moves = (FastMoves if dp == 16 else PlainMoves)(dp, order, me, role, level)
        weights = (
            norm1_gain,
            norm1_bias,
            output_bias,
            norm2_gain,
            norm2_bias,
            router_weight.transpose(0, 2, 1),
            expert_out_bias,
            qv_bias,
            expert_in_bias,
            qkv_weight.transpose(0, 2, 1, 3),
            output_weight.transpose(0, 2, 1),
            expert_in,
            expert_out.transpose(0, 1, 3, 2),
        )

        att0, exp0, gathered1, exp1 = moves.begin(weights)

        choice = lax.dynamic_index_in_dim(routes, core, axis=1, keepdims=False)
        hot = (choice[..., None] == jnp.arange(EXPERTS)).astype(BF16)
        any_hot = hot[:, :, 0] + hot[:, :, 1]
        below = jnp.tril(jnp.ones((SEQ, SEQ), BF16), -1)
        slot = jnp.einsum("ts,lse->lte", below, any_hot, preferred_element_type=F32)
        slot = jnp.sum(hot.astype(F32) * slot[:, :, None], axis=-1).astype(jnp.int32)
        target = (choice ^ role) * CAP + slot
        columns = jnp.pad(
            jnp.concatenate([target, choice], axis=-1),
            ((0, 0), (0, SP - SEQ), (0, 0)),
            constant_values=-1,
        )
        target_rows = columns[:, :, 0:2].transpose(0, 2, 1)

        def image(values):
            values = lax.dynamic_index_in_dim(values, core, axis=0, keepdims=False)
            return jnp.pad(values, ((0, SP - SEQ), (0, 0)))

        rows, grad = image(tokens), image(grad_out)

        exp0 = moves.plane0(exp0)
        att0 = moves.stack0(att0)
        given = [rows, grad, columns[0], columns[1], target_rows[0], target_rows[1]]
        attention0, exp0, exp1, given = moves.join0(att0, exp0, exp1, given)
        rows, grad, columns, target_rows = given[0], given[1], given[2:4], given[4:6]

        kept0, _ = order.main(
            first_forward_kernel,
            forward_outs(False),
            (rows, *all_far(attention0), columns[0], target_rows[0]),
            "attention_first",
        )
        middle0, normed0, normed2_0, qkv0, mixed0, log0, probs0, small0 = kept0[:8]
        blocks0 = moves.exchange(kept0[8:])
        expert0, exp1[1:] = moves.join_levels(exp0, exp1[1:])
        exp1, early1 = moves.plane1(exp1)
        next1 = moves.to_level(early1, 2)
        (hidden0, slope0, *results), (exp1,) = order.main(
            expert_forward_kernel,
            expert_outs(False),
            all_far((*blocks0, *expert0)) + [small0],
            "expert_forward",
            [exp1],
            place=True,
        )
        slots0 = moves.exchange(results)
        near1 = moves.to_level(exp1, 1)
        next1, gathered1, *slots0[1:] = order.gate([next1, moves.kept(gathered1), *slots0[1:]])
        exp1 = [exp1, near1, next1, moves.forward(next1)]
        attention1 = moves.join_last(gathered1)

        (rows1, *kept1), _ = order.main(
            last_forward_kernel,
            [far_shape((SP, D), F32)] + forward_outs(True),
            (
                *all_far((middle0, probs0)),
                columns[0],
                *all_far(slots0),
                grad,
                *all_far(attention1),
                columns[1],
                target_rows[1],
            ),
            "attention_last",
        )
        middle1, normed1, normed2_1, qkv1, mixed1, log1, probs1, small1 = kept1[:8]
        blocks1 = moves.exchange(kept1[8:])
        expert1, _ = moves.join_levels(exp1)
        (hidden1, grad_pre1, *results), _ = order.main(
            expert_both_kernel,
            expert_outs(True),
            (*all_far(blocks1), *expert1, small1),
            "expert_both",
            place=True,
        )
        pairs1 = moves.exchange(results)
        sums1 = moves.last_expert_1((*all_far(blocks1), hidden1, grad_pre1))
        back1, _ = order.main(
            backward_last_kernel,
            backward_outs(True),
            (
                grad,
                *pairs1,
                *all_far((rows1, middle1, normed2_1, qkv1, mixed1, log1, probs1)),
                columns[1],
                *all_far(attention1),
                far(probs0),
                columns[0],
                target_rows[0],
            ),
            "attention_back_last",
        )
        grad_rows1, grad_qkv1, grad_att1, keep1, send1, output = back1[:6]
        grads0 = moves.exchange(back1[6:])
        output_got = moves.swap_core(output)
        sums1 = moves.last_sums_1(*sums1)
        att_owned1 = moves.last_attention_1((far(normed1), grad_qkv1, grad_att1, far(mixed1)))

        (grad_pre0, *results), (output_got,) = order.main(
            expert_back_kernel,
            EXPERT_BACK,
            all_far((*grads0, slope0, *expert0)),
            "expert_back",
            [output_got],
        )
        slot_grads0 = moves.exchange(results)
        sums0, _ = order.main(
            expert_grads_single_kernel,
            EXPERT_SUMS,
            all_far((*blocks0, *grads0, hidden0)) + [grad_pre0],
            "expert_grads0",
        )
        att_owned1 = moves.last_attention_2(*att_owned1)
        sums0, slot_grads0[1:] = moves.expert_sum_2(
            sums0[0], moves.swap_core(sums0[1]), slot_grads0[1:]
        )
        (grad_rows0, grad_qkv0, grad_att0, keep0, send0), _ = order.main(
            backward_first_kernel,
            backward_outs(False),
            (
                far(grad_rows1),
                *all_far(slots0),
                *slot_grads0,
                rows,
                *all_far((middle0, normed2_0, qkv0, mixed0, log0, probs0)),
                columns[0],
                *all_far(attention0),
            ),
            "attention_back_first",
        )
        att_sums0, _ = order.main(
            attention_grads_small_kernel,
            ATTENTION_SUMS,
            (
                far(normed0),
                grad_qkv0,
                grad_att0,
                far(mixed0),
                keep0,
                send0,
                far(keep1),
                far(send1),
            ),
            "attention_grads0",
        )

        att_sums0 = moves.attention_sum_1(att_sums0[0], att_sums0[1:])
        sums0 = moves.expert_sum_3(sums0)
        att_sums0, (sums1,) = moves.attention_sum_2(att_sums0, [moves.kept(sums1)])
        att_sums0, _ = moves.attention_sum_3(att_sums0, att_owned1)
        sums0, (grad_rows0,) = moves.expert_sum_4(sums0, sums1, [grad_rows0])
        att_sums0 = moves.attention_sum_4(att_sums0)
        rows_got = moves.swap_core(grad_rows0)
        gain1, bias1, qkv, qv, out, shift, gain2, bias2, router = moves.own_attention(att_sums0)
        inner, in_bias, outer, out_bias = moves.own_experts(sums0)

        def both(values, others):
            first = jnp.where(core == 0, values, others)[:SEQ]
            second = jnp.where(core == 0, others, values)[:SEQ]
            return jnp.stack([first, second], axis=1).transpose(1, 0, 2)

        return (
            both(output, output_got),
            both(grad_rows0, rows_got),
            gain1,
            bias1,
            qkv.transpose(0, 2, 1, 3),
            qv,
            out.transpose(0, 2, 1),
            shift,
            gain2,
            bias2,
            router.transpose(0, 2, 1),
            inner,
            in_bias,
            outer.transpose(0, 1, 3, 2),
            out_bias,
        )

    return local


def solution(mesh):
    weights = (
        P(None, "dp"),
        P(None, "dp"),
        P(None, "dp", None, "tensor"),
        P(None, None, ("tensor", "dp")),
        P(None, "tensor", "dp"),
        P(None, "dp"),
        P(None, "dp"),
        P(None, "dp"),
        P(None, "dp", None),
        P(None, None, "dp", "tensor"),
        P(None, None, ("tensor", "dp")),
        P(None, None, "tensor", "dp"),
        P(None, None, "dp"),
    )
    images = P("dp", None, None)
    return jax.shard_map(
        build(mesh.shape["dp"]),
        mesh=mesh,
        in_specs=(images, P(None, "dp", None, None)) + weights + (images,),
        out_specs=(images, images) + weights,
        check_vma=False,
    )
```

```python
import jax
import jax.numpy as jnp
from jax import lax
from jax.experimental import pallas as pl
from jax.experimental.pallas import tpu as pltpu
from jax.sharding import PartitionSpec as P

D = 512
HD = 64
HALF = 256
FFH = 1024
SEQ = 197
SP = 208
EXPERTS = 4
CAP = 128
SLOTS = EXPERTS * CAP
PLANE = 4
SMALL = 16
EPSILON = 1e-06
SCALE = HD ** (-0.5)
MIB = 2**20
VMEM_MIB = 32
F32 = jnp.float32
BF16 = jnp.bfloat16


def call(kernel, out_shape, operands, name, after, through, scalars):
    inputs, outputs = len(operands), len(out_shape)

    def body(*refs):
        first = inputs + len(after) + len(through)
        kernel(*refs[:inputs], *refs[first : first + outputs])

    anywhere = pl.BlockSpec(memory_space=pl.ANY)
    whole = pl.BlockSpec(memory_space=pltpu.VMEM)
    return pl.pallas_call(
        body,
        out_shape=list(out_shape) + [shape(array.shape, array.dtype) for array in through],
        in_specs=[pl.BlockSpec(memory_space=pltpu.SMEM)] * scalars
        + [whole] * (inputs - scalars)
        + [anywhere] * (len(after) + len(through)),
        out_specs=[whole] * outputs + [anywhere] * len(through),
        input_output_aliases={
            inputs + len(after) + i: outputs + i for i in range(len(through))
        },
        compiler_params=pltpu.CompilerParams(vmem_limit_bytes=VMEM_MIB * MIB),
        cost_estimate=pl.CostEstimate(flops=1, bytes_accessed=1, transcendentals=0),
        name=name,
    )(*operands, *after, *through)


def shape(dims, dtype):
    return jax.ShapeDtypeStruct(dims, dtype)


def far_shape(dims, dtype):
    return pltpu.HBM(dims, dtype)


def far(array):
    return pltpu.with_memory_space_constraint(array, pltpu.HBM)


def all_far(arrays):
    return [far(array) for array in arrays]


def mm(a, b):
    return lax.dot_general(a, b, (((1,), (0,)), ((), ())), preferred_element_type=F32)


def mm_t(a, b):
    return lax.dot_general(a, b, (((1,), (1,)), ((), ())), preferred_element_type=F32)


def mm_tn(a, b):
    return lax.dot_general(a, b, (((0,), (0,)), ((), ())), preferred_element_type=F32)


def normalise(rows):
    center = rows - jnp.mean(rows, axis=-1, keepdims=True)
    inverse = lax.rsqrt(jnp.mean(center * center, axis=-1, keepdims=True) + EPSILON)
    return center * inverse, inverse


def norm_back(grad, hat, inverse, gain):
    scaled = grad * gain
    return inverse * (
        scaled
        - jnp.mean(scaled, axis=-1, keepdims=True)
        - hat * jnp.mean(scaled * hat, axis=-1, keepdims=True)
    )


def small_row(small, row, part):
    return small[row : row + 1, part * D : (part + 1) * D]


def router_rows(small):
    return [small_row(small, 3 + e // 2, e % 2) for e in range(EXPERTS)]


def select_columns(targets, j):
    lanes = lax.broadcasted_iota(jnp.int32, (SP, SLOTS), 1)
    return jnp.where(lanes == targets[:, j : j + 1], 1.0, 0.0).astype(BF16)


def select_rows(target_rows, j):
    subs = lax.broadcasted_iota(jnp.int32, (SLOTS, SP), 0)
    return jnp.where(subs == target_rows[j : j + 1, :], 1.0, 0.0).astype(BF16)


def chosen_of(targets, j):
    lanes = lax.broadcasted_iota(jnp.int32, (SP, EXPERTS), 1)
    return jnp.where(lanes == targets[:, 2 + j : 3 + j], 1.0, 0.0)


def gates_of(probs, targets):
    return [jnp.sum(chosen_of(targets, j) * probs, axis=-1, keepdims=True) for j in range(2)]


def attention_forward(rows, halves, targets, target_rows, outs, grad_rows):
    middle_ref, normed_ref, normed2_ref, qkv_ref, mixed_ref, log_ref, probs_ref = outs[:7]
    small_ref, send_refs = outs[7], outs[8:]
    small_ref[0] = halves[0][D : D + SMALL, :]
    small_ref[1] = halves[1][D : D + SMALL, :]
    small = halves[0][D : D + SMALL, :].astype(F32)
    hat, _ = normalise(rows)
    normed = (hat * small_row(small, 0, 0) + small_row(small, 0, 1)).astype(BF16)
    normed_ref[...] = normed
    attended = jnp.zeros((SP, D), F32)
    key_ok = lax.broadcasted_iota(jnp.int32, (SP, SP), 1) < SEQ
    logs = []
    for half in range(2):
        qkv = mm(normed, halves[half][0:D, 0 : 3 * HALF])
        shift = halves[half][D : D + SMALL, :][2:3, D : 2 * D].astype(F32)
        query = (qkv[:, 0:HALF] + shift[:, 0:HALF]).astype(BF16)
        key = qkv[:, HALF : 2 * HALF].astype(BF16)
        value = (qkv[:, 2 * HALF : 3 * HALF] + shift[:, HALF : 2 * HALF]).astype(BF16)
        qkv_ref[half] = jnp.concatenate([query, key, value], axis=1)
        mixed = []
        for head in range(HALF // HD):
            cut = slice(head * HD, (head + 1) * HD)
            scores = jnp.where(key_ok, mm_t(query[:, cut], key[:, cut]) * SCALE, -1e30)
            top = jnp.max(scores, axis=-1, keepdims=True)
            weight = jnp.exp(scores - top)
            total = jnp.sum(weight, axis=-1, keepdims=True)
            logs.append(top + jnp.log(total))
            low = (weight * (1.0 / total)).astype(BF16)
            mixed.append(mm(low, value[:, cut]).astype(BF16))
        mixed = jnp.concatenate(mixed, axis=1)
        mixed_ref[half] = mixed
        attended = attended + mm_t(mixed, halves[half][0:D, 3 * HALF : 4 * HALF])
    log_ref[...] = jnp.concatenate(logs, axis=1)
    middle = rows + attended + small_row(small, 1, 0)
    middle_ref[...] = middle
    hat2, _ = normalise(middle)
    normed2 = (hat2 * small_row(small, 1, 1) + small_row(small, 2, 0)).astype(BF16)
    normed2_ref[...] = normed2
    router = jnp.concatenate(router_rows(small) + [jnp.zeros((4, D), F32)], axis=0).astype(BF16)
    logits = mm_t(normed2, router)[:, 0:EXPERTS]
    weight = jnp.exp(logits - jnp.max(logits, axis=-1, keepdims=True))
    probs = weight / jnp.sum(weight, axis=-1, keepdims=True)
    probs_ref[...] = probs
    picks = [select_rows(target_rows, j) for j in range(2)]
    sent = mm(picks[0] + picks[1], normed2).astype(BF16)
    if grad_rows is None:
        for k in range(PLANE):
            send_refs[k][...] = sent[k * CAP : (k + 1) * CAP]
    else:
        gates = gates_of(probs, targets)
        grads = (
            mm(picks[0], (gates[0] * grad_rows).astype(BF16))
            + mm(picks[1], (gates[1] * grad_rows).astype(BF16))
        ).astype(BF16)
        for k in range(PLANE):
            send_refs[k][0] = sent[k * CAP : (k + 1) * CAP]
            send_refs[k][1] = grads[k * CAP : (k + 1) * CAP]


def first_forward_kernel(rows_ref, own_ref, other_ref, targets_ref, target_rows_ref, *outs):
    attention_forward(
        rows_ref[...].astype(F32),
        (own_ref, other_ref),
        targets_ref[...],
        target_rows_ref[...],
        outs,
        None,
    )


def combine(middle, probs, targets, slot_rows):
    gates = gates_of(probs, targets)
    picked = [mm(select_columns(targets, j), slot_rows) for j in range(2)]
    return middle + gates[0] * picked[0] + gates[1] * picked[1], picked


def last_forward_kernel(
    middle_ref,
    probs_ref,
    prior_targets_ref,
    f0,
    f1,
    f2,
    f3,
    grad_ref,
    own_ref,
    left_ref,
    right_ref,
    targets_ref,
    target_rows_ref,
    rows_ref,
    *outs,
):
    slot_rows = jnp.concatenate([f0[...], f1[...], f2[...], f3[...]], axis=0)
    rows, _ = combine(middle_ref[...], probs_ref[...], prior_targets_ref[...], slot_rows)
    rows_ref[...] = rows
    attention_forward(
        rows,
        (own_ref, jnp.concatenate([left_ref[...], right_ref[...]], axis=1)),
        targets_ref[...],
        target_rows_ref[...],
        outs,
        grad_ref[...].astype(F32),
    )


def forward_outs(pair):
    block = (2, CAP, D) if pair else (CAP, D)
    return [
        far_shape((SP, D), F32),
        far_shape((SP, D), BF16),
        far_shape((SP, D), BF16),
        far_shape((2, SP, 3 * HALF), BF16),
        far_shape((2, SP, HALF), BF16),
        far_shape((SP, 8), F32),
        far_shape((SP, EXPERTS), F32),
        shape((2, SMALL, 2 * D), BF16),
    ] + [shape(block, BF16)] * PLANE


def backward_kernel(final, *refs):
    grad_ref, f0, f1, f2, f3 = refs[:5]
    refs = refs[5:]
    if not final:
        d0, d1, d2, d3 = refs[:4]
        refs = refs[4:]
    (
        rows_ref,
        middle_ref,
        normed2_ref,
        qkv_ref,
        mixed_ref,
        log_ref,
        probs_ref,
        targets_ref,
        own_ref,
        other,
    ) = refs[:10]
    rest = refs[10:]
    if final:
        other = jnp.concatenate([other[...], rest[0][...]], axis=1)
        rest = rest[1:]
        prior_probs_ref, prior_targets_ref, prior_target_rows_ref = rest[:3]
        rest = rest[3:]
    grad_rows_ref, grad_qkv_ref, grad_att_ref, small_keep_ref, small_send_ref = rest[:5]
    rest = rest[5:]
    halves = (own_ref, other)
    small = own_ref[D : D + SMALL, :].astype(F32)
    grad = grad_ref[...].astype(F32)
    targets = targets_ref[...]
    probs = probs_ref[...]
    middle = middle_ref[...]
    if final:
        slot_rows = jnp.concatenate([f0[0], f1[0], f2[0], f3[0]], axis=0)
        slot_grads = jnp.concatenate([f0[1], f1[1], f2[1], f3[1]], axis=0)
    else:
        slot_rows = jnp.concatenate([f0[...], f1[...], f2[...], f3[...]], axis=0)
        slot_grads = jnp.concatenate([d0[...], d1[...], d2[...], d3[...]], axis=0)
    picks = [select_columns(targets, j) for j in range(2)]
    picked = [mm(picks[j], slot_rows) for j in range(2)]
    if final:
        gates = gates_of(probs, targets)
        rest[0][...] = middle + gates[0] * picked[0] + gates[1] * picked[1]
    grad_probs = jnp.zeros((SP, EXPERTS), F32)
    for j in range(2):
        grad_probs = grad_probs + chosen_of(targets, j) * jnp.sum(
            grad * picked[j], axis=-1, keepdims=True
        )
    grad_logits = probs * (grad_probs - jnp.sum(probs * grad_probs, axis=-1, keepdims=True))
    grad_logits = grad_logits.astype(BF16).astype(F32)
    grad_normed2 = mm(picks[0] + picks[1], slot_grads)
    normed2 = normed2_ref[...].astype(F32)
    routers = router_rows(small)
    grad_router = []
    for e in range(EXPERTS):
        column = grad_logits[:, e : e + 1]
        grad_normed2 = grad_normed2 + column * routers[e]
        grad_router.append(jnp.sum(column * normed2, axis=0, keepdims=True))
    hat2, inverse2 = normalise(middle)
    grad_gain2 = jnp.sum(grad_normed2 * hat2, axis=0, keepdims=True)
    grad_bias2 = jnp.sum(grad_normed2, axis=0, keepdims=True)
    grad_middle = grad + norm_back(grad_normed2, hat2, inverse2, small_row(small, 1, 1))
    grad_att = grad_middle.astype(BF16)
    grad_att_ref[...] = grad_att
    grad_shift = jnp.sum(grad_att.astype(F32), axis=0, keepdims=True)
    key_ok = lax.broadcasted_iota(jnp.int32, (SP, SP), 1) < SEQ
    grad_normed = jnp.zeros((SP, D), F32)
    qv_rows = []
    for half in range(2):
        grad_mixed = mm(grad_att, halves[half][0:D, 3 * HALF : 4 * HALF]).astype(BF16)
        query = qkv_ref[half, :, 0:HALF]
        key = qkv_ref[half, :, HALF : 2 * HALF]
        value = qkv_ref[half, :, 2 * HALF : 3 * HALF]
        grad_q, grad_k, grad_v = [], [], []
        for head in range(HALF // HD):
            cut = slice(head * HD, (head + 1) * HD)
            at = half * (HALF // HD) + head
            scores = mm_t(query[:, cut], key[:, cut]) * SCALE - log_ref[:, at : at + 1]
            weight = jnp.exp(jnp.where(key_ok, scores, -1e30))
            grad_v.append(mm_tn(weight.astype(BF16), grad_mixed[:, cut]).astype(BF16))
            grad_weight = mm_t(grad_mixed[:, cut], value[:, cut])
            mean = jnp.sum(weight * grad_weight, axis=-1, keepdims=True)
            grad_scores = (weight * (grad_weight - mean)).astype(BF16)
            grad_q.append((mm(grad_scores, key[:, cut]) * SCALE).astype(BF16))
            grad_k.append((mm_tn(grad_scores, query[:, cut]) * SCALE).astype(BF16))
        grad_qkv = jnp.concatenate(grad_q + grad_k + grad_v, axis=1)
        grad_qkv_ref[half] = grad_qkv
        grad_normed = grad_normed + mm_t(grad_qkv, halves[half][0:D, 0 : 3 * HALF])
        sums = jnp.sum(grad_qkv.astype(F32), axis=0, keepdims=True)
        qv_rows.append(jnp.concatenate([sums[:, 0:HALF], sums[:, 2 * HALF : 3 * HALF]], axis=1))
    hat, inverse = normalise(rows_ref[...].astype(F32))
    grad_gain = jnp.sum(grad_normed * hat, axis=0, keepdims=True)
    grad_bias = jnp.sum(grad_normed, axis=0, keepdims=True)
    grad_rows = grad_middle + norm_back(grad_normed, hat, inverse, small_row(small, 0, 0))
    grad_rows_ref[...] = grad_rows
    for half, ref in enumerate((small_keep_ref, small_send_ref)):
        left = [grad_gain, grad_shift, grad_bias2, grad_router[0], grad_router[2]]
        right = [grad_bias, grad_gain2, qv_rows[half], grad_router[1], grad_router[3]]
        ref[...] = jnp.concatenate(
            [
                jnp.concatenate(left + [jnp.zeros((SMALL - 5, D), F32)], axis=0),
                jnp.concatenate(right + [jnp.zeros((SMALL - 5, D), F32)], axis=0),
            ],
            axis=1,
        )
    if final:
        prior_gates = gates_of(prior_probs_ref[...], prior_targets_ref[...])
        prior_rows = prior_target_rows_ref[...]
        sent = (
            mm(select_rows(prior_rows, 0), (prior_gates[0] * grad_rows).astype(BF16))
            + mm(select_rows(prior_rows, 1), (prior_gates[1] * grad_rows).astype(BF16))
        ).astype(BF16)
        for k in range(PLANE):
            rest[1 + k][...] = sent[k * CAP : (k + 1) * CAP]


def backward_last_kernel(*refs):
    backward_kernel(True, *refs)


def backward_first_kernel(*refs):
    backward_kernel(False, *refs)


def backward_outs(final):
    keep = far_shape if final else shape
    outs = [
        keep((SP, D), F32),
        shape((2, SP, 3 * HALF), BF16),
        shape((SP, D), BF16),
        keep((SMALL, 2 * D), F32),
        keep((SMALL, 2 * D), F32),
    ]
    if final:
        outs += [shape((SP, D), F32)] + [shape((CAP, D), BF16)] * PLANE
    return outs


def attention_grads_kernel(normed_ref, grad_qkv_ref, grad_att_ref, mixed_ref, *outs):
    normed = normed_ref[...]
    grad_att = grad_att_ref[...]
    for half, ref in enumerate(outs):
        ref[0:D, 0 : 3 * HALF] = mm_tn(normed, grad_qkv_ref[half]).astype(ref.dtype)
        ref[0:D, 3 * HALF : 4 * HALF] = mm_tn(grad_att, mixed_ref[half]).astype(ref.dtype)


PARTS = (slice(0, 384), slice(384, 768), slice(768, 1024))


def attention_grads_small_kernel(*refs):
    normed = refs[0][...]
    grad_qkv_ref, grad_att, mixed_ref, small = refs[1], refs[2][...], refs[3], refs[4:8]
    keep_ref, sends = refs[8], refs[9:]
    tails = [
        jnp.concatenate([small[half][0:8, :], small[2 + half][0:8, :]], axis=0)
        for half in range(2)
    ]
    keep_ref[0:D, 0 : 3 * HALF] = mm_tn(normed, grad_qkv_ref[0])
    keep_ref[0:D, 3 * HALF : 4 * HALF] = mm_tn(grad_att, mixed_ref[0])
    keep_ref[D : D + SMALL, :] = tails[0]
    for ref, cut in zip(sends, PARTS):
        if cut.stop <= 3 * HALF:
            ref[0:D, :] = mm_tn(normed, grad_qkv_ref[1, :, cut]).astype(BF16)
        else:
            ref[0:D, :] = mm_tn(grad_att, mixed_ref[1]).astype(BF16)
        ref[D : D + SMALL, :] = tails[1][:, cut].astype(BF16)


ATTENTION_SUMS = [far_shape((D + SMALL, 2 * D), F32)] + [
    shape((D + SMALL, cut.stop - cut.start), BF16) for cut in PARTS
]


CHUNK = 512


def gelu_parts(values):
    tail = 0.5 * (1.0 + lax.erf(values * 0.7071067811865476))
    density = jnp.exp(-0.5 * values * values) * 0.3989422804014327
    return values * tail, tail + values * density


def expert_bias(small, role):
    out_shift = jnp.zeros((1, D), F32)
    in_shift = jnp.zeros((1, FFH), F32)
    for e in range(EXPERTS):
        at = jnp.where(role == e, 1.0, 0.0)
        out_shift = out_shift + at * small_row(small, 5 + e // 2, e % 2)
        in_shift = in_shift + at * small[7 + e : 8 + e, :]
    return out_shift, in_shift


def expert_kernel(both, place_ref, *refs):
    blocks, (own_ref, other_ref, small_ref), outs = (
        refs[:PLANE],
        refs[PLANE : PLANE + 3],
        refs[PLANE + 3 :],
    )
    role = place_ref[1]
    hidden_ref, slope_ref = outs[:2]
    if both:
        inputs = jnp.concatenate([block[0] for block in blocks], axis=0)
        grads = jnp.concatenate([block[1] for block in blocks], axis=0)
        result = jnp.zeros((SLOTS, D), F32)
        result_grad = jnp.zeros((SLOTS, D), F32)
    else:
        inputs = jnp.concatenate([block[...] for block in blocks], axis=0)
        result = jnp.zeros((SLOTS, D), F32)
    out_shift = None
    for half, ref in enumerate((own_ref, other_ref)):
        shift, in_shift = expert_bias(small_ref[half].astype(F32), role)
        if half == 0:
            out_shift = shift
        for chunk in range(FFH // CHUNK):
            cut = slice(chunk * CHUNK, (chunk + 1) * CHUNK)
            columns = slice(half * FFH + chunk * CHUNK, half * FFH + (chunk + 1) * CHUNK)
            hidden, slope = gelu_parts(mm(inputs, ref[0, :, cut]) + in_shift[:, cut])
            hidden = hidden.astype(BF16)
            hidden_ref[:, columns] = hidden
            result = result + mm_t(hidden, ref[1, :, cut])
            if both:
                grad_pre = (mm(grads, ref[1, :, cut]) * slope).astype(BF16)
                slope_ref[:, columns] = grad_pre
                result_grad = result_grad + mm_t(grad_pre, ref[0, :, cut])
            else:
                slope_ref[:, columns] = slope.astype(BF16)
    result = (result + out_shift).astype(BF16)
    for k in range(PLANE):
        if both:
            outs[2 + k][0] = result[k * CAP : (k + 1) * CAP]
            outs[2 + k][1] = result_grad[k * CAP : (k + 1) * CAP].astype(BF16)
        else:
            outs[2 + k][...] = result[k * CAP : (k + 1) * CAP]


def expert_forward_kernel(*refs):
    expert_kernel(False, *refs)


def expert_both_kernel(*refs):
    expert_kernel(True, *refs)


def expert_outs(both):
    block = (2, CAP, D) if both else (CAP, D)
    kept = shape if both else far_shape
    return [kept((SLOTS, 2 * FFH), BF16)] * 2 + [shape(block, BF16)] * PLANE


def expert_back_kernel(*refs):
    blocks, (slope_ref, own_ref, other_ref, grad_pre_ref), outs = (
        refs[:PLANE],
        refs[PLANE : PLANE + 4],
        refs[PLANE + 4 :],
    )
    grads = jnp.concatenate([block[...] for block in blocks], axis=0)
    result = jnp.zeros((SLOTS, D), F32)
    for half, ref in enumerate((own_ref, other_ref)):
        for chunk in range(FFH // CHUNK):
            cut = slice(chunk * CHUNK, (chunk + 1) * CHUNK)
            columns = slice(half * FFH + chunk * CHUNK, half * FFH + (chunk + 1) * CHUNK)
            grad_pre = (mm(grads, ref[1, :, cut]) * slope_ref[:, columns].astype(F32)).astype(BF16)
            grad_pre_ref[:, columns] = grad_pre
            result = result + mm_t(grad_pre, ref[0, :, cut])
    for k in range(PLANE):
        outs[k][...] = result[k * CAP : (k + 1) * CAP].astype(BF16)


EXPERT_BACK = [shape((SLOTS, 2 * FFH), BF16)] + [shape((CAP, D), BF16)] * PLANE


def expert_grads_kernel(pair, *refs):
    if pair:
        blocks, (hidden_ref, grad_pre_ref, keep_ref, send_ref) = refs[:PLANE], refs[PLANE:]
        inputs = jnp.concatenate([block[0] for block in blocks], axis=0)
        grads = jnp.concatenate([block[1] for block in blocks], axis=0)
    else:
        blocks, (hidden_ref, grad_pre_ref, keep_ref, send_ref) = refs[: 2 * PLANE], refs[2 * PLANE :]
        inputs = jnp.concatenate([block[...] for block in blocks[:PLANE]], axis=0)
        grads = jnp.concatenate([block[...] for block in blocks[PLANE:]], axis=0)
    out_shift = jnp.sum(grads.astype(F32), axis=0, keepdims=True)
    out_shift = jnp.concatenate([out_shift, jnp.zeros((1, FFH - D), F32)], axis=1)
    for half, ref in enumerate((keep_ref, send_ref)):
        shifts = []
        for chunk in range(FFH // CHUNK):
            cut = slice(chunk * CHUNK, (chunk + 1) * CHUNK)
            columns = slice(half * FFH + chunk * CHUNK, half * FFH + (chunk + 1) * CHUNK)
            grad_pre = grad_pre_ref[:, columns]
            ref[0:D, cut] = mm_tn(inputs, grad_pre).astype(ref.dtype)
            ref[D : 2 * D, cut] = mm_tn(grads, hidden_ref[:, columns]).astype(ref.dtype)
            shifts.append(jnp.sum(grad_pre.astype(F32), axis=0, keepdims=True))
        tail = [out_shift, jnp.concatenate(shifts, axis=1), jnp.zeros((SMALL - 2, FFH), F32)]
        ref[2 * D : 2 * D + SMALL, :] = jnp.concatenate(tail, axis=0).astype(ref.dtype)


def expert_grads_pair_kernel(*refs):
    expert_grads_kernel(True, *refs)


def expert_grads_owned_kernel(levels, place_ref, *refs):
    blocks, (hidden_ref, grad_pre_ref, out_ref) = refs[:PLANE], refs[PLANE:]
    inputs = jnp.concatenate([block[0] for block in blocks], axis=0)
    grads = jnp.concatenate([block[1] for block in blocks], axis=0)
    out_shift = jnp.sum(grads.astype(F32), axis=0, keepdims=True)
    out_shift = jnp.concatenate([out_shift, jnp.zeros((1, FFH - D), F32)], axis=1)
    size = D // levels
    for half in range(2):
        shifts = []
        for chunk in range(FFH // CHUNK):
            cut = slice(chunk * CHUNK, (chunk + 1) * CHUNK)
            columns = slice(half * FFH + chunk * CHUNK, half * FFH + (chunk + 1) * CHUNK)
            grad_pre = grad_pre_ref[:, columns]
            sums = (mm_tn(inputs, grad_pre), mm_tn(grads, hidden_ref[:, columns]))
            for part in range(2):
                values = sums[part].astype(BF16)
                for level in range(levels):
                    out_ref[
                        2 * level + (place_ref[5] ^ half), part * size : (part + 1) * size, cut
                    ] = values[level * size : (level + 1) * size]
            shifts.append(jnp.sum(grad_pre.astype(F32), axis=0, keepdims=True))
        tail = [out_shift, jnp.concatenate(shifts, axis=1), jnp.zeros((SMALL - 2, FFH), F32)]
        tail = jnp.concatenate(tail, axis=0).astype(BF16)
        for level in range(levels):
            out_ref[2 * level + (place_ref[5] ^ half), 2 * size : 2 * size + SMALL, :] = tail


def expert_grads_single_kernel(*refs):
    expert_grads_kernel(False, *refs)


EXPERT_SUMS = [far_shape((2 * D + SMALL, FFH), BF16), shape((2 * D + SMALL, FFH), BF16)]


def spot_of(level, role):
    return role + PLANE * level


def rows_at(index, size, base=0):
    return pl.ds(base + pl.multiple_of(index * size, size), size)


def one_hot(me, extent, width, dtype=BF16):
    row = lax.broadcasted_iota(jnp.int32, (extent, width), 0)
    column = lax.broadcasted_iota(jnp.int32, (extent, width), 1)
    return jnp.where(row + me * extent == column, 1.0, 0.0).astype(dtype)


def pack_shard(layer, rows, me, refs, shard_ref):
    (gain1, bias1, shift, gain2, bias2, router, out_bias, qv, in_bias, qkv, output) = refs
    vectors = [ref[layer : layer + 1, :].astype(F32) for ref in (gain1, bias1, shift, gain2, bias2)]
    vectors = jnp.concatenate(vectors + [out_bias[layer].astype(F32)], axis=0)
    place = one_hot(me, rows, D)
    wide = mm(vectors.astype(BF16), place)
    router = mm(router[layer], place)
    shifts = mm(qv[layer], one_hot(me, qv.shape[2], HALF))
    shifts = jnp.concatenate([shifts[0:1], shifts[1:2]], axis=1)
    inner = mm(in_bias[layer], one_hot(me, in_bias.shape[2], FFH))
    left = [wide[0:1], wide[2:3], wide[4:5], router[0:1], router[2:3], wide[5:6], wide[7:8]]
    right = [wide[1:2], wide[3:4], shifts, router[1:2], router[3:4], wide[6:7], wide[8:9]]
    small = jnp.concatenate(
        [jnp.concatenate(left, axis=0), jnp.concatenate(right, axis=0)], axis=1
    )
    small = jnp.concatenate([small, inner, jnp.zeros((SMALL - 11, 2 * D), F32)], axis=0)
    shard_ref[rows : rows + SMALL, :] = small.astype(BF16)
    for part in range(3):
        shard_ref[0:rows, part * HALF : (part + 1) * HALF] = qkv[layer, part]
    shard_ref[0:rows, 3 * HALF : 4 * HALF] = output[layer]


def pack_kernel(rows, place_ref, *refs):
    first_ref, last_ref = refs[13:15]
    role = place_ref[1]
    expert_in, expert_out = refs[11:13]
    for layer in range(2):
        for k, ref in enumerate(refs[15 + layer * PLANE : 15 + (layer + 1) * PLANE]):
            ref[0:rows, :] = expert_in[layer, role ^ k]
            ref[rows : 2 * rows, :] = expert_out[layer, role ^ k]
    pack_shard(0, rows, place_ref[0], refs[:11], first_ref)
    pack_shard(1, rows, place_ref[0], refs[:11], last_ref)
    last_ref[rows + SMALL : rows + 2 * SMALL, :] = jnp.zeros((SMALL, 2 * D), BF16)


def stack_attention_kernel(rows, place_ref, *refs):
    pieces, out_ref = refs[:-1], refs[-1]
    high = place_ref[3]
    tail = jnp.zeros((SMALL, 2 * D), F32)
    for j, piece in enumerate(pieces):
        out_ref[rows_at(high ^ j, rows), :] = piece[0:rows, :]
        tail = tail + piece[rows : rows + SMALL, :].astype(F32)
    out_ref[len(pieces) * rows : len(pieces) * rows + SMALL, :] = tail.astype(BF16)


def join_attention_kernel(rows, depth, place_ref, *refs):
    pieces, out_ref = refs[:-1], refs[-1]
    low = place_ref[4]
    tail = jnp.zeros((SMALL, 2 * D), F32)
    for k, piece in enumerate(pieces):
        for high in range(depth):
            out_ref[rows_at(high * 4 + (low ^ k), rows), :] = piece[
                high * rows : (high + 1) * rows, :
            ]
        tail = tail + piece[depth * rows : depth * rows + SMALL, :].astype(F32)
    out_ref[D : D + SMALL, :] = tail.astype(BF16)


def join_gathered_kernel(rows, pieces_ref, out_ref, *sends):
    tail = jnp.zeros((SMALL, 2 * D), F32)
    for at in range(D // rows):
        piece = pieces_ref[at, 0:rows, :]
        out_ref[at * rows : (at + 1) * rows, :] = piece
        for half, ref in enumerate(sends):
            ref[at * rows : (at + 1) * rows, :] = piece[:, half * D : (half + 1) * D]
        tail = tail + pieces_ref[at, rows : rows + SMALL, :].astype(F32)
    out_ref[D : D + SMALL, :] = tail.astype(BF16)
    for half, ref in enumerate(sends):
        ref[D : D + SMALL, :] = tail[:, half * D : (half + 1) * D].astype(BF16)


def join_plane_kernel(rows, place_ref, *refs):
    pieces, outs = refs[:PLANE], refs[PLANE:]
    count = 2 * PLANE * rows
    for out_ref in outs:
        for k, piece in enumerate(pieces):
            out_ref[rows_at(place_ref[1] ^ k, 2 * rows), :] = piece[...]
        if out_ref.shape[0] > count:
            out_ref[count : count + SMALL, :] = jnp.zeros((SMALL, FFH), BF16)


def join_levels_kernel(rows, place_ref, *refs):
    pieces, outs = refs[:-2], refs[-2:]
    for j, piece in enumerate(pieces):
        for role in range(PLANE):
            at = rows_at(spot_of(place_ref[2] ^ j, role), rows)
            for part in range(2):
                first = (2 * role + part) * rows
                for out_ref in outs:
                    out_ref[part, at, :] = piece[first : first + rows, :]


def split_roles_kernel(rows, depth, keep_ref, got_ref, out_ref):
    for role in range(PLANE):
        for level in range(depth):
            first = spot_of(level, role) * rows
            at = slice(first, first + rows)
            out_ref[role, level * rows : (level + 1) * rows, :] = (
                keep_ref[at, :].astype(F32) + got_ref[at, :].astype(F32)
            ).astype(BF16)


def split_expert_kernel(rows, place_ref, keep_ref, got_ref, own_ref, far_ref, near_ref, next_ref):
    block = PLANE * rows
    low = slice(2 * D, 2 * D + SMALL)
    tail = keep_ref[low, :].astype(F32) + got_ref[low, :].astype(F32)
    for j, ref in ((3, far_ref), (1, near_ref), (2, next_ref), (0, own_ref)):
        for part in range(2):
            for role in range(PLANE):
                at = rows_at(spot_of(place_ref[2] ^ j, role), rows, part * D)
                first = part * block + role * rows
                ref[first : first + rows, :] = (
                    keep_ref[at, :].astype(F32) + got_ref[at, :].astype(F32)
                ).astype(ref.dtype)
        if j != 1:
            ref[2 * block : 2 * block + SMALL, :] = tail.astype(ref.dtype)


def add_kernel(own_ref, got_ref, out_ref):
    out_ref[...] = (own_ref[...].astype(F32) + got_ref[...].astype(F32)).astype(BF16)


def spread_expert_kernel(
    rows, place_ref, own_ref, far_ref, near_ref, next_ref, last_ref, *outs
):
    block = PLANE * rows
    base = 2 * block
    each = 2 * rows + SMALL
    tail = own_ref[base : base + SMALL, :] + far_ref[base : base + SMALL, :].astype(F32)
    tail = tail + next_ref[base : base + SMALL, :].astype(F32)
    for k, out in enumerate(outs):
        for part in range(2):
            at = rows_at(place_ref[1] ^ k, rows, part * block)
            first = part * rows
            out[first : first + rows, :] = (
                own_ref[at, :] + near_ref[at, :].astype(F32) + next_ref[at, :].astype(F32)
            ).astype(BF16)
            out[each + first : each + first + rows, :] = last_ref[at, :]
        out[2 * rows : each, :] = tail.astype(BF16)
        out[each + 2 * rows : 2 * each, :] = last_ref[base : base + SMALL, :]


def split_attention_kernel(rows, depth, place_ref, keep_ref, *refs):
    gots, outs = refs[: len(PARTS)], refs[len(PARTS) :]
    low = place_ref[4]
    for got_ref, cut in zip(gots, PARTS):
        tail = keep_ref[D : D + SMALL, cut] + got_ref[D : D + SMALL, :].astype(F32)
        for k, out in enumerate(outs):
            for high in range(depth):
                at = rows_at(high * 4 + (low ^ k), rows)
                out[high * rows : (high + 1) * rows, cut] = (
                    keep_ref[at, cut] + got_ref[at, :].astype(F32)
                ).astype(out.dtype)
            out[depth * rows : depth * rows + SMALL, cut] = tail.astype(out.dtype)


def spread_attention_kernel(rows, depth, place_ref, *refs):
    pieces, last_ref, (keep_ref, send_ref) = refs[:PLANE], refs[PLANE], refs[PLANE + 1 :]
    high = place_ref[3]
    base = depth * rows

    def summed(at):
        total = pieces[0][at, :]
        for piece in pieces[1:]:
            total = total + piece[at, :].astype(F32)
        return total

    tail = summed(slice(base, base + SMALL))
    for ref, flip in ((keep_ref, 0), (send_ref, 1)):
        for at in range(2):
            index = rows_at(high ^ (flip + 2 * at), rows)
            first = 2 * at * rows
            ref[first : first + rows, :] = summed(index).astype(ref.dtype)
            ref[first + rows : first + 2 * rows, :] = last_ref[index, :].astype(ref.dtype)
        ref[4 * rows : 4 * rows + SMALL, :] = tail.astype(ref.dtype)


def halve_attention_kernel(rows, own_ref, got_ref, keep_ref, send_ref):
    total = own_ref[...] + got_ref[...].astype(F32)
    tail = total[4 * rows : 4 * rows + SMALL]
    for ref, at in ((keep_ref, 0), (send_ref, 2 * rows)):
        ref[0 : 2 * rows, :] = total[at : at + 2 * rows].astype(ref.dtype)
        ref[2 * rows : 2 * rows + SMALL, :] = tail.astype(ref.dtype)


def exact(a, b):
    return lax.dot_general(
        a, b, (((1,), (1,)), ((), ())), precision=lax.Precision.HIGHEST, preferred_element_type=F32
    )


def own_attention(rows, me, first, tail, last, outs):
    gain1, bias1, qkv, qv, output, shift, gain2, bias2, router = outs
    for layer, body in enumerate((first, last)):
        for part in range(3):
            qkv[layer, part] = body[:, part * HALF : (part + 1) * HALF]
        output[layer] = body[:, 3 * HALF : 4 * HALF]
        small = tail[8 * layer : 8 * layer + 8]
        left = exact(small[:, 0:D], one_hot(me, rows, D, F32))
        right = exact(small[:, D : 2 * D], one_hot(me, rows, D, F32))
        for ref, values, row in (
            (gain1, left, 0),
            (bias1, right, 0),
            (shift, left, 1),
            (gain2, right, 1),
            (bias2, left, 2),
        ):
            ref[layer : layer + 1, :] = values[row : row + 1]
        for e in range(EXPERTS):
            values = (left, right)[e % 2]
            router[layer, e : e + 1, :] = values[3 + e // 2 : 4 + e // 2]
        width = qv.shape[2]
        for part in range(2):
            values = exact(
                small[:, D + part * HALF : D + (part + 1) * HALF], one_hot(me, width, HALF, F32)
            )
            qv[layer, part : part + 1, :] = values[2:3]


def own_attention_kernel(rows, place_ref, own_ref, got_ref, *outs):
    total = own_ref[...] + got_ref[...].astype(F32)
    tail = total[2 * rows : 2 * rows + SMALL]
    own_attention(rows, place_ref[0], total[0:rows], tail, total[rows : 2 * rows], outs)


def own_experts_kernel(rows, place_ref, *refs):
    pieces = refs[:PLANE]
    inner_ref, in_bias_ref, outer_ref, out_bias_ref = refs[PLANE:]
    each = 2 * rows + SMALL
    me, role = place_ref[0], place_ref[1]
    in_place = one_hot(me, in_bias_ref.shape[2], FFH)
    out_place = one_hot(me, rows, D)
    for layer in range(2):
        for k in range(PLANE):
            piece = pieces[k].at[layer * each : (layer + 1) * each]
            expert = role ^ k
            inner_ref[layer, expert] = piece[0:rows, :].astype(F32)
            outer_ref[layer, expert] = piece[rows : 2 * rows, :].astype(F32)
            tail = piece[2 * rows : 2 * rows + SMALL, :]
            out_bias_ref[layer, pl.ds(expert, 1), :] = mm_t(tail[:, 0:D], out_place)[0:1]
            in_bias_ref[layer, pl.ds(expert, 1), :] = mm_t(tail, in_place)[1:2]


class Order:
    def __init__(self, place):
        self.last = ()
        self.place = place

    def run(self, kernel, out_shape, operands, name, fixed=(), place=True, through=()):
        count = len(out_shape)
        fars = [at for at in range(count) if not isinstance(out_shape[at], jax.ShapeDtypeStruct)]
        if not fars:
            out_shape = [*out_shape, shape((8, 128), F32)]

        def body(*refs):
            if fars:
                kernel(*fixed, *refs)
            else:
                kernel(*fixed, *refs[:-1])
                refs[-1][...] = jnp.zeros((8, 128), F32)

        if place:
            operands = (self.place, *operands)
        outs = list(call(body, out_shape, operands, name, self.last, through, int(place)))
        if fars:
            sized = [outs[at] for at in fars]
            token = far(min(sized, key=lambda out: out.size * out.dtype.itemsize))
        else:
            token = outs.pop(count)
        self.last = (token,)
        return outs

    def gate(self, through):
        def kernel(place_ref, out_ref):
            out_ref[...] = jnp.zeros_like(out_ref)

        return self.run(kernel, [shape((8, 128), F32)], (), "gate", through=through)[1:]

    def main(self, kernel, out_shape, operands, name, through=(), place=False):
        outs = self.run(kernel, out_shape, operands, name, (), place, through)
        count = len(out_shape)
        return outs[:count], outs[count:]


class Moves:
    def __init__(self, dp, order, me, role, level):
        self.dp, self.order = dp, order
        self.me, self.role, self.level = me, role, level
        self.depth, self.rows = dp // PLANE, D // dp

    def swap(self, x, mask):
        return lax.ppermute(x, "dp", [(i, i ^ mask) for i in range(self.dp)])

    def swap_core(self, x):
        return lax.ppermute(x, "tensor", [(0, 1), (1, 0)])

    def kept(self, x):
        return far(x)

    def to_role(self, x, k):
        return self.swap(x, spot_of(0, k))

    def to_level(self, x, j):
        return self.swap(x, spot_of(j, 0))

    def exchange(self, blocks):
        return [blocks[0]] + [self.to_role(blocks[k], k) for k in range(1, PLANE)]


class FastMoves(Moves):
    def one(self, *args, **kwargs):
        return self.order.run(*args, **kwargs)[0]

    def begin(self, weights):
        rows = self.rows
        outs = [shape((rows + SMALL, 2 * D), BF16), shape((rows + 2 * SMALL, 2 * D), BF16)]
        outs += [shape((2 * rows, FFH), BF16)] * (2 * PLANE)
        first, last, *sends = self.order.run(
            pack_kernel, outs, all_far(weights), "pack", (rows,)
        )
        exp0 = self.exchange(sends[:PLANE])
        att0 = [first] + [self.swap(first, 4 * j) for j in range(1, self.depth)]
        return att0, exp0, lax.all_gather(last, "dp"), sends[PLANE:]

    def groups(self, index):
        firsts = {}
        for level in range(self.depth):
            for role in range(PLANE):
                key = level if index == 0 else role
                firsts.setdefault(key, []).append(spot_of(level, role))
        return list(firsts.values())

    def plane0(self, pieces):
        out = [shape((2 * PLANE * self.rows, FFH), BF16)]
        own = self.one(join_plane_kernel, out, pieces, "join_plane", (self.rows,))
        return [own, self.to_level(own, 1), self.to_level(own, 2)]

    def stack0(self, pieces):
        out = [shape((self.depth * self.rows + SMALL, 2 * D), BF16)]
        message = self.one(stack_attention_kernel, out, pieces, "stack_attention", (self.rows,))
        return [message] + [self.swap(message, k) for k in range(1, 4)]

    def join0(self, pieces, exp0, exp1, given):
        out = [far_shape((D + SMALL, 2 * D), BF16)]
        fixed = (self.rows, self.depth)
        own, near, next_, *rest = self.order.run(
            join_attention_kernel,
            out,
            pieces,
            "join_attention",
            fixed,
            through=[*exp0[1:3], *exp1[1:], *given],
        )
        sends, given = rest[: PLANE - 1], rest[PLANE - 1 :]
        exp0 = [exp0[0], near, next_, self.to_level(next_, 1)]
        return (own, self.swap_core(own)), exp0, self.exchange([exp1[0], *sends]), given

    def plane1(self, pieces):
        count = 2 * PLANE * self.rows
        out = [shape((count + SMALL, FFH), BF16), shape((count, FFH), BF16)]
        return self.order.run(join_plane_kernel, out, pieces, "join_plane", (self.rows,))

    def forward(self, piece):
        return self.to_level(piece, 1)

    def join_last(self, gathered):
        out = [far_shape((D + SMALL, 2 * D), BF16)] + [shape((D + SMALL, D), BF16)] * 2
        own, left, right = self.order.run(
            join_gathered_kernel, out, (far(gathered),), "join_gathered", (self.rows,), False
        )
        return own, self.swap_core(left), self.swap_core(right)

    def join_levels(self, pieces, through=()):
        out = [far_shape((2, D, FFH), BF16), shape((2, D, FFH), BF16)]
        own, send, *through = self.order.run(
            join_levels_kernel, out, all_far(pieces), "join_levels", (self.rows,), through=through
        )
        return (own, self.swap_core(send)), through

    def last_attention_1(self, operands):
        (keep, send), _ = self.order.main(
            attention_grads_kernel,
            [shape((D, 2 * D), BF16)] * 2,
            operands,
            "attention_grads1",
        )
        return keep, self.swap_core(send)

    def last_expert(self, operands):
        out = [far_shape((2 * self.depth, 2 * PLANE * self.rows + SMALL, FFH), BF16)]
        sums = self.one(
            expert_grads_owned_kernel, out, operands, "expert_grads1", (self.depth,)
        )
        groups = [
            [2 * member + core for member in group for core in range(2)]
            for group in self.groups(1)
        ]
        return lax.psum_scatter(
            sums, ("dp", "tensor"), scatter_dimension=0, axis_index_groups=groups
        )

    def last_attention_2(self, keep, got):
        out = [far_shape((PLANE, self.depth * self.rows, 2 * D), BF16)]
        fixed = (self.rows, self.depth)
        sums = self.one(split_roles_kernel, out, (keep, got), "split_roles", fixed, False)
        return lax.psum_scatter(
            sums, "dp", scatter_dimension=0, axis_index_groups=self.groups(0)
        )

    def expert_sum_2(self, keep, got, through=()):
        count = 2 * PLANE * self.rows
        outs = [
            far_shape((count + SMALL, FFH), F32),
            shape((count + SMALL, FFH), BF16),
            shape((count, FFH), BF16),
            far_shape((count + SMALL, FFH), BF16),
        ]
        own, third, near, next_, *through = self.order.run(
            split_expert_kernel, outs, (far(keep), got), "split_expert", (self.rows,), through=through
        )
        return [own, self.to_level(third, 1), self.to_level(near, 1), next_], through

    def expert_sum_3(self, state):
        own, third, near, next_ = state
        message = self.one(
            add_kernel,
            [shape(third.shape, BF16)],
            (far(next_), far(third)),
            "add_expert",
            place=False,
        )
        return [own, third, near, self.to_level(message, 2)]

    def expert_sum_4(self, state, last, through=()):
        outs = [shape((2 * (2 * self.rows + SMALL), FFH), BF16)] * PLANE
        state = (*state, last.reshape(2 * PLANE * self.rows + SMALL, FFH))
        blocks = self.order.run(
            spread_expert_kernel,
            outs,
            all_far(state),
            "spread_expert",
            (self.rows,),
            through=through,
        )
        return self.exchange(blocks[:PLANE]), blocks[PLANE:]

    def attention_sum_1(self, keep, sends):
        return keep, [self.swap_core(send) for send in sends]

    def attention_sum_2(self, state, through):
        dims = (self.depth * self.rows + SMALL, 2 * D)
        outs = [far_shape(dims, F32)] + [shape(dims, BF16)] * 3
        fixed = (self.rows, self.depth)
        operands = (far(state[0]), *state[1])
        blocks = self.order.run(
            split_attention_kernel, outs, operands, "split_attention", fixed, through=through
        )
        return [blocks[0]] + [self.swap(blocks[k], k) for k in range(1, 4)], blocks[4:]

    def attention_sum_3(self, pieces, last, through=()):
        outs = [
            shape((4 * self.rows + SMALL, 2 * D), F32),
            shape((4 * self.rows + SMALL, 2 * D), BF16),
        ]
        fixed = (self.rows, self.depth)
        operands = all_far((*pieces, last.reshape(self.depth * self.rows, 2 * D)))
        keep, send, *through = self.order.run(
            spread_attention_kernel, outs, operands, "spread_attention", fixed, through=through
        )
        return (keep, self.swap(send, 4)), through

    def attention_sum_4(self, state):
        outs = [
            shape((2 * self.rows + SMALL, 2 * D), F32),
            shape((2 * self.rows + SMALL, 2 * D), BF16),
        ]
        keep, send = self.order.run(
            halve_attention_kernel, outs, state, "halve_attention", (self.rows,), False
        )
        return keep, self.swap(send, 8)

    def own_attention(self, pieces):
        rows, dp = self.rows, self.dp
        outs = [
            shape((2, rows), F32),
            shape((2, rows), F32),
            shape((2, 3, rows, HALF), F32),
            shape((2, 2, HALF // dp), F32),
            shape((2, rows, HALF), F32),
            shape((2, rows), F32),
            shape((2, rows), F32),
            shape((2, rows), F32),
            shape((2, EXPERTS, rows), F32),
        ]
        return self.order.run(
            own_attention_kernel, outs, pieces, "own_attention", (rows,)
        )

    def own_experts(self, pieces):
        rows = self.rows
        outs = [
            shape((2, EXPERTS, rows, FFH), F32),
            shape((2, EXPERTS, FFH // self.dp), F32),
            shape((2, EXPERTS, rows, FFH), F32),
            shape((2, EXPERTS, rows), F32),
        ]
        return self.order.run(own_experts_kernel, outs, pieces, "own_experts", (rows,))


class PlainMoves(Moves):
    def kept(self, x):
        return x

    def by_index(self, pieces, me):
        return jnp.take(jnp.stack(pieces), me ^ jnp.arange(len(pieces)), axis=0)

    def relative(self, array, me, axis):
        return jnp.take(array, me ^ jnp.arange(array.shape[axis]), axis=axis)

    def spots(self):
        return [spot_of(j, k) for j in range(self.depth) for k in range(PLANE)]

    def total(self, pieces):
        return sum(piece.astype(F32) for piece in pieces)

    def pack(self, layer, weights):
        (
            norm1_gain,
            norm1_bias,
            output_bias,
            norm2_gain,
            norm2_bias,
            router_weight,
            expert_out_bias,
            qv_bias,
            expert_in_bias,
            qkv_weight,
            output_weight,
            expert_in,
            expert_out,
        ) = [weight[layer] for weight in weights]
        vectors = (norm1_gain, norm1_bias, output_bias, norm2_gain, norm2_bias)

        def placed(values, width):
            extent = values.shape[-1]
            column = jnp.arange(extent)[:, None] + self.me * extent
            spot = (column == jnp.arange(width)[None, :]).astype(BF16)
            return jnp.dot(values, spot, preferred_element_type=F32).astype(BF16)

        wide = placed(jnp.stack(vectors), D)
        router = placed(router_weight, D)
        shifts = placed(qv_bias, HALF).reshape(1, D)
        outer = placed(expert_out_bias, D)
        small = jnp.concatenate([wide, shifts, router, outer], axis=0).reshape(7, 2 * D)
        inner = placed(expert_in_bias, FFH)
        body = jnp.concatenate([*qkv_weight, output_weight], axis=1)
        blank = jnp.zeros((SMALL - 11, 2 * D), BF16)
        shard = jnp.concatenate([body, small, inner, blank], axis=0)
        experts = jnp.stack([expert_in, expert_out], axis=1)
        return shard, list(self.relative(experts, self.role, 0))

    def begin(self, weights):
        shard0, sends0 = self.pack(0, weights)
        shard1, sends1 = self.pack(1, weights)
        return shard0, [jnp.stack(sends0)], shard1, [jnp.stack(sends1)]

    def plane0(self, pieces):
        return pieces * 3

    def plane1(self, pieces):
        return pieces * 2

    def stack0(self, shard):
        return shard

    def join0(self, shard, exp0, exp1, given):
        own, left, right = self.join_last(shard)
        return (own, jnp.concatenate([left, right], axis=1)), exp0, exp1, given

    def forward(self, piece):
        return piece

    def join_last(self, shard):
        gathered = lax.all_gather(shard, "dp")
        body = gathered[:, : self.rows].reshape(D, 2 * D)
        tail = jnp.sum(gathered[:, self.rows :].astype(F32), axis=0).astype(BF16)
        own = jnp.concatenate([body, tail], axis=0)
        other = self.swap_core(own)
        return own, other[:, :D], other[:, D:]

    def join_levels(self, pieces, through=()):
        body = self.by_index(self.exchange(list(pieces[0])), self.role)
        pieces = [body] + [self.to_level(body, j) for j in range(1, self.depth)]
        stacked = self.by_index(pieces, self.level).reshape(self.dp, 2, self.rows, FFH)
        order = sorted(range(self.dp), key=lambda at: self.spots()[at])
        own = stacked[jnp.array(order)].transpose(1, 0, 2, 3).reshape(2, D, FFH)
        return (own, self.swap_core(own)), through

    def expert_sum_2(self, keep, got, through=()):
        return [keep, got, got, got], through

    def expert_sum_3(self, state):
        return state

    def expert_sum_4(self, state, last, through=()):
        return (self.sum_expert(*state[:2]), self.sum_expert(*last)), through

    def sum_expert(self, keep, got):
        rows, depth = self.rows, self.depth
        whole = keep.astype(F32) + got.astype(F32)
        tail = whole[2 * D :]
        body = whole[: 2 * D].reshape(2, self.dp, rows, FFH)[:, jnp.array(self.spots())]
        body = self.relative(body.reshape(2, depth, PLANE * rows, FFH), self.level, 1)
        low, low_tail = body.astype(BF16), tail.astype(BF16)
        count = 2 * PLANE * rows
        pieces = []
        for j in range(1, depth):
            message = jnp.concatenate([low[:, j].reshape(count, FFH), low_tail], axis=0)
            pieces.append(self.to_level(message, j))
        body = body[:, 0].reshape(count, FFH) + self.total([piece[:count] for piece in pieces])
        tail = tail + self.total([piece[count:] for piece in pieces])
        body = self.relative(body.reshape(2, PLANE, rows, FFH), self.role, 1).astype(BF16)
        tail = tail.astype(BF16)
        count = 2 * rows
        blocks = [
            jnp.concatenate([body[:, k].reshape(count, FFH), tail], axis=0) for k in range(PLANE)
        ]
        return self.exchange(blocks)

    def attention_sum_1(self, keep, sends):
        return keep, jnp.concatenate(sends, axis=1)

    def attention_sum_2(self, state, through):
        return state, through

    def attention_sum_3(self, state, last, through=()):
        return (state, last), through

    def attention_sum_4(self, state):
        (keep, send), last = state
        whole = keep + self.swap_core(send).astype(F32)
        body = lax.psum_scatter(whole[:D], "dp", scatter_dimension=0, tiled=True)
        return jnp.concatenate([body, lax.psum(whole[D:], "dp")], axis=0), last

    def last_attention_1(self, operands):
        (keep, send), _ = self.order.main(
            attention_grads_kernel,
            [shape((D, 2 * D), F32), shape((D, 2 * D), BF16)],
            operands,
            "attention_grads1",
        )
        return keep, self.swap_core(send)

    def last_expert(self, operands):
        (keep, send), _ = self.order.main(
            expert_grads_pair_kernel, EXPERT_SUMS, operands, "expert_grads1"
        )
        return keep, self.swap_core(send)

    def last_attention_2(self, keep, got):
        whole = keep + got.astype(F32)
        return lax.psum_scatter(whole, "dp", scatter_dimension=0, tiled=True)

    def own_attention(self, state):
        total, last = state
        rows = self.rows
        body = jnp.stack([total[:rows], last])
        tail = total[rows:].reshape(2, 16, D)

        def owned(values, width):
            return lax.dynamic_slice_in_dim(
                values, self.me * width, width, axis=values.ndim - 1
            )

        wide = owned(tail, rows)
        qkv = body[:, :, : 3 * HALF].reshape(2, rows, 3, HALF).transpose(0, 2, 1, 3)
        qv = owned(tail[:, 5].reshape(2, 2, HALF), HALF // self.dp)
        vectors = [wide[:, row] for row in range(5)]
        return (
            *vectors[:2],
            qkv,
            qv,
            body[:, :, 3 * HALF :],
            *vectors[2:],
            wide[:, 6:10],
        )

    def own_experts(self, state):
        first, last = state
        rows = self.rows
        owned = jnp.stack([self.by_index(first, self.role), self.by_index(last, self.role)])
        owned = owned.astype(F32)
        tail = owned[:, :, 2 * rows :]
        width = FFH // self.dp
        in_bias = lax.dynamic_slice_in_dim(tail[:, :, 1], self.me * width, width, axis=2)
        out_bias = lax.dynamic_slice_in_dim(tail[:, :, 0], self.me * rows, rows, axis=2)
        return owned[:, :, :rows], in_bias, owned[:, :, rows : 2 * rows], out_bias


def build(dp):
    def local(
        tokens,
        routes,
        norm1_gain,
        norm1_bias,
        qkv_weight,
        qv_bias,
        output_weight,
        output_bias,
        norm2_gain,
        norm2_bias,
        router_weight,
        expert_in,
        expert_in_bias,
        expert_out,
        expert_out_bias,
        grad_out,
    ):
        me = lax.axis_index("dp").astype(jnp.int32)
        core = lax.axis_index("tensor")
        role, level = me % PLANE, me // PLANE
        order = Order(
            jnp.stack([me, role, level, me // 4, me % 4, core.astype(jnp.int32)])
        )
        moves = (FastMoves if dp == 16 else PlainMoves)(dp, order, me, role, level)
        weights = (
            norm1_gain,
            norm1_bias,
            output_bias,
            norm2_gain,
            norm2_bias,
            router_weight.transpose(0, 2, 1),
            expert_out_bias,
            qv_bias,
            expert_in_bias,
            qkv_weight.transpose(0, 2, 1, 3),
            output_weight.transpose(0, 2, 1),
            expert_in,
            expert_out.transpose(0, 1, 3, 2),
        )

        att0, exp0, gathered1, exp1 = moves.begin(weights)

        choice = lax.dynamic_index_in_dim(routes, core, axis=1, keepdims=False)
        hot = (choice[..., None] == jnp.arange(EXPERTS)).astype(BF16)
        any_hot = hot[:, :, 0] + hot[:, :, 1]
        below = jnp.tril(jnp.ones((SEQ, SEQ), BF16), -1)
        slot = jnp.einsum("ts,lse->lte", below, any_hot, preferred_element_type=F32)
        slot = jnp.sum(hot.astype(F32) * slot[:, :, None], axis=-1).astype(jnp.int32)
        target = (choice ^ role) * CAP + slot
        columns = jnp.pad(
            jnp.concatenate([target, choice], axis=-1),
            ((0, 0), (0, SP - SEQ), (0, 0)),
            constant_values=-1,
        )
        target_rows = columns[:, :, 0:2].transpose(0, 2, 1)

        def image(values):
            values = lax.dynamic_index_in_dim(values, core, axis=0, keepdims=False)
            return jnp.pad(values, ((0, SP - SEQ), (0, 0)))

        rows, grad = image(tokens), image(grad_out)

        exp0 = moves.plane0(exp0)
        att0 = moves.stack0(att0)
        given = [rows, grad, columns[0], columns[1], target_rows[0], target_rows[1]]
        attention0, exp0, exp1, given = moves.join0(att0, exp0, exp1, given)
        rows, grad, columns, target_rows = given[0], given[1], given[2:4], given[4:6]

        kept0, _ = order.main(
            first_forward_kernel,
            forward_outs(False),
            (rows, far(attention0[0]), attention0[1], columns[0], target_rows[0]),
            "attention_first",
        )
        middle0, normed0, normed2_0, qkv0, mixed0, log0, probs0, small0 = kept0[:8]
        blocks0 = moves.exchange(kept0[8:])
        expert0, exp1[1:] = moves.join_levels(exp0, exp1[1:])
        exp1, early1 = moves.plane1(exp1)
        next1 = moves.to_level(early1, 2)
        (hidden0, slope0, *results), (exp1,) = order.main(
            expert_forward_kernel,
            expert_outs(False),
            all_far((*blocks0, *expert0)) + [small0],
            "expert_forward",
            [exp1],
            place=True,
        )
        slots0 = moves.exchange(results)
        near1 = moves.to_level(exp1, 1)
        next1, gathered1, *slots0[1:] = order.gate([next1, moves.kept(gathered1), *slots0[1:]])
        exp1 = [exp1, near1, next1, moves.forward(next1)]
        attention1 = moves.join_last(gathered1)

        (rows1, *kept1), _ = order.main(
            last_forward_kernel,
            [far_shape((SP, D), F32)] + forward_outs(True),
            (
                *all_far((middle0, probs0)),
                columns[0],
                *all_far(slots0),
                grad,
                *all_far(attention1),
                columns[1],
                target_rows[1],
            ),
            "attention_last",
        )
        middle1, normed1, normed2_1, qkv1, mixed1, log1, probs1, small1 = kept1[:8]
        blocks1 = moves.exchange(kept1[8:])
        expert1, _ = moves.join_levels(exp1)
        (hidden1, grad_pre1, *results), _ = order.main(
            expert_both_kernel,
            expert_outs(True),
            (*all_far(blocks1), *expert1, small1),
            "expert_both",
            place=True,
        )
        pairs1 = moves.exchange(results)
        sums1 = moves.last_expert((*all_far(blocks1), hidden1, grad_pre1))
        back1, _ = order.main(
            backward_last_kernel,
            backward_outs(True),
            (
                grad,
                *pairs1,
                *all_far((rows1, middle1, normed2_1, qkv1, mixed1, log1, probs1)),
                columns[1],
                *all_far(attention1),
                far(probs0),
                columns[0],
                target_rows[0],
            ),
            "attention_back_last",
        )
        grad_rows1, grad_qkv1, grad_att1, keep1, send1, output = back1[:6]
        grads0 = moves.exchange(back1[6:])
        output_got = moves.swap_core(output)
        att_owned1 = moves.last_attention_1((far(normed1), grad_qkv1, grad_att1, far(mixed1)))

        att_owned1 = moves.last_attention_2(*att_owned1)
        (grad_pre0, *results), (output_got,) = order.main(
            expert_back_kernel,
            EXPERT_BACK,
            all_far((*grads0, slope0, *expert0)),
            "expert_back",
            [output_got],
        )
        slot_grads0 = moves.exchange(results)
        sums0, _ = order.main(
            expert_grads_single_kernel,
            EXPERT_SUMS,
            all_far((*blocks0, *grads0, hidden0)) + [grad_pre0],
            "expert_grads0",
        )
        sums0, slot_grads0[1:] = moves.expert_sum_2(
            sums0[0], moves.swap_core(sums0[1]), slot_grads0[1:]
        )
        (grad_rows0, grad_qkv0, grad_att0, keep0, send0), _ = order.main(
            backward_first_kernel,
            backward_outs(False),
            (
                far(grad_rows1),
                *all_far(slots0),
                *slot_grads0,
                rows,
                *all_far((middle0, normed2_0, qkv0, mixed0, log0, probs0)),
                columns[0],
                *all_far(attention0),
            ),
            "attention_back_first",
        )
        att_sums0, _ = order.main(
            attention_grads_small_kernel,
            ATTENTION_SUMS,
            (
                far(normed0),
                grad_qkv0,
                grad_att0,
                far(mixed0),
                keep0,
                send0,
                far(keep1),
                far(send1),
            ),
            "attention_grads0",
        )

        att_sums0 = moves.attention_sum_1(att_sums0[0], att_sums0[1:])
        sums0 = moves.expert_sum_3(sums0)
        att_sums0, (sums1,) = moves.attention_sum_2(att_sums0, [moves.kept(sums1)])
        att_sums0, _ = moves.attention_sum_3(att_sums0, att_owned1)
        sums0, (grad_rows0,) = moves.expert_sum_4(sums0, sums1, [grad_rows0])
        att_sums0 = moves.attention_sum_4(att_sums0)
        rows_got = moves.swap_core(grad_rows0)
        gain1, bias1, qkv, qv, out, shift, gain2, bias2, router = moves.own_attention(att_sums0)
        inner, in_bias, outer, out_bias = moves.own_experts(sums0)

        def both(values, others):
            first = jnp.where(core == 0, values, others)[:SEQ]
            second = jnp.where(core == 0, others, values)[:SEQ]
            return jnp.stack([first, second], axis=1).transpose(1, 0, 2)

        return (
            both(output, output_got),
            both(grad_rows0, rows_got),
            gain1,
            bias1,
            qkv.transpose(0, 2, 1, 3),
            qv,
            out.transpose(0, 2, 1),
            shift,
            gain2,
            bias2,
            router.transpose(0, 2, 1),
            inner,
            in_bias,
            outer.transpose(0, 1, 3, 2),
            out_bias,
        )

    return local


def solution(mesh):
    weights = (
        P(None, "dp"),
        P(None, "dp"),
        P(None, "dp", None, "tensor"),
        P(None, None, ("tensor", "dp")),
        P(None, "tensor", "dp"),
        P(None, "dp"),
        P(None, "dp"),
        P(None, "dp"),
        P(None, "dp", None),
        P(None, None, "dp", "tensor"),
        P(None, None, ("tensor", "dp")),
        P(None, None, "tensor", "dp"),
        P(None, None, "dp"),
    )
    images = P("dp", None, None)
    return jax.shard_map(
        build(mesh.shape["dp"]),
        mesh=mesh,
        in_specs=(images, P(None, "dp", None, None)) + weights + (images,),
        out_specs=(images, images) + weights,
        check_vma=False,
    )
```

```python
import jax
import jax.numpy as jnp
from jax import lax
from jax.experimental import pallas as pl
from jax.experimental.pallas import tpu as pltpu
from jax.sharding import PartitionSpec as P

D = 512
HD = 64
HALF = 256
FFH = 1024
SEQ = 197
SP = 208
EXPERTS = 4
CAP = 128
SLOTS = EXPERTS * CAP
PLANE = 4
SMALL = 16
EPSILON = 1e-06
SCALE = HD ** (-0.5)
MIB = 2**20
VMEM_MIB = 32
F32 = jnp.float32
BF16 = jnp.bfloat16


def call(kernel, out_shape, operands, name, after, through, scalars):
    inputs, outputs = len(operands), len(out_shape)

    def body(*refs):
        first = inputs + len(after) + len(through)
        kernel(*refs[:inputs], *refs[first : first + outputs])

    anywhere = pl.BlockSpec(memory_space=pl.ANY)
    whole = pl.BlockSpec(memory_space=pltpu.VMEM)
    return pl.pallas_call(
        body,
        out_shape=list(out_shape) + [shape(array.shape, array.dtype) for array in through],
        in_specs=[pl.BlockSpec(memory_space=pltpu.SMEM)] * scalars
        + [whole] * (inputs - scalars)
        + [anywhere] * (len(after) + len(through)),
        out_specs=[whole] * outputs + [anywhere] * len(through),
        input_output_aliases={
            inputs + len(after) + i: outputs + i for i in range(len(through))
        },
        compiler_params=pltpu.CompilerParams(vmem_limit_bytes=VMEM_MIB * MIB),
        cost_estimate=pl.CostEstimate(flops=1, bytes_accessed=1, transcendentals=0),
        name=name,
    )(*operands, *after, *through)


def shape(dims, dtype):
    return jax.ShapeDtypeStruct(dims, dtype)


def far_shape(dims, dtype):
    return pltpu.HBM(dims, dtype)


def far(array):
    return pltpu.with_memory_space_constraint(array, pltpu.HBM)


def all_far(arrays):
    return [far(array) for array in arrays]


def mm(a, b):
    return lax.dot_general(a, b, (((1,), (0,)), ((), ())), preferred_element_type=F32)


def mm_t(a, b):
    return lax.dot_general(a, b, (((1,), (1,)), ((), ())), preferred_element_type=F32)


def mm_tn(a, b):
    return lax.dot_general(a, b, (((0,), (0,)), ((), ())), preferred_element_type=F32)


def normalise(rows):
    center = rows - jnp.mean(rows, axis=-1, keepdims=True)
    inverse = lax.rsqrt(jnp.mean(center * center, axis=-1, keepdims=True) + EPSILON)
    return center * inverse, inverse


def norm_back(grad, hat, inverse, gain):
    scaled = grad * gain
    return inverse * (
        scaled
        - jnp.mean(scaled, axis=-1, keepdims=True)
        - hat * jnp.mean(scaled * hat, axis=-1, keepdims=True)
    )


def small_row(small, row, part):
    return small[row : row + 1, part * D : (part + 1) * D]


def router_rows(small):
    return [small_row(small, 3 + e // 2, e % 2) for e in range(EXPERTS)]


def select_columns(targets, j):
    lanes = lax.broadcasted_iota(jnp.int32, (SP, SLOTS), 1)
    return jnp.where(lanes == targets[:, j : j + 1], 1.0, 0.0).astype(BF16)


def select_rows(target_rows, j):
    subs = lax.broadcasted_iota(jnp.int32, (SLOTS, SP), 0)
    return jnp.where(subs == target_rows[j : j + 1, :], 1.0, 0.0).astype(BF16)


def chosen_of(targets, j):
    lanes = lax.broadcasted_iota(jnp.int32, (SP, EXPERTS), 1)
    return jnp.where(lanes == targets[:, 2 + j : 3 + j], 1.0, 0.0)


def gates_of(probs, targets):
    return [jnp.sum(chosen_of(targets, j) * probs, axis=-1, keepdims=True) for j in range(2)]


def attention_forward(rows, halves, targets, target_rows, outs, grad_rows):
    middle_ref, normed_ref, normed2_ref, qkv_ref, mixed_ref, log_ref, probs_ref = outs[:7]
    small_ref, send_refs = outs[7], outs[8:]
    small_ref[0] = halves[0][D : D + SMALL, :]
    small_ref[1] = halves[1][D : D + SMALL, :]
    small = halves[0][D : D + SMALL, :].astype(F32)
    hat, _ = normalise(rows)
    normed = (hat * small_row(small, 0, 0) + small_row(small, 0, 1)).astype(BF16)
    normed_ref[...] = normed
    attended = jnp.zeros((SP, D), F32)
    key_ok = lax.broadcasted_iota(jnp.int32, (SP, SP), 1) < SEQ
    logs = []
    for half in range(2):
        qkv = mm(normed, halves[half][0:D, 0 : 3 * HALF])
        shift = halves[half][D : D + SMALL, :][2:3, D : 2 * D].astype(F32)
        query = (qkv[:, 0:HALF] + shift[:, 0:HALF]).astype(BF16)
        key = qkv[:, HALF : 2 * HALF].astype(BF16)
        value = (qkv[:, 2 * HALF : 3 * HALF] + shift[:, HALF : 2 * HALF]).astype(BF16)
        qkv_ref[half] = jnp.concatenate([query, key, value], axis=1)
        mixed = []
        for head in range(HALF // HD):
            cut = slice(head * HD, (head + 1) * HD)
            scores = jnp.where(key_ok, mm_t(query[:, cut], key[:, cut]) * SCALE, -1e30)
            top = jnp.max(scores, axis=-1, keepdims=True)
            weight = jnp.exp(scores - top)
            total = jnp.sum(weight, axis=-1, keepdims=True)
            logs.append(top + jnp.log(total))
            low = (weight * (1.0 / total)).astype(BF16)
            mixed.append(mm(low, value[:, cut]).astype(BF16))
        mixed = jnp.concatenate(mixed, axis=1)
        mixed_ref[half] = mixed
        attended = attended + mm_t(mixed, halves[half][0:D, 3 * HALF : 4 * HALF])
    log_ref[...] = jnp.concatenate(logs, axis=1)
    middle = rows + attended + small_row(small, 1, 0)
    middle_ref[...] = middle
    hat2, _ = normalise(middle)
    normed2 = (hat2 * small_row(small, 1, 1) + small_row(small, 2, 0)).astype(BF16)
    normed2_ref[...] = normed2
    router = jnp.concatenate(router_rows(small) + [jnp.zeros((4, D), F32)], axis=0).astype(BF16)
    logits = mm_t(normed2, router)[:, 0:EXPERTS]
    weight = jnp.exp(logits - jnp.max(logits, axis=-1, keepdims=True))
    probs = weight / jnp.sum(weight, axis=-1, keepdims=True)
    probs_ref[...] = probs
    picks = [select_rows(target_rows, j) for j in range(2)]
    sent = mm(picks[0] + picks[1], normed2).astype(BF16)
    if grad_rows is None:
        for k in range(PLANE):
            send_refs[k][...] = sent[k * CAP : (k + 1) * CAP]
    else:
        gates = gates_of(probs, targets)
        grads = (
            mm(picks[0], (gates[0] * grad_rows).astype(BF16))
            + mm(picks[1], (gates[1] * grad_rows).astype(BF16))
        ).astype(BF16)
        for k in range(PLANE):
            send_refs[k][0] = sent[k * CAP : (k + 1) * CAP]
            send_refs[k][1] = grads[k * CAP : (k + 1) * CAP]


def first_forward_kernel(rows_ref, own_ref, other_ref, targets_ref, target_rows_ref, *outs):
    attention_forward(
        rows_ref[...].astype(F32),
        (own_ref, other_ref),
        targets_ref[...],
        target_rows_ref[...],
        outs,
        None,
    )


def combine(middle, probs, targets, slot_rows):
    gates = gates_of(probs, targets)
    picked = [mm(select_columns(targets, j), slot_rows) for j in range(2)]
    return middle + gates[0] * picked[0] + gates[1] * picked[1], picked


def last_forward_kernel(
    middle_ref,
    probs_ref,
    prior_targets_ref,
    f0,
    f1,
    f2,
    f3,
    grad_ref,
    own_ref,
    left_ref,
    right_ref,
    targets_ref,
    target_rows_ref,
    rows_ref,
    *outs,
):
    slot_rows = jnp.concatenate([f0[...], f1[...], f2[...], f3[...]], axis=0)
    rows, _ = combine(middle_ref[...], probs_ref[...], prior_targets_ref[...], slot_rows)
    rows_ref[...] = rows
    attention_forward(
        rows,
        (own_ref, jnp.concatenate([left_ref[...], right_ref[...]], axis=1)),
        targets_ref[...],
        target_rows_ref[...],
        outs,
        grad_ref[...].astype(F32),
    )


def forward_outs(pair):
    block = (2, CAP, D) if pair else (CAP, D)
    return [
        far_shape((SP, D), F32),
        far_shape((SP, D), BF16),
        far_shape((SP, D), BF16),
        far_shape((2, SP, 3 * HALF), BF16),
        far_shape((2, SP, HALF), BF16),
        far_shape((SP, 8), F32),
        far_shape((SP, EXPERTS), F32),
        shape((2, SMALL, 2 * D), BF16),
    ] + [shape(block, BF16)] * PLANE


def backward_kernel(final, *refs):
    grad_ref, f0, f1, f2, f3 = refs[:5]
    refs = refs[5:]
    if not final:
        d0, d1, d2, d3 = refs[:4]
        refs = refs[4:]
    (
        rows_ref,
        middle_ref,
        normed2_ref,
        qkv_ref,
        mixed_ref,
        log_ref,
        probs_ref,
        targets_ref,
        own_ref,
        other,
    ) = refs[:10]
    rest = refs[10:]
    if final:
        other = jnp.concatenate([other[...], rest[0][...]], axis=1)
        rest = rest[1:]
        prior_probs_ref, prior_targets_ref, prior_target_rows_ref = rest[:3]
        rest = rest[3:]
    grad_rows_ref, grad_qkv_ref, grad_att_ref, small_keep_ref, small_send_ref = rest[:5]
    rest = rest[5:]
    halves = (own_ref, other)
    small = own_ref[D : D + SMALL, :].astype(F32)
    grad = grad_ref[...].astype(F32)
    targets = targets_ref[...]
    probs = probs_ref[...]
    middle = middle_ref[...]
    if final:
        slot_rows = jnp.concatenate([f0[0], f1[0], f2[0], f3[0]], axis=0)
        slot_grads = jnp.concatenate([f0[1], f1[1], f2[1], f3[1]], axis=0)
    else:
        slot_rows = jnp.concatenate([f0[...], f1[...], f2[...], f3[...]], axis=0)
        slot_grads = jnp.concatenate([d0[...], d1[...], d2[...], d3[...]], axis=0)
    picks = [select_columns(targets, j) for j in range(2)]
    picked = [mm(picks[j], slot_rows) for j in range(2)]
    if final:
        gates = gates_of(probs, targets)
        rest[0][...] = middle + gates[0] * picked[0] + gates[1] * picked[1]
    grad_probs = jnp.zeros((SP, EXPERTS), F32)
    for j in range(2):
        grad_probs = grad_probs + chosen_of(targets, j) * jnp.sum(
            grad * picked[j], axis=-1, keepdims=True
        )
    grad_logits = probs * (grad_probs - jnp.sum(probs * grad_probs, axis=-1, keepdims=True))
    grad_logits = grad_logits.astype(BF16).astype(F32)
    grad_normed2 = mm(picks[0] + picks[1], slot_grads)
    normed2 = normed2_ref[...].astype(F32)
    routers = router_rows(small)
    grad_router = []
    for e in range(EXPERTS):
        column = grad_logits[:, e : e + 1]
        grad_normed2 = grad_normed2 + column * routers[e]
        grad_router.append(jnp.sum(column * normed2, axis=0, keepdims=True))
    hat2, inverse2 = normalise(middle)
    grad_gain2 = jnp.sum(grad_normed2 * hat2, axis=0, keepdims=True)
    grad_bias2 = jnp.sum(grad_normed2, axis=0, keepdims=True)
    grad_middle = grad + norm_back(grad_normed2, hat2, inverse2, small_row(small, 1, 1))
    grad_att = grad_middle.astype(BF16)
    grad_att_ref[...] = grad_att
    grad_shift = jnp.sum(grad_att.astype(F32), axis=0, keepdims=True)
    key_ok = lax.broadcasted_iota(jnp.int32, (SP, SP), 1) < SEQ
    grad_normed = jnp.zeros((SP, D), F32)
    qv_rows = []
    for half in range(2):
        grad_mixed = mm(grad_att, halves[half][0:D, 3 * HALF : 4 * HALF]).astype(BF16)
        query = qkv_ref[half, :, 0:HALF]
        key = qkv_ref[half, :, HALF : 2 * HALF]
        value = qkv_ref[half, :, 2 * HALF : 3 * HALF]
        grad_q, grad_k, grad_v = [], [], []
        for head in range(HALF // HD):
            cut = slice(head * HD, (head + 1) * HD)
            at = half * (HALF // HD) + head
            scores = mm_t(query[:, cut], key[:, cut]) * SCALE - log_ref[:, at : at + 1]
            weight = jnp.exp(jnp.where(key_ok, scores, -1e30))
            grad_v.append(mm_tn(weight.astype(BF16), grad_mixed[:, cut]).astype(BF16))
            grad_weight = mm_t(grad_mixed[:, cut], value[:, cut])
            mean = jnp.sum(weight * grad_weight, axis=-1, keepdims=True)
            grad_scores = (weight * (grad_weight - mean)).astype(BF16)
            grad_q.append((mm(grad_scores, key[:, cut]) * SCALE).astype(BF16))
            grad_k.append((mm_tn(grad_scores, query[:, cut]) * SCALE).astype(BF16))
        grad_qkv = jnp.concatenate(grad_q + grad_k + grad_v, axis=1)
        grad_qkv_ref[half] = grad_qkv
        grad_normed = grad_normed + mm_t(grad_qkv, halves[half][0:D, 0 : 3 * HALF])
        sums = jnp.sum(grad_qkv.astype(F32), axis=0, keepdims=True)
        qv_rows.append(jnp.concatenate([sums[:, 0:HALF], sums[:, 2 * HALF : 3 * HALF]], axis=1))
    hat, inverse = normalise(rows_ref[...].astype(F32))
    grad_gain = jnp.sum(grad_normed * hat, axis=0, keepdims=True)
    grad_bias = jnp.sum(grad_normed, axis=0, keepdims=True)
    grad_rows = grad_middle + norm_back(grad_normed, hat, inverse, small_row(small, 0, 0))
    grad_rows_ref[...] = grad_rows
    for half, ref in enumerate((small_keep_ref, small_send_ref)):
        left = [grad_gain, grad_shift, grad_bias2, grad_router[0], grad_router[2]]
        right = [grad_bias, grad_gain2, qv_rows[half], grad_router[1], grad_router[3]]
        ref[...] = jnp.concatenate(
            [
                jnp.concatenate(left + [jnp.zeros((SMALL - 5, D), F32)], axis=0),
                jnp.concatenate(right + [jnp.zeros((SMALL - 5, D), F32)], axis=0),
            ],
            axis=1,
        )
    if final:
        prior_gates = gates_of(prior_probs_ref[...], prior_targets_ref[...])
        prior_rows = prior_target_rows_ref[...]
        sent = (
            mm(select_rows(prior_rows, 0), (prior_gates[0] * grad_rows).astype(BF16))
            + mm(select_rows(prior_rows, 1), (prior_gates[1] * grad_rows).astype(BF16))
        ).astype(BF16)
        for k in range(PLANE):
            rest[1 + k][...] = sent[k * CAP : (k + 1) * CAP]


def backward_last_kernel(*refs):
    backward_kernel(True, *refs)


def backward_first_kernel(*refs):
    backward_kernel(False, *refs)


def backward_outs(final):
    keep = far_shape if final else shape
    outs = [
        keep((SP, D), F32),
        shape((2, SP, 3 * HALF), BF16),
        shape((SP, D), BF16),
        keep((SMALL, 2 * D), F32),
        keep((SMALL, 2 * D), F32),
    ]
    if final:
        outs += [shape((SP, D), F32)] + [shape((CAP, D), BF16)] * PLANE
    return outs


def attention_grads_kernel(normed_ref, grad_qkv_ref, grad_att_ref, mixed_ref, *outs):
    normed_t = normed_ref[...].T
    grad_att_t = grad_att_ref[...].T
    for half, ref in enumerate(outs):
        ref[0:D, 0 : 3 * HALF] = mm(normed_t, grad_qkv_ref[half]).astype(ref.dtype)
        ref[0:D, 3 * HALF : 4 * HALF] = mm(grad_att_t, mixed_ref[half]).astype(ref.dtype)


PARTS = (slice(0, 384), slice(384, 768), slice(768, 1024))


def attention_grads_small_kernel(*refs):
    normed_t, grad_att_t = refs[0][...].T, refs[2][...].T
    grad_qkv_ref, mixed_ref, small = refs[1], refs[3], refs[4:8]
    keep_ref, sends = refs[8], refs[9:]
    tails = [
        jnp.concatenate([small[half][0:8, :], small[2 + half][0:8, :]], axis=0)
        for half in range(2)
    ]
    keep_ref[0:D, 0 : 3 * HALF] = mm(normed_t, grad_qkv_ref[0]).astype(BF16)
    keep_ref[0:D, 3 * HALF : 4 * HALF] = mm(grad_att_t, mixed_ref[0]).astype(BF16)
    keep_ref[D : D + SMALL, :] = tails[0].astype(BF16)
    for ref, cut in zip(sends, PARTS):
        if cut.stop <= 3 * HALF:
            ref[0:D, :] = mm(normed_t, grad_qkv_ref[1, :, cut]).astype(BF16)
        else:
            ref[0:D, :] = mm(grad_att_t, mixed_ref[1]).astype(BF16)
        ref[D : D + SMALL, :] = tails[1][:, cut].astype(BF16)


ATTENTION_SUMS = [far_shape((D + SMALL, 2 * D), BF16)] + [
    shape((D + SMALL, cut.stop - cut.start), BF16) for cut in PARTS
]


CHUNK = 512


def gelu_parts(values):
    tail = 0.5 * (1.0 + lax.erf(values * 0.7071067811865476))
    density = jnp.exp(-0.5 * values * values) * 0.3989422804014327
    return values * tail, tail + values * density


def expert_bias(small, role):
    out_shift = jnp.zeros((1, D), F32)
    in_shift = jnp.zeros((1, FFH), F32)
    for e in range(EXPERTS):
        at = jnp.where(role == e, 1.0, 0.0)
        out_shift = out_shift + at * small_row(small, 5 + e // 2, e % 2)
        in_shift = in_shift + at * small[7 + e : 8 + e, :]
    return out_shift, in_shift


def expert_kernel(both, place_ref, *refs):
    blocks, (own_ref, other_ref, small_ref), outs = (
        refs[:PLANE],
        refs[PLANE : PLANE + 3],
        refs[PLANE + 3 :],
    )
    role = place_ref[1]
    hidden_ref, slope_ref = outs[:2]
    if both:
        inputs = jnp.concatenate([block[0] for block in blocks], axis=0)
        grads = jnp.concatenate([block[1] for block in blocks], axis=0)
        result = jnp.zeros((SLOTS, D), F32)
        result_grad = jnp.zeros((SLOTS, D), F32)
    else:
        inputs = jnp.concatenate([block[...] for block in blocks], axis=0)
        result = jnp.zeros((SLOTS, D), F32)
    out_shift = None
    for half, ref in enumerate((own_ref, other_ref)):
        shift, in_shift = expert_bias(small_ref[half].astype(F32), role)
        if half == 0:
            out_shift = shift
        for chunk in range(FFH // CHUNK):
            cut = slice(chunk * CHUNK, (chunk + 1) * CHUNK)
            columns = slice(half * FFH + chunk * CHUNK, half * FFH + (chunk + 1) * CHUNK)
            hidden, slope = gelu_parts(mm(inputs, ref[0, :, cut]) + in_shift[:, cut])
            hidden = hidden.astype(BF16)
            hidden_ref[:, columns] = hidden
            result = result + mm_t(hidden, ref[1, :, cut])
            if both:
                grad_pre = (mm(grads, ref[1, :, cut]) * slope).astype(BF16)
                slope_ref[:, columns] = grad_pre
                result_grad = result_grad + mm_t(grad_pre, ref[0, :, cut])
            else:
                slope_ref[:, columns] = slope.astype(BF16)
    result = (result + out_shift).astype(BF16)
    for k in range(PLANE):
        if both:
            outs[2 + k][0] = result[k * CAP : (k + 1) * CAP]
            outs[2 + k][1] = result_grad[k * CAP : (k + 1) * CAP].astype(BF16)
        else:
            outs[2 + k][...] = result[k * CAP : (k + 1) * CAP]


def expert_forward_kernel(*refs):
    expert_kernel(False, *refs)


def expert_both_kernel(*refs):
    expert_kernel(True, *refs)


def expert_outs(both):
    block = (2, CAP, D) if both else (CAP, D)
    kept = shape if both else far_shape
    return [kept((SLOTS, 2 * FFH), BF16)] * 2 + [shape(block, BF16)] * PLANE


def expert_back_kernel(*refs):
    blocks, (slope_ref, own_ref, other_ref, grad_pre_ref), outs = (
        refs[:PLANE],
        refs[PLANE : PLANE + 4],
        refs[PLANE + 4 :],
    )
    grads = jnp.concatenate([block[...] for block in blocks], axis=0)
    result = jnp.zeros((SLOTS, D), F32)
    for half, ref in enumerate((own_ref, other_ref)):
        for chunk in range(FFH // CHUNK):
            cut = slice(chunk * CHUNK, (chunk + 1) * CHUNK)
            columns = slice(half * FFH + chunk * CHUNK, half * FFH + (chunk + 1) * CHUNK)
            grad_pre = (mm(grads, ref[1, :, cut]) * slope_ref[:, columns].astype(F32)).astype(BF16)
            grad_pre_ref[:, columns] = grad_pre
            result = result + mm_t(grad_pre, ref[0, :, cut])
    for k in range(PLANE):
        outs[k][...] = result[k * CAP : (k + 1) * CAP].astype(BF16)


EXPERT_BACK = [shape((SLOTS, 2 * FFH), BF16)] + [shape((CAP, D), BF16)] * PLANE


def expert_grads_kernel(pair, *refs):
    if pair:
        blocks, (hidden_ref, grad_pre_ref, keep_ref, send_ref) = refs[:PLANE], refs[PLANE:]
        inputs = jnp.concatenate([block[0] for block in blocks], axis=0)
        grads = jnp.concatenate([block[1] for block in blocks], axis=0)
    else:
        blocks, (hidden_ref, grad_pre_ref, keep_ref, send_ref) = refs[: 2 * PLANE], refs[2 * PLANE :]
        inputs = jnp.concatenate([block[...] for block in blocks[:PLANE]], axis=0)
        grads = jnp.concatenate([block[...] for block in blocks[PLANE:]], axis=0)
    out_shift = jnp.sum(grads.astype(F32), axis=0, keepdims=True)
    out_shift = jnp.concatenate([out_shift, jnp.zeros((1, FFH - D), F32)], axis=1)
    inputs_t, grads_t = inputs.T, grads.T
    for half, ref in enumerate((keep_ref, send_ref)):
        shifts = []
        for chunk in range(FFH // CHUNK):
            cut = slice(chunk * CHUNK, (chunk + 1) * CHUNK)
            columns = slice(half * FFH + chunk * CHUNK, half * FFH + (chunk + 1) * CHUNK)
            grad_pre = grad_pre_ref[:, columns]
            ref[0:D, cut] = mm(inputs_t, grad_pre).astype(ref.dtype)
            ref[D : 2 * D, cut] = mm(grads_t, hidden_ref[:, columns]).astype(ref.dtype)
            shifts.append(jnp.sum(grad_pre.astype(F32), axis=0, keepdims=True))
        tail = [out_shift, jnp.concatenate(shifts, axis=1), jnp.zeros((SMALL - 2, FFH), F32)]
        ref[2 * D : 2 * D + SMALL, :] = jnp.concatenate(tail, axis=0).astype(ref.dtype)


def expert_grads_pair_kernel(*refs):
    expert_grads_kernel(True, *refs)


def expert_grads_owned_kernel(levels, place_ref, *refs):
    blocks, (hidden_ref, grad_pre_ref, out_ref) = refs[:PLANE], refs[PLANE:]
    inputs = jnp.concatenate([block[0] for block in blocks], axis=0)
    grads = jnp.concatenate([block[1] for block in blocks], axis=0)
    out_shift = jnp.sum(grads.astype(F32), axis=0, keepdims=True)
    out_shift = jnp.concatenate([out_shift, jnp.zeros((1, FFH - D), F32)], axis=1)
    size = D // levels
    inputs_t, grads_t = inputs.T, grads.T
    for half in range(2):
        shifts = []
        for chunk in range(FFH // CHUNK):
            cut = slice(chunk * CHUNK, (chunk + 1) * CHUNK)
            columns = slice(half * FFH + chunk * CHUNK, half * FFH + (chunk + 1) * CHUNK)
            grad_pre = grad_pre_ref[:, columns]
            sums = (mm(inputs_t, grad_pre), mm(grads_t, hidden_ref[:, columns]))
            for part in range(2):
                values = sums[part].astype(BF16)
                for level in range(levels):
                    out_ref[
                        2 * level + (place_ref[5] ^ half), part * size : (part + 1) * size, cut
                    ] = values[level * size : (level + 1) * size]
            shifts.append(jnp.sum(grad_pre.astype(F32), axis=0, keepdims=True))
        tail = [out_shift, jnp.concatenate(shifts, axis=1), jnp.zeros((SMALL - 2, FFH), F32)]
        tail = jnp.concatenate(tail, axis=0).astype(BF16)
        for level in range(levels):
            out_ref[2 * level + (place_ref[5] ^ half), 2 * size : 2 * size + SMALL, :] = tail


def expert_grads_single_kernel(*refs):
    expert_grads_kernel(False, *refs)


EXPERT_SUMS = [shape((2 * D + SMALL, FFH), BF16), shape((2 * D + SMALL, FFH), BF16)]


def spot_of(level, role):
    return role + PLANE * level


def rows_at(index, size, base=0):
    return pl.ds(base + pl.multiple_of(index * size, size), size)


def one_hot(me, extent, width, dtype=BF16):
    row = lax.broadcasted_iota(jnp.int32, (extent, width), 0)
    column = lax.broadcasted_iota(jnp.int32, (extent, width), 1)
    return jnp.where(row + me * extent == column, 1.0, 0.0).astype(dtype)


def pack_shard(layer, rows, me, refs, shard_ref):
    (gain1, bias1, shift, gain2, bias2, router, out_bias, qv, in_bias, qkv, output) = refs
    vectors = [ref[layer : layer + 1, :].astype(F32) for ref in (gain1, bias1, shift, gain2, bias2)]
    vectors = jnp.concatenate(vectors + [out_bias[layer].astype(F32)], axis=0)
    place = one_hot(me, rows, D)
    wide = mm(vectors.astype(BF16), place)
    router = mm(router[layer], place)
    shifts = mm(qv[layer], one_hot(me, qv.shape[2], HALF))
    shifts = jnp.concatenate([shifts[0:1], shifts[1:2]], axis=1)
    inner = mm(in_bias[layer], one_hot(me, in_bias.shape[2], FFH))
    left = [wide[0:1], wide[2:3], wide[4:5], router[0:1], router[2:3], wide[5:6], wide[7:8]]
    right = [wide[1:2], wide[3:4], shifts, router[1:2], router[3:4], wide[6:7], wide[8:9]]
    small = jnp.concatenate(
        [jnp.concatenate(left, axis=0), jnp.concatenate(right, axis=0)], axis=1
    )
    small = jnp.concatenate([small, inner, jnp.zeros((SMALL - 11, 2 * D), F32)], axis=0)
    shard_ref[rows : rows + SMALL, :] = small.astype(BF16)
    for part in range(3):
        shard_ref[0:rows, part * HALF : (part + 1) * HALF] = qkv[layer, part]
    shard_ref[0:rows, 3 * HALF : 4 * HALF] = output[layer]


def pack_kernel(rows, place_ref, *refs):
    first_ref, last_ref = refs[13:15]
    role = place_ref[1]
    expert_in, expert_out = refs[11:13]
    for layer in range(2):
        for k, ref in enumerate(refs[15 + layer * PLANE : 15 + (layer + 1) * PLANE]):
            ref[0:rows, :] = expert_in[layer, role ^ k]
            ref[rows : 2 * rows, :] = expert_out[layer, role ^ k]
    pack_shard(0, rows, place_ref[0], refs[:11], first_ref)
    pack_shard(1, rows, place_ref[0], refs[:11], last_ref)
    last_ref[rows + SMALL : rows + 2 * SMALL, :] = jnp.zeros((SMALL, 2 * D), BF16)


def stack_attention_kernel(rows, place_ref, *refs):
    pieces, out_ref = refs[:-1], refs[-1]
    high = place_ref[3]
    tail = jnp.zeros((SMALL, 2 * D), F32)
    for j, piece in enumerate(pieces):
        out_ref[rows_at(high ^ j, rows), :] = piece[0:rows, :]
        tail = tail + piece[rows : rows + SMALL, :].astype(F32)
    out_ref[len(pieces) * rows : len(pieces) * rows + SMALL, :] = tail.astype(BF16)


def join_attention_kernel(rows, depth, place_ref, *refs):
    pieces, out_ref = refs[:-1], refs[-1]
    low = place_ref[4]
    tail = jnp.zeros((SMALL, 2 * D), F32)
    for k, piece in enumerate(pieces):
        for high in range(depth):
            out_ref[rows_at(high * 4 + (low ^ k), rows), :] = piece[
                high * rows : (high + 1) * rows, :
            ]
        tail = tail + piece[depth * rows : depth * rows + SMALL, :].astype(F32)
    out_ref[D : D + SMALL, :] = tail.astype(BF16)


def join_gathered_kernel(rows, pieces_ref, out_ref, *sends):
    tail = jnp.zeros((SMALL, 2 * D), F32)
    for at in range(D // rows):
        piece = pieces_ref[at, 0:rows, :]
        out_ref[at * rows : (at + 1) * rows, :] = piece
        for half, ref in enumerate(sends):
            ref[at * rows : (at + 1) * rows, :] = piece[:, half * D : (half + 1) * D]
        tail = tail + pieces_ref[at, rows : rows + SMALL, :].astype(F32)
    out_ref[D : D + SMALL, :] = tail.astype(BF16)
    for half, ref in enumerate(sends):
        ref[D : D + SMALL, :] = tail[:, half * D : (half + 1) * D].astype(BF16)


def join_plane_kernel(rows, place_ref, *refs):
    pieces, outs = refs[:PLANE], refs[PLANE:]
    count = 2 * PLANE * rows
    for out_ref in outs:
        for k, piece in enumerate(pieces):
            out_ref[rows_at(place_ref[1] ^ k, 2 * rows), :] = piece[...]
        if out_ref.shape[0] > count:
            out_ref[count : count + SMALL, :] = jnp.zeros((SMALL, FFH), BF16)


def join_levels_kernel(rows, place_ref, *refs):
    pieces, outs = refs[:-2], refs[-2:]
    for j, piece in enumerate(pieces):
        for role in range(PLANE):
            at = rows_at(spot_of(place_ref[2] ^ j, role), rows)
            for part in range(2):
                first = (2 * role + part) * rows
                for out_ref in outs:
                    out_ref[part, at, :] = piece[first : first + rows, :]


def split_roles_kernel(rows, depth, keep_ref, got_ref, out_ref):
    for role in range(PLANE):
        for level in range(depth):
            first = spot_of(level, role) * rows
            at = slice(first, first + rows)
            out_ref[role, level * rows : (level + 1) * rows, :] = (
                keep_ref[at, :].astype(F32) + got_ref[at, :].astype(F32)
            ).astype(BF16)


def split_expert_kernel(rows, place_ref, keep_ref, got_ref, own_ref, far_ref, near_ref, next_ref):
    block = PLANE * rows
    low = slice(2 * D, 2 * D + SMALL)
    tail = keep_ref[low, :].astype(F32) + got_ref[low, :].astype(F32)
    for j, ref in ((3, far_ref), (1, near_ref), (2, next_ref), (0, own_ref)):
        for part in range(2):
            for role in range(PLANE):
                at = rows_at(spot_of(place_ref[2] ^ j, role), rows, part * D)
                first = part * block + role * rows
                ref[first : first + rows, :] = (
                    keep_ref[at, :].astype(F32) + got_ref[at, :].astype(F32)
                ).astype(ref.dtype)
        if j != 1:
            ref[2 * block : 2 * block + SMALL, :] = tail.astype(ref.dtype)


def add_kernel(own_ref, got_ref, out_ref):
    out_ref[...] = (own_ref[...].astype(F32) + got_ref[...].astype(F32)).astype(BF16)


def spread_expert_kernel(
    rows, place_ref, own_ref, far_ref, near_ref, next_ref, last_ref, *outs
):
    block = PLANE * rows
    base = 2 * block
    each = 2 * rows + SMALL
    tail = own_ref[base : base + SMALL, :].astype(F32) + far_ref[base : base + SMALL, :].astype(F32)
    tail = tail + next_ref[base : base + SMALL, :].astype(F32)
    for k, out in enumerate(outs):
        for part in range(2):
            at = rows_at(place_ref[1] ^ k, rows, part * block)
            first = part * rows
            out[first : first + rows, :] = (
                own_ref[at, :].astype(F32)
                + near_ref[at, :].astype(F32)
                + next_ref[at, :].astype(F32)
            ).astype(BF16)
            out[each + first : each + first + rows, :] = last_ref[at, :]
        out[2 * rows : each, :] = tail.astype(BF16)
        out[each + 2 * rows : 2 * each, :] = last_ref[base : base + SMALL, :]


def split_attention_kernel(rows, depth, place_ref, keep_ref, *refs):
    gots, outs = refs[: len(PARTS)], refs[len(PARTS) :]
    low = place_ref[4]
    for got_ref, cut in zip(gots, PARTS):
        tail = keep_ref[D : D + SMALL, cut].astype(F32) + got_ref[D : D + SMALL, :].astype(F32)
        for k, out in enumerate(outs):
            for high in range(depth):
                at = rows_at(high * 4 + (low ^ k), rows)
                out[high * rows : (high + 1) * rows, cut] = (
                    keep_ref[at, cut].astype(F32) + got_ref[at, :].astype(F32)
                ).astype(out.dtype)
            out[depth * rows : depth * rows + SMALL, cut] = tail.astype(out.dtype)


def spread_attention_kernel(rows, depth, place_ref, *refs):
    pieces, last_ref, (keep_ref, send_ref) = refs[:PLANE], refs[PLANE], refs[PLANE + 1 :]
    high = place_ref[3]
    base = depth * rows

    def summed(at):
        total = pieces[0][at, :]
        for piece in pieces[1:]:
            total = total + piece[at, :].astype(F32)
        return total

    tail = summed(slice(base, base + SMALL))
    for ref, flip in ((keep_ref, 0), (send_ref, 1)):
        for at in range(2):
            index = rows_at(high ^ (flip + 2 * at), rows)
            first = 2 * at * rows
            ref[first : first + rows, :] = summed(index).astype(ref.dtype)
            ref[first + rows : first + 2 * rows, :] = last_ref[index, :].astype(ref.dtype)
        ref[4 * rows : 4 * rows + SMALL, :] = tail.astype(ref.dtype)


def halve_attention_kernel(rows, own_ref, got_ref, keep_ref, send_ref):
    total = own_ref[...] + got_ref[...].astype(F32)
    tail = total[4 * rows : 4 * rows + SMALL]
    for ref, at in ((keep_ref, 0), (send_ref, 2 * rows)):
        ref[0 : 2 * rows, :] = total[at : at + 2 * rows].astype(ref.dtype)
        ref[2 * rows : 2 * rows + SMALL, :] = tail.astype(ref.dtype)


def exact(a, b):
    return lax.dot_general(
        a, b, (((1,), (1,)), ((), ())), precision=lax.Precision.HIGHEST, preferred_element_type=F32
    )


def own_attention(rows, me, first, tail, last, outs):
    gain1, bias1, qkv, qv, output, shift, gain2, bias2, router = outs
    for layer, body in enumerate((first, last)):
        for part in range(3):
            qkv[layer, part] = body[:, part * HALF : (part + 1) * HALF]
        output[layer] = body[:, 3 * HALF : 4 * HALF]
        small = tail[8 * layer : 8 * layer + 8]
        left = exact(small[:, 0:D], one_hot(me, rows, D, F32))
        right = exact(small[:, D : 2 * D], one_hot(me, rows, D, F32))
        for ref, values, row in (
            (gain1, left, 0),
            (bias1, right, 0),
            (shift, left, 1),
            (gain2, right, 1),
            (bias2, left, 2),
        ):
            ref[layer : layer + 1, :] = values[row : row + 1]
        for e in range(EXPERTS):
            values = (left, right)[e % 2]
            router[layer, e : e + 1, :] = values[3 + e // 2 : 4 + e // 2]
        width = qv.shape[2]
        for part in range(2):
            values = exact(
                small[:, D + part * HALF : D + (part + 1) * HALF], one_hot(me, width, HALF, F32)
            )
            qv[layer, part : part + 1, :] = values[2:3]


def own_attention_kernel(rows, place_ref, own_ref, got_ref, *outs):
    total = own_ref[...] + got_ref[...].astype(F32)
    tail = total[2 * rows : 2 * rows + SMALL]
    own_attention(rows, place_ref[0], total[0:rows], tail, total[rows : 2 * rows], outs)


def own_experts_kernel(rows, place_ref, *refs):
    pieces = refs[:PLANE]
    inner_ref, in_bias_ref, outer_ref, out_bias_ref = refs[PLANE:]
    each = 2 * rows + SMALL
    me, role = place_ref[0], place_ref[1]
    in_place = one_hot(me, in_bias_ref.shape[2], FFH)
    out_place = one_hot(me, rows, D)
    for layer in range(2):
        for k in range(PLANE):
            piece = pieces[k].at[layer * each : (layer + 1) * each]
            expert = role ^ k
            inner_ref[layer, expert] = piece[0:rows, :].astype(F32)
            outer_ref[layer, expert] = piece[rows : 2 * rows, :].astype(F32)
            tail = piece[2 * rows : 2 * rows + SMALL, :]
            out_bias_ref[layer, pl.ds(expert, 1), :] = mm_t(tail[:, 0:D], out_place)[0:1]
            in_bias_ref[layer, pl.ds(expert, 1), :] = mm_t(tail, in_place)[1:2]


class Order:
    def __init__(self, place):
        self.last = ()
        self.place = place

    def run(self, kernel, out_shape, operands, name, fixed=(), place=True, through=()):
        count = len(out_shape)
        fars = [at for at in range(count) if not isinstance(out_shape[at], jax.ShapeDtypeStruct)]
        if not fars:
            out_shape = [*out_shape, shape((8, 128), F32)]

        def body(*refs):
            if fars:
                kernel(*fixed, *refs)
            else:
                kernel(*fixed, *refs[:-1])
                refs[-1][...] = jnp.zeros((8, 128), F32)

        if place:
            operands = (self.place, *operands)
        outs = list(call(body, out_shape, operands, name, self.last, through, int(place)))
        if fars:
            sized = [outs[at] for at in fars]
            token = far(min(sized, key=lambda out: out.size * out.dtype.itemsize))
        else:
            token = outs.pop(count)
        self.last = (token,)
        return outs

    def gate(self, through):
        def kernel(place_ref, out_ref):
            out_ref[...] = jnp.zeros_like(out_ref)

        return self.run(kernel, [shape((8, 128), F32)], (), "gate", through=through)[1:]

    def main(self, kernel, out_shape, operands, name, through=(), place=False):
        outs = self.run(kernel, out_shape, operands, name, (), place, through)
        count = len(out_shape)
        return outs[:count], outs[count:]


class Moves:
    def __init__(self, dp, order, me, role, level):
        self.dp, self.order = dp, order
        self.me, self.role, self.level = me, role, level
        self.depth, self.rows = dp // PLANE, D // dp

    def swap(self, x, mask):
        return lax.ppermute(x, "dp", [(i, i ^ mask) for i in range(self.dp)])

    def swap_core(self, x):
        return lax.ppermute(x, "tensor", [(0, 1), (1, 0)])

    def kept(self, x):
        return far(x)

    def to_role(self, x, k):
        return self.swap(x, spot_of(0, k))

    def to_level(self, x, j):
        return self.swap(x, spot_of(j, 0))

    def exchange(self, blocks):
        return [blocks[0]] + [self.to_role(blocks[k], k) for k in range(1, PLANE)]


class FastMoves(Moves):
    def one(self, *args, **kwargs):
        return self.order.run(*args, **kwargs)[0]

    def begin(self, weights):
        rows = self.rows
        outs = [shape((rows + SMALL, 2 * D), BF16), shape((rows + 2 * SMALL, 2 * D), BF16)]
        outs += [shape((2 * rows, FFH), BF16)] * (2 * PLANE)
        first, last, *sends = self.order.run(
            pack_kernel, outs, all_far(weights), "pack", (rows,)
        )
        exp0 = self.exchange(sends[:PLANE])
        att0 = [first] + [self.swap(first, 4 * j) for j in range(1, self.depth)]
        return att0, exp0, lax.all_gather(last, "dp"), sends[PLANE:]

    def groups(self, index):
        firsts = {}
        for level in range(self.depth):
            for role in range(PLANE):
                key = level if index == 0 else role
                firsts.setdefault(key, []).append(spot_of(level, role))
        return list(firsts.values())

    def plane0(self, pieces):
        out = [shape((2 * PLANE * self.rows, FFH), BF16)]
        own = self.one(join_plane_kernel, out, pieces, "join_plane", (self.rows,))
        return [own, self.to_level(own, 1), self.to_level(own, 2)]

    def stack0(self, pieces):
        out = [shape((self.depth * self.rows + SMALL, 2 * D), BF16)]
        message = self.one(stack_attention_kernel, out, pieces, "stack_attention", (self.rows,))
        return [message] + [self.swap(message, k) for k in range(1, 4)]

    def join0(self, pieces, exp0, exp1, given):
        out = [far_shape((D + SMALL, 2 * D), BF16)]
        fixed = (self.rows, self.depth)
        own, near, next_, *rest = self.order.run(
            join_attention_kernel,
            out,
            pieces,
            "join_attention",
            fixed,
            through=[*exp0[1:3], *exp1[1:], *given],
        )
        sends, given = rest[: PLANE - 1], rest[PLANE - 1 :]
        exp0 = [exp0[0], near, next_, self.to_level(next_, 1)]
        return (own, self.swap_core(own)), exp0, self.exchange([exp1[0], *sends]), given

    def plane1(self, pieces):
        count = 2 * PLANE * self.rows
        out = [shape((count + SMALL, FFH), BF16), shape((count, FFH), BF16)]
        return self.order.run(join_plane_kernel, out, pieces, "join_plane", (self.rows,))

    def forward(self, piece):
        return self.to_level(piece, 1)

    def join_last(self, gathered):
        out = [far_shape((D + SMALL, 2 * D), BF16)] + [shape((D + SMALL, D), BF16)] * 2
        own, left, right = self.order.run(
            join_gathered_kernel, out, (far(gathered),), "join_gathered", (self.rows,), False
        )
        return own, self.swap_core(left), self.swap_core(right)

    def join_levels(self, pieces, through=()):
        out = [far_shape((2, D, FFH), BF16), shape((2, D, FFH), BF16)]
        own, send, *through = self.order.run(
            join_levels_kernel, out, all_far(pieces), "join_levels", (self.rows,), through=through
        )
        return (own, self.swap_core(send)), through

    def last_attention_1(self, operands):
        (keep, send), _ = self.order.main(
            attention_grads_kernel,
            [shape((D, 2 * D), BF16)] * 2,
            operands,
            "attention_grads1",
        )
        return keep, self.swap_core(send)

    def last_expert(self, operands):
        out = [far_shape((2 * self.depth, 2 * PLANE * self.rows + SMALL, FFH), BF16)]
        sums = self.one(
            expert_grads_owned_kernel, out, operands, "expert_grads1", (self.depth,)
        )
        groups = [
            [2 * member + core for member in group for core in range(2)]
            for group in self.groups(1)
        ]
        return lax.psum_scatter(
            sums, ("dp", "tensor"), scatter_dimension=0, axis_index_groups=groups
        )

    def last_attention_2(self, keep, got):
        out = [far_shape((PLANE, self.depth * self.rows, 2 * D), BF16)]
        fixed = (self.rows, self.depth)
        sums = self.one(split_roles_kernel, out, (keep, got), "split_roles", fixed, False)
        return lax.psum_scatter(
            sums, "dp", scatter_dimension=0, axis_index_groups=self.groups(0)
        )

    def expert_sum_2(self, keep, got, through=()):
        count = 2 * PLANE * self.rows
        outs = [
            far_shape((count + SMALL, FFH), BF16),
            shape((count + SMALL, FFH), BF16),
            shape((count, FFH), BF16),
            far_shape((count + SMALL, FFH), BF16),
        ]
        own, third, near, next_, *through = self.order.run(
            split_expert_kernel, outs, (keep, got), "split_expert", (self.rows,), through=through
        )
        return [own, self.to_level(third, 1), self.to_level(near, 1), next_], through

    def expert_sum_3(self, state):
        own, third, near, next_ = state
        message = self.one(
            add_kernel,
            [shape(third.shape, BF16)],
            (far(next_), third),
            "add_expert",
            place=False,
        )
        return [own, third, near, self.to_level(message, 2)]

    def expert_sum_4(self, state, last, through=()):
        outs = [shape((2 * (2 * self.rows + SMALL), FFH), BF16)] * PLANE
        state = (*state, last.reshape(2 * PLANE * self.rows + SMALL, FFH))
        blocks = self.order.run(
            spread_expert_kernel,
            outs,
            all_far(state),
            "spread_expert",
            (self.rows,),
            through=through,
        )
        return self.exchange(blocks[:PLANE]), blocks[PLANE:]

    def attention_sum_1(self, keep, sends):
        return keep, [self.swap_core(send) for send in sends]

    def attention_sum_2(self, state, through):
        dims = (self.depth * self.rows + SMALL, 2 * D)
        outs = [far_shape(dims, F32)] + [shape(dims, BF16)] * 3
        fixed = (self.rows, self.depth)
        operands = (far(state[0]), *state[1])
        blocks = self.order.run(
            split_attention_kernel, outs, operands, "split_attention", fixed, through=through
        )
        return [blocks[0]] + [self.swap(blocks[k], k) for k in range(1, 4)], blocks[4:]

    def attention_sum_3(self, pieces, last, through=()):
        outs = [
            shape((4 * self.rows + SMALL, 2 * D), F32),
            shape((4 * self.rows + SMALL, 2 * D), BF16),
        ]
        fixed = (self.rows, self.depth)
        operands = all_far((*pieces, last.reshape(self.depth * self.rows, 2 * D)))
        keep, send, *through = self.order.run(
            spread_attention_kernel, outs, operands, "spread_attention", fixed, through=through
        )
        return (keep, self.swap(send, 4)), through

    def attention_sum_4(self, state):
        outs = [
            shape((2 * self.rows + SMALL, 2 * D), F32),
            shape((2 * self.rows + SMALL, 2 * D), BF16),
        ]
        keep, send = self.order.run(
            halve_attention_kernel, outs, state, "halve_attention", (self.rows,), False
        )
        return keep, self.swap(send, 8)

    def own_attention(self, pieces):
        rows, dp = self.rows, self.dp
        outs = [
            shape((2, rows), F32),
            shape((2, rows), F32),
            shape((2, 3, rows, HALF), F32),
            shape((2, 2, HALF // dp), F32),
            shape((2, rows, HALF), F32),
            shape((2, rows), F32),
            shape((2, rows), F32),
            shape((2, rows), F32),
            shape((2, EXPERTS, rows), F32),
        ]
        return self.order.run(
            own_attention_kernel, outs, pieces, "own_attention", (rows,)
        )

    def own_experts(self, pieces):
        rows = self.rows
        outs = [
            shape((2, EXPERTS, rows, FFH), F32),
            shape((2, EXPERTS, FFH // self.dp), F32),
            shape((2, EXPERTS, rows, FFH), F32),
            shape((2, EXPERTS, rows), F32),
        ]
        return self.order.run(own_experts_kernel, outs, pieces, "own_experts", (rows,))


class PlainMoves(Moves):
    def kept(self, x):
        return x

    def by_index(self, pieces, me):
        return jnp.take(jnp.stack(pieces), me ^ jnp.arange(len(pieces)), axis=0)

    def relative(self, array, me, axis):
        return jnp.take(array, me ^ jnp.arange(array.shape[axis]), axis=axis)

    def spots(self):
        return [spot_of(j, k) for j in range(self.depth) for k in range(PLANE)]

    def total(self, pieces):
        return sum(piece.astype(F32) for piece in pieces)

    def pack(self, layer, weights):
        (
            norm1_gain,
            norm1_bias,
            output_bias,
            norm2_gain,
            norm2_bias,
            router_weight,
            expert_out_bias,
            qv_bias,
            expert_in_bias,
            qkv_weight,
            output_weight,
            expert_in,
            expert_out,
        ) = [weight[layer] for weight in weights]
        vectors = (norm1_gain, norm1_bias, output_bias, norm2_gain, norm2_bias)

        def placed(values, width):
            extent = values.shape[-1]
            column = jnp.arange(extent)[:, None] + self.me * extent
            spot = (column == jnp.arange(width)[None, :]).astype(BF16)
            return jnp.dot(values, spot, preferred_element_type=F32).astype(BF16)

        wide = placed(jnp.stack(vectors), D)
        router = placed(router_weight, D)
        shifts = placed(qv_bias, HALF).reshape(1, D)
        outer = placed(expert_out_bias, D)
        small = jnp.concatenate([wide, shifts, router, outer], axis=0).reshape(7, 2 * D)
        inner = placed(expert_in_bias, FFH)
        body = jnp.concatenate([*qkv_weight, output_weight], axis=1)
        blank = jnp.zeros((SMALL - 11, 2 * D), BF16)
        shard = jnp.concatenate([body, small, inner, blank], axis=0)
        experts = jnp.stack([expert_in, expert_out], axis=1)
        return shard, list(self.relative(experts, self.role, 0))

    def begin(self, weights):
        shard0, sends0 = self.pack(0, weights)
        shard1, sends1 = self.pack(1, weights)
        return shard0, [jnp.stack(sends0)], shard1, [jnp.stack(sends1)]

    def plane0(self, pieces):
        return pieces * 3

    def plane1(self, pieces):
        return pieces * 2

    def stack0(self, shard):
        return shard

    def join0(self, shard, exp0, exp1, given):
        own, left, right = self.join_last(shard)
        return (own, jnp.concatenate([left, right], axis=1)), exp0, exp1, given

    def forward(self, piece):
        return piece

    def join_last(self, shard):
        gathered = lax.all_gather(shard, "dp")
        body = gathered[:, : self.rows].reshape(D, 2 * D)
        tail = jnp.sum(gathered[:, self.rows :].astype(F32), axis=0).astype(BF16)
        own = jnp.concatenate([body, tail], axis=0)
        other = self.swap_core(own)
        return own, other[:, :D], other[:, D:]

    def join_levels(self, pieces, through=()):
        body = self.by_index(self.exchange(list(pieces[0])), self.role)
        pieces = [body] + [self.to_level(body, j) for j in range(1, self.depth)]
        stacked = self.by_index(pieces, self.level).reshape(self.dp, 2, self.rows, FFH)
        order = sorted(range(self.dp), key=lambda at: self.spots()[at])
        own = stacked[jnp.array(order)].transpose(1, 0, 2, 3).reshape(2, D, FFH)
        return (own, self.swap_core(own)), through

    def expert_sum_2(self, keep, got, through=()):
        return [keep, got, got, got], through

    def expert_sum_3(self, state):
        return state

    def expert_sum_4(self, state, last, through=()):
        return (self.sum_expert(*state[:2]), self.sum_expert(*last)), through

    def sum_expert(self, keep, got):
        rows, depth = self.rows, self.depth
        whole = keep.astype(F32) + got.astype(F32)
        tail = whole[2 * D :]
        body = whole[: 2 * D].reshape(2, self.dp, rows, FFH)[:, jnp.array(self.spots())]
        body = self.relative(body.reshape(2, depth, PLANE * rows, FFH), self.level, 1)
        low, low_tail = body.astype(BF16), tail.astype(BF16)
        count = 2 * PLANE * rows
        pieces = []
        for j in range(1, depth):
            message = jnp.concatenate([low[:, j].reshape(count, FFH), low_tail], axis=0)
            pieces.append(self.to_level(message, j))
        body = body[:, 0].reshape(count, FFH) + self.total([piece[:count] for piece in pieces])
        tail = tail + self.total([piece[count:] for piece in pieces])
        body = self.relative(body.reshape(2, PLANE, rows, FFH), self.role, 1).astype(BF16)
        tail = tail.astype(BF16)
        count = 2 * rows
        blocks = [
            jnp.concatenate([body[:, k].reshape(count, FFH), tail], axis=0) for k in range(PLANE)
        ]
        return self.exchange(blocks)

    def attention_sum_1(self, keep, sends):
        return keep, jnp.concatenate(sends, axis=1)

    def attention_sum_2(self, state, through):
        return state, through

    def attention_sum_3(self, state, last, through=()):
        return (state, last), through

    def attention_sum_4(self, state):
        (keep, send), last = state
        whole = keep + self.swap_core(send).astype(F32)
        body = lax.psum_scatter(whole[:D], "dp", scatter_dimension=0, tiled=True)
        return jnp.concatenate([body, lax.psum(whole[D:], "dp")], axis=0), last

    def last_attention_1(self, operands):
        (keep, send), _ = self.order.main(
            attention_grads_kernel,
            [shape((D, 2 * D), F32), shape((D, 2 * D), BF16)],
            operands,
            "attention_grads1",
        )
        return keep, self.swap_core(send)

    def last_expert(self, operands):
        (keep, send), _ = self.order.main(
            expert_grads_pair_kernel, EXPERT_SUMS, operands, "expert_grads1"
        )
        return keep, self.swap_core(send)

    def last_attention_2(self, keep, got):
        whole = keep + got.astype(F32)
        return lax.psum_scatter(whole, "dp", scatter_dimension=0, tiled=True)

    def own_attention(self, state):
        total, last = state
        rows = self.rows
        body = jnp.stack([total[:rows], last])
        tail = total[rows:].reshape(2, 16, D)

        def owned(values, width):
            return lax.dynamic_slice_in_dim(
                values, self.me * width, width, axis=values.ndim - 1
            )

        wide = owned(tail, rows)
        qkv = body[:, :, : 3 * HALF].reshape(2, rows, 3, HALF).transpose(0, 2, 1, 3)
        qv = owned(tail[:, 5].reshape(2, 2, HALF), HALF // self.dp)
        vectors = [wide[:, row] for row in range(5)]
        return (
            *vectors[:2],
            qkv,
            qv,
            body[:, :, 3 * HALF :],
            *vectors[2:],
            wide[:, 6:10],
        )

    def own_experts(self, state):
        first, last = state
        rows = self.rows
        owned = jnp.stack([self.by_index(first, self.role), self.by_index(last, self.role)])
        owned = owned.astype(F32)
        tail = owned[:, :, 2 * rows :]
        width = FFH // self.dp
        in_bias = lax.dynamic_slice_in_dim(tail[:, :, 1], self.me * width, width, axis=2)
        out_bias = lax.dynamic_slice_in_dim(tail[:, :, 0], self.me * rows, rows, axis=2)
        return owned[:, :, :rows], in_bias, owned[:, :, rows : 2 * rows], out_bias


def build(dp):
    def local(
        tokens,
        routes,
        norm1_gain,
        norm1_bias,
        qkv_weight,
        qv_bias,
        output_weight,
        output_bias,
        norm2_gain,
        norm2_bias,
        router_weight,
        expert_in,
        expert_in_bias,
        expert_out,
        expert_out_bias,
        grad_out,
    ):
        me = lax.axis_index("dp").astype(jnp.int32)
        core = lax.axis_index("tensor")
        role, level = me % PLANE, me // PLANE
        order = Order(
            jnp.stack([me, role, level, me // 4, me % 4, core.astype(jnp.int32)])
        )
        moves = (FastMoves if dp == 16 else PlainMoves)(dp, order, me, role, level)
        weights = (
            norm1_gain,
            norm1_bias,
            output_bias,
            norm2_gain,
            norm2_bias,
            router_weight.transpose(0, 2, 1),
            expert_out_bias,
            qv_bias,
            expert_in_bias,
            qkv_weight.transpose(0, 2, 1, 3),
            output_weight.transpose(0, 2, 1),
            expert_in,
            expert_out.transpose(0, 1, 3, 2),
        )

        att0, exp0, gathered1, exp1 = moves.begin(weights)

        choice = lax.dynamic_index_in_dim(routes, core, axis=1, keepdims=False)
        hot = (choice[..., None] == jnp.arange(EXPERTS)).astype(BF16)
        any_hot = hot[:, :, 0] + hot[:, :, 1]
        below = jnp.tril(jnp.ones((SEQ, SEQ), BF16), -1)
        slot = jnp.einsum("ts,lse->lte", below, any_hot, preferred_element_type=F32)
        slot = jnp.sum(hot.astype(F32) * slot[:, :, None], axis=-1).astype(jnp.int32)
        target = (choice ^ role) * CAP + slot
        columns = jnp.pad(
            jnp.concatenate([target, choice], axis=-1),
            ((0, 0), (0, SP - SEQ), (0, 0)),
            constant_values=-1,
        )
        target_rows = columns[:, :, 0:2].transpose(0, 2, 1)

        def image(values):
            values = lax.dynamic_index_in_dim(values, core, axis=0, keepdims=False)
            return jnp.pad(values, ((0, SP - SEQ), (0, 0)))

        rows, grad = image(tokens), image(grad_out)

        exp0 = moves.plane0(exp0)
        att0 = moves.stack0(att0)
        given = [rows, grad, columns[0], columns[1], target_rows[0], target_rows[1]]
        attention0, exp0, exp1, given = moves.join0(att0, exp0, exp1, given)
        rows, grad, columns, target_rows = given[0], given[1], given[2:4], given[4:6]

        kept0, _ = order.main(
            first_forward_kernel,
            forward_outs(False),
            (rows, far(attention0[0]), attention0[1], columns[0], target_rows[0]),
            "attention_first",
        )
        middle0, normed0, normed2_0, qkv0, mixed0, log0, probs0, small0 = kept0[:8]
        blocks0 = moves.exchange(kept0[8:])
        expert0, exp1[1:] = moves.join_levels(exp0, exp1[1:])
        exp1, early1 = moves.plane1(exp1)
        next1 = moves.to_level(early1, 2)
        (hidden0, slope0, *results), (exp1,) = order.main(
            expert_forward_kernel,
            expert_outs(False),
            all_far((*blocks0, *expert0)) + [small0],
            "expert_forward",
            [exp1],
            place=True,
        )
        slots0 = moves.exchange(results)
        near1 = moves.to_level(exp1, 1)
        next1, gathered1, *slots0[1:] = order.gate([next1, moves.kept(gathered1), *slots0[1:]])
        exp1 = [exp1, near1, next1, moves.forward(next1)]
        attention1 = moves.join_last(gathered1)

        (rows1, *kept1), _ = order.main(
            last_forward_kernel,
            [far_shape((SP, D), F32)] + forward_outs(True),
            (
                *all_far((middle0, probs0)),
                columns[0],
                *all_far(slots0),
                grad,
                *all_far(attention1),
                columns[1],
                target_rows[1],
            ),
            "attention_last",
        )
        middle1, normed1, normed2_1, qkv1, mixed1, log1, probs1, small1 = kept1[:8]
        blocks1 = moves.exchange(kept1[8:])
        expert1, _ = moves.join_levels(exp1)
        (hidden1, grad_pre1, *results), _ = order.main(
            expert_both_kernel,
            expert_outs(True),
            (*all_far(blocks1), *expert1, small1),
            "expert_both",
            place=True,
        )
        pairs1 = moves.exchange(results)
        sums1 = moves.last_expert((*all_far(blocks1), hidden1, grad_pre1))
        back1, _ = order.main(
            backward_last_kernel,
            backward_outs(True),
            (
                grad,
                *pairs1,
                *all_far((rows1, middle1, normed2_1, qkv1, mixed1, log1, probs1)),
                columns[1],
                *all_far(attention1),
                far(probs0),
                columns[0],
                target_rows[0],
            ),
            "attention_back_last",
        )
        grad_rows1, grad_qkv1, grad_att1, keep1, send1, output = back1[:6]
        grads0 = moves.exchange(back1[6:])
        output_got = moves.swap_core(output)
        att_owned1 = moves.last_attention_1((far(normed1), grad_qkv1, grad_att1, far(mixed1)))

        att_owned1 = moves.last_attention_2(*att_owned1)
        (grad_pre0, *results), (output_got,) = order.main(
            expert_back_kernel,
            EXPERT_BACK,
            all_far((*grads0, slope0, *expert0)),
            "expert_back",
            [output_got],
        )
        slot_grads0 = moves.exchange(results)
        sums0, _ = order.main(
            expert_grads_single_kernel,
            EXPERT_SUMS,
            all_far((*blocks0, *grads0, hidden0)) + [grad_pre0],
            "expert_grads0",
        )
        sums0, slot_grads0[1:] = moves.expert_sum_2(
            sums0[0], moves.swap_core(sums0[1]), slot_grads0[1:]
        )
        (grad_rows0, grad_qkv0, grad_att0, keep0, send0), _ = order.main(
            backward_first_kernel,
            backward_outs(False),
            (
                far(grad_rows1),
                *all_far(slots0),
                *slot_grads0,
                rows,
                *all_far((middle0, normed2_0, qkv0, mixed0, log0, probs0)),
                columns[0],
                *all_far(attention0),
            ),
            "attention_back_first",
        )
        att_sums0, _ = order.main(
            attention_grads_small_kernel,
            ATTENTION_SUMS,
            (
                far(normed0),
                grad_qkv0,
                grad_att0,
                far(mixed0),
                keep0,
                send0,
                far(keep1),
                far(send1),
            ),
            "attention_grads0",
        )

        att_sums0 = moves.attention_sum_1(att_sums0[0], att_sums0[1:])
        sums0 = moves.expert_sum_3(sums0)
        att_sums0, (sums1,) = moves.attention_sum_2(att_sums0, [moves.kept(sums1)])
        att_sums0, _ = moves.attention_sum_3(att_sums0, att_owned1)
        sums0, (grad_rows0,) = moves.expert_sum_4(sums0, sums1, [grad_rows0])
        att_sums0 = moves.attention_sum_4(att_sums0)
        rows_got = moves.swap_core(grad_rows0)
        gain1, bias1, qkv, qv, out, shift, gain2, bias2, router = moves.own_attention(att_sums0)
        inner, in_bias, outer, out_bias = moves.own_experts(sums0)

        def both(values, others):
            first = jnp.where(core == 0, values, others)[:SEQ]
            second = jnp.where(core == 0, others, values)[:SEQ]
            return jnp.stack([first, second], axis=1).transpose(1, 0, 2)

        return (
            both(output, output_got),
            both(grad_rows0, rows_got),
            gain1,
            bias1,
            qkv.transpose(0, 2, 1, 3),
            qv,
            out.transpose(0, 2, 1),
            shift,
            gain2,
            bias2,
            router.transpose(0, 2, 1),
            inner,
            in_bias,
            outer.transpose(0, 1, 3, 2),
            out_bias,
        )

    return local


def solution(mesh):
    weights = (
        P(None, "dp"),
        P(None, "dp"),
        P(None, "dp", None, "tensor"),
        P(None, None, ("tensor", "dp")),
        P(None, "tensor", "dp"),
        P(None, "dp"),
        P(None, "dp"),
        P(None, "dp"),
        P(None, "dp", None),
        P(None, None, "dp", "tensor"),
        P(None, None, ("tensor", "dp")),
        P(None, None, "tensor", "dp"),
        P(None, None, "dp"),
    )
    images = P("dp", None, None)
    return jax.shard_map(
        build(mesh.shape["dp"]),
        mesh=mesh,
        in_specs=(images, P(None, "dp", None, None)) + weights + (images,),
        out_specs=(images, images) + weights,
        check_vma=False,
    )
```

```python
import jax
import jax.numpy as jnp
from jax import lax
from jax.experimental import pallas as pl
from jax.experimental.pallas import tpu as pltpu
from jax.sharding import PartitionSpec as P

D = 512
HD = 64
HALF = 256
FFH = 1024
SEQ = 197
SP = 208
EXPERTS = 4
CAP = 128
SLOTS = EXPERTS * CAP
PLANE = 4
SMALL = 16
EPSILON = 1e-06
SCALE = HD ** (-0.5)
MIB = 2**20
VMEM_MIB = 32
F32 = jnp.float32
BF16 = jnp.bfloat16


def call(kernel, out_shape, operands, name, after, through, scalars):
    inputs, outputs = len(operands), len(out_shape)

    def body(*refs):
        first = inputs + len(after) + len(through)
        kernel(*refs[:inputs], *refs[first : first + outputs])

    anywhere = pl.BlockSpec(memory_space=pl.ANY)
    whole = pl.BlockSpec(memory_space=pltpu.VMEM)
    return pl.pallas_call(
        body,
        out_shape=list(out_shape) + [shape(array.shape, array.dtype) for array in through],
        in_specs=[pl.BlockSpec(memory_space=pltpu.SMEM)] * scalars
        + [whole] * (inputs - scalars)
        + [anywhere] * (len(after) + len(through)),
        out_specs=[whole] * outputs + [anywhere] * len(through),
        input_output_aliases={
            inputs + len(after) + i: outputs + i for i in range(len(through))
        },
        compiler_params=pltpu.CompilerParams(vmem_limit_bytes=VMEM_MIB * MIB),
        cost_estimate=pl.CostEstimate(flops=1, bytes_accessed=1, transcendentals=0),
        name=name,
    )(*operands, *after, *through)


def shape(dims, dtype):
    return jax.ShapeDtypeStruct(dims, dtype)


def far_shape(dims, dtype):
    return pltpu.HBM(dims, dtype)


def far(array):
    return pltpu.with_memory_space_constraint(array, pltpu.HBM)


def all_far(arrays):
    return [far(array) for array in arrays]


def mm(a, b):
    return lax.dot_general(a, b, (((1,), (0,)), ((), ())), preferred_element_type=F32)


def mm_t(a, b):
    return lax.dot_general(a, b, (((1,), (1,)), ((), ())), preferred_element_type=F32)


def mm_tn(a, b):
    return lax.dot_general(a, b, (((0,), (0,)), ((), ())), preferred_element_type=F32)


def normalise(rows):
    center = rows - jnp.mean(rows, axis=-1, keepdims=True)
    inverse = lax.rsqrt(jnp.mean(center * center, axis=-1, keepdims=True) + EPSILON)
    return center * inverse, inverse


def norm_back(grad, hat, inverse, gain):
    scaled = grad * gain
    return inverse * (
        scaled
        - jnp.mean(scaled, axis=-1, keepdims=True)
        - hat * jnp.mean(scaled * hat, axis=-1, keepdims=True)
    )


def small_row(small, row, part):
    return small[row : row + 1, part * D : (part + 1) * D]


def router_rows(small):
    return [small_row(small, 3 + e // 2, e % 2) for e in range(EXPERTS)]


def select_columns(targets, j):
    lanes = lax.broadcasted_iota(jnp.int32, (SP, SLOTS), 1)
    return jnp.where(lanes == targets[:, j : j + 1], 1.0, 0.0).astype(BF16)


def select_rows(target_rows, j):
    subs = lax.broadcasted_iota(jnp.int32, (SLOTS, SP), 0)
    return jnp.where(subs == target_rows[j : j + 1, :], 1.0, 0.0).astype(BF16)


def chosen_of(targets, j):
    lanes = lax.broadcasted_iota(jnp.int32, (SP, EXPERTS), 1)
    return jnp.where(lanes == targets[:, 2 + j : 3 + j], 1.0, 0.0)


def gates_of(probs, targets):
    return [jnp.sum(chosen_of(targets, j) * probs, axis=-1, keepdims=True) for j in range(2)]


def attention_forward(rows, halves, targets, target_rows, outs, grad_rows):
    middle_ref, normed_ref, normed2_ref, qkv_ref, mixed_ref, log_ref, probs_ref = outs[:7]
    small_ref, send_refs = outs[7], outs[8:]
    small_ref[0] = halves[0][D : D + SMALL, :]
    small_ref[1] = halves[1][D : D + SMALL, :]
    small = halves[0][D : D + SMALL, :].astype(F32)
    hat, _ = normalise(rows)
    normed = (hat * small_row(small, 0, 0) + small_row(small, 0, 1)).astype(BF16)
    normed_ref[...] = normed
    attended = jnp.zeros((SP, D), F32)
    key_ok = lax.broadcasted_iota(jnp.int32, (SP, SP), 1) < SEQ
    logs = []
    for half in range(2):
        qkv = mm(normed, halves[half][0:D, 0 : 3 * HALF])
        shift = halves[half][D : D + SMALL, :][2:3, D : 2 * D].astype(F32)
        query = (qkv[:, 0:HALF] + shift[:, 0:HALF]).astype(BF16)
        key = qkv[:, HALF : 2 * HALF].astype(BF16)
        value = (qkv[:, 2 * HALF : 3 * HALF] + shift[:, HALF : 2 * HALF]).astype(BF16)
        qkv_ref[half] = jnp.concatenate([query, key, value], axis=1)
        mixed = []
        for head in range(HALF // HD):
            cut = slice(head * HD, (head + 1) * HD)
            scores = jnp.where(key_ok, mm_t(query[:, cut], key[:, cut]) * SCALE, -1e30)
            top = jnp.max(scores, axis=-1, keepdims=True)
            weight = jnp.exp(scores - top)
            total = jnp.sum(weight, axis=-1, keepdims=True)
            logs.append(top + jnp.log(total))
            low = (weight * (1.0 / total)).astype(BF16)
            mixed.append(mm(low, value[:, cut]).astype(BF16))
        mixed = jnp.concatenate(mixed, axis=1)
        mixed_ref[half] = mixed
        attended = attended + mm_t(mixed, halves[half][0:D, 3 * HALF : 4 * HALF])
    log_ref[...] = jnp.concatenate(logs, axis=1)
    middle = rows + attended + small_row(small, 1, 0)
    middle_ref[...] = middle
    hat2, _ = normalise(middle)
    normed2 = (hat2 * small_row(small, 1, 1) + small_row(small, 2, 0)).astype(BF16)
    normed2_ref[...] = normed2
    router = jnp.concatenate(router_rows(small) + [jnp.zeros((4, D), F32)], axis=0).astype(BF16)
    logits = mm_t(normed2, router)[:, 0:EXPERTS]
    weight = jnp.exp(logits - jnp.max(logits, axis=-1, keepdims=True))
    probs = weight / jnp.sum(weight, axis=-1, keepdims=True)
    probs_ref[...] = probs
    picks = [select_rows(target_rows, j) for j in range(2)]
    sent = mm(picks[0] + picks[1], normed2).astype(BF16)
    if grad_rows is None:
        for k in range(PLANE):
            send_refs[k][...] = sent[k * CAP : (k + 1) * CAP]
    else:
        gates = gates_of(probs, targets)
        grads = (
            mm(picks[0], (gates[0] * grad_rows).astype(BF16))
            + mm(picks[1], (gates[1] * grad_rows).astype(BF16))
        ).astype(BF16)
        for k in range(PLANE):
            send_refs[k][0] = sent[k * CAP : (k + 1) * CAP]
            send_refs[k][1] = grads[k * CAP : (k + 1) * CAP]


def first_forward_kernel(rows_ref, own_ref, other_ref, targets_ref, target_rows_ref, *outs):
    attention_forward(
        rows_ref[...].astype(F32),
        (own_ref, other_ref),
        targets_ref[...],
        target_rows_ref[...],
        outs,
        None,
    )


def combine(middle, probs, targets, slot_rows):
    gates = gates_of(probs, targets)
    picked = [mm(select_columns(targets, j), slot_rows) for j in range(2)]
    return middle + gates[0] * picked[0] + gates[1] * picked[1], picked


def last_forward_kernel(
    middle_ref,
    probs_ref,
    prior_targets_ref,
    f0,
    f1,
    f2,
    f3,
    grad_ref,
    own_ref,
    left_ref,
    right_ref,
    targets_ref,
    target_rows_ref,
    rows_ref,
    *outs,
):
    slot_rows = jnp.concatenate([f0[...], f1[...], f2[...], f3[...]], axis=0)
    rows, _ = combine(middle_ref[...], probs_ref[...], prior_targets_ref[...], slot_rows)
    rows_ref[...] = rows
    attention_forward(
        rows,
        (own_ref, jnp.concatenate([left_ref[...], right_ref[...]], axis=1)),
        targets_ref[...],
        target_rows_ref[...],
        outs,
        grad_ref[...].astype(F32),
    )


def forward_outs(pair):
    block = (2, CAP, D) if pair else (CAP, D)
    return [
        far_shape((SP, D), F32),
        far_shape((SP, D), BF16),
        far_shape((SP, D), BF16),
        far_shape((2, SP, 3 * HALF), BF16),
        far_shape((2, SP, HALF), BF16),
        far_shape((SP, 8), F32),
        far_shape((SP, EXPERTS), F32),
        shape((2, SMALL, 2 * D), BF16),
    ] + [shape(block, BF16)] * PLANE


def backward_kernel(final, *refs):
    grad_ref, f0, f1, f2, f3 = refs[:5]
    refs = refs[5:]
    if not final:
        d0, d1, d2, d3 = refs[:4]
        refs = refs[4:]
    (
        rows_ref,
        middle_ref,
        normed2_ref,
        qkv_ref,
        mixed_ref,
        log_ref,
        probs_ref,
        targets_ref,
        own_ref,
        other,
    ) = refs[:10]
    rest = refs[10:]
    if final:
        other = jnp.concatenate([other[...], rest[0][...]], axis=1)
        rest = rest[1:]
        prior_probs_ref, prior_targets_ref, prior_target_rows_ref = rest[:3]
        rest = rest[3:]
    grad_rows_ref, grad_qkv_ref, grad_att_ref, small_keep_ref, small_send_ref = rest[:5]
    rest = rest[5:]
    halves = (own_ref, other)
    small = own_ref[D : D + SMALL, :].astype(F32)
    grad = grad_ref[...].astype(F32)
    targets = targets_ref[...]
    probs = probs_ref[...]
    middle = middle_ref[...]
    if final:
        slot_rows = jnp.concatenate([f0[0], f1[0], f2[0], f3[0]], axis=0)
        slot_grads = jnp.concatenate([f0[1], f1[1], f2[1], f3[1]], axis=0)
    else:
        slot_rows = jnp.concatenate([f0[...], f1[...], f2[...], f3[...]], axis=0)
        slot_grads = jnp.concatenate([d0[...], d1[...], d2[...], d3[...]], axis=0)
    picks = [select_columns(targets, j) for j in range(2)]
    picked = [mm(picks[j], slot_rows) for j in range(2)]
    if final:
        gates = gates_of(probs, targets)
        rest[0][...] = middle + gates[0] * picked[0] + gates[1] * picked[1]
    grad_probs = jnp.zeros((SP, EXPERTS), F32)
    for j in range(2):
        grad_probs = grad_probs + chosen_of(targets, j) * jnp.sum(
            grad * picked[j], axis=-1, keepdims=True
        )
    grad_logits = probs * (grad_probs - jnp.sum(probs * grad_probs, axis=-1, keepdims=True))
    grad_logits = grad_logits.astype(BF16).astype(F32)
    grad_normed2 = mm(picks[0] + picks[1], slot_grads)
    normed2 = normed2_ref[...].astype(F32)
    routers = router_rows(small)
    grad_router = []
    for e in range(EXPERTS):
        column = grad_logits[:, e : e + 1]
        grad_normed2 = grad_normed2 + column * routers[e]
        grad_router.append(jnp.sum(column * normed2, axis=0, keepdims=True))
    hat2, inverse2 = normalise(middle)
    grad_gain2 = jnp.sum(grad_normed2 * hat2, axis=0, keepdims=True)
    grad_bias2 = jnp.sum(grad_normed2, axis=0, keepdims=True)
    grad_middle = grad + norm_back(grad_normed2, hat2, inverse2, small_row(small, 1, 1))
    grad_att = grad_middle.astype(BF16)
    grad_att_ref[...] = grad_att
    grad_shift = jnp.sum(grad_att.astype(F32), axis=0, keepdims=True)
    key_ok = lax.broadcasted_iota(jnp.int32, (SP, SP), 1) < SEQ
    grad_normed = jnp.zeros((SP, D), F32)
    qv_rows = []
    for half in range(2):
        grad_mixed = mm(grad_att, halves[half][0:D, 3 * HALF : 4 * HALF]).astype(BF16)
        query = qkv_ref[half, :, 0:HALF]
        key = qkv_ref[half, :, HALF : 2 * HALF]
        value = qkv_ref[half, :, 2 * HALF : 3 * HALF]
        grad_q, grad_k, grad_v = [], [], []
        for head in range(HALF // HD):
            cut = slice(head * HD, (head + 1) * HD)
            at = half * (HALF // HD) + head
            scores = mm_t(query[:, cut], key[:, cut]) * SCALE - log_ref[:, at : at + 1]
            weight = jnp.exp(jnp.where(key_ok, scores, -1e30))
            grad_v.append(mm_tn(weight.astype(BF16), grad_mixed[:, cut]).astype(BF16))
            grad_weight = mm_t(grad_mixed[:, cut], value[:, cut])
            mean = jnp.sum(weight * grad_weight, axis=-1, keepdims=True)
            grad_scores = (weight * (grad_weight - mean)).astype(BF16)
            grad_q.append((mm(grad_scores, key[:, cut]) * SCALE).astype(BF16))
            grad_k.append((mm_tn(grad_scores, query[:, cut]) * SCALE).astype(BF16))
        grad_qkv = jnp.concatenate(grad_q + grad_k + grad_v, axis=1)
        grad_qkv_ref[half] = grad_qkv
        grad_normed = grad_normed + mm_t(grad_qkv, halves[half][0:D, 0 : 3 * HALF])
        sums = jnp.sum(grad_qkv.astype(F32), axis=0, keepdims=True)
        qv_rows.append(jnp.concatenate([sums[:, 0:HALF], sums[:, 2 * HALF : 3 * HALF]], axis=1))
    hat, inverse = normalise(rows_ref[...].astype(F32))
    grad_gain = jnp.sum(grad_normed * hat, axis=0, keepdims=True)
    grad_bias = jnp.sum(grad_normed, axis=0, keepdims=True)
    grad_rows = grad_middle + norm_back(grad_normed, hat, inverse, small_row(small, 0, 0))
    grad_rows_ref[...] = grad_rows
    for half, ref in enumerate((small_keep_ref, small_send_ref)):
        left = [grad_gain, grad_shift, grad_bias2, grad_router[0], grad_router[2]]
        right = [grad_bias, grad_gain2, qv_rows[half], grad_router[1], grad_router[3]]
        ref[...] = jnp.concatenate(
            [
                jnp.concatenate(left + [jnp.zeros((SMALL - 5, D), F32)], axis=0),
                jnp.concatenate(right + [jnp.zeros((SMALL - 5, D), F32)], axis=0),
            ],
            axis=1,
        )
    if final:
        prior_gates = gates_of(prior_probs_ref[...], prior_targets_ref[...])
        prior_rows = prior_target_rows_ref[...]
        sent = (
            mm(select_rows(prior_rows, 0), (prior_gates[0] * grad_rows).astype(BF16))
            + mm(select_rows(prior_rows, 1), (prior_gates[1] * grad_rows).astype(BF16))
        ).astype(BF16)
        for k in range(PLANE):
            rest[1 + k][...] = sent[k * CAP : (k + 1) * CAP]


def backward_last_kernel(*refs):
    backward_kernel(True, *refs)


def backward_first_kernel(*refs):
    backward_kernel(False, *refs)


def backward_outs(final):
    keep = far_shape if final else shape
    outs = [
        keep((SP, D), F32),
        shape((2, SP, 3 * HALF), BF16),
        shape((SP, D), BF16),
        keep((SMALL, 2 * D), F32),
        keep((SMALL, 2 * D), F32),
    ]
    if final:
        outs += [shape((SP, D), F32)] + [shape((CAP, D), BF16)] * PLANE
    return outs


def attention_grads_kernel(normed_ref, grad_qkv_ref, grad_att_ref, mixed_ref, *outs):
    normed_t = normed_ref[...].T
    grad_att_t = grad_att_ref[...].T
    for half, ref in enumerate(outs):
        ref[0:D, 0 : 3 * HALF] = mm(normed_t, grad_qkv_ref[half]).astype(ref.dtype)
        ref[0:D, 3 * HALF : 4 * HALF] = mm(grad_att_t, mixed_ref[half]).astype(ref.dtype)


PARTS = (slice(0, 384), slice(384, 768), slice(768, 1024))


def attention_grads_small_kernel(*refs):
    normed_t, grad_att_t = refs[0][...].T, refs[2][...].T
    grad_qkv_ref, mixed_ref, small = refs[1], refs[3], refs[4:8]
    keep_ref, sends = refs[8], refs[9:]
    tails = [
        jnp.concatenate([small[half][0:8, :], small[2 + half][0:8, :]], axis=0)
        for half in range(2)
    ]
    keep_ref[0:D, 0 : 3 * HALF] = mm(normed_t, grad_qkv_ref[0]).astype(BF16)
    keep_ref[0:D, 3 * HALF : 4 * HALF] = mm(grad_att_t, mixed_ref[0]).astype(BF16)
    keep_ref[D : D + SMALL, :] = tails[0].astype(BF16)
    for ref, cut in zip(sends, PARTS):
        if cut.stop <= 3 * HALF:
            ref[0:D, :] = mm(normed_t, grad_qkv_ref[1, :, cut]).astype(BF16)
        else:
            ref[0:D, :] = mm(grad_att_t, mixed_ref[1]).astype(BF16)
        ref[D : D + SMALL, :] = tails[1][:, cut].astype(BF16)


ATTENTION_SUMS = [far_shape((D + SMALL, 2 * D), BF16)] + [
    shape((D + SMALL, cut.stop - cut.start), BF16) for cut in PARTS
]


CHUNK = 512


def gelu_parts(values):
    tail = 0.5 * (1.0 + lax.erf(values * 0.7071067811865476))
    density = jnp.exp(-0.5 * values * values) * 0.3989422804014327
    return values * tail, tail + values * density


def expert_bias(small, role):
    out_shift = jnp.zeros((1, D), F32)
    in_shift = jnp.zeros((1, FFH), F32)
    for e in range(EXPERTS):
        at = jnp.where(role == e, 1.0, 0.0)
        out_shift = out_shift + at * small_row(small, 5 + e // 2, e % 2)
        in_shift = in_shift + at * small[7 + e : 8 + e, :]
    return out_shift, in_shift


def expert_kernel(both, place_ref, *refs):
    blocks, (own_ref, other_ref, small_ref), outs = (
        refs[:PLANE],
        refs[PLANE : PLANE + 3],
        refs[PLANE + 3 :],
    )
    role = place_ref[1]
    hidden_ref, slope_ref = outs[:2]
    if both:
        inputs = jnp.concatenate([block[0] for block in blocks], axis=0)
        grads = jnp.concatenate([block[1] for block in blocks], axis=0)
        result = jnp.zeros((SLOTS, D), F32)
        result_grad = jnp.zeros((SLOTS, D), F32)
    else:
        inputs = jnp.concatenate([block[...] for block in blocks], axis=0)
        result = jnp.zeros((SLOTS, D), F32)
    out_shift = None
    for half, ref in enumerate((own_ref, other_ref)):
        shift, in_shift = expert_bias(small_ref[half].astype(F32), role)
        if half == 0:
            out_shift = shift
        for chunk in range(FFH // CHUNK):
            cut = slice(chunk * CHUNK, (chunk + 1) * CHUNK)
            columns = slice(half * FFH + chunk * CHUNK, half * FFH + (chunk + 1) * CHUNK)
            hidden, slope = gelu_parts(mm(inputs, ref[0, :, cut]) + in_shift[:, cut])
            hidden = hidden.astype(BF16)
            hidden_ref[:, columns] = hidden
            result = result + mm_t(hidden, ref[1, :, cut])
            if both:
                grad_pre = (mm(grads, ref[1, :, cut]) * slope).astype(BF16)
                slope_ref[:, columns] = grad_pre
                result_grad = result_grad + mm_t(grad_pre, ref[0, :, cut])
            else:
                slope_ref[:, columns] = slope.astype(BF16)
    result = (result + out_shift).astype(BF16)
    for k in range(PLANE):
        if both:
            outs[2 + k][0] = result[k * CAP : (k + 1) * CAP]
            outs[2 + k][1] = result_grad[k * CAP : (k + 1) * CAP].astype(BF16)
        else:
            outs[2 + k][...] = result[k * CAP : (k + 1) * CAP]


def expert_forward_kernel(*refs):
    expert_kernel(False, *refs)


def expert_both_kernel(*refs):
    expert_kernel(True, *refs)


def expert_outs(both):
    block = (2, CAP, D) if both else (CAP, D)
    kept = shape if both else far_shape
    return [kept((SLOTS, 2 * FFH), BF16)] * 2 + [shape(block, BF16)] * PLANE


def expert_back_kernel(*refs):
    blocks, (slope_ref, own_ref, other_ref, grad_pre_ref), outs = (
        refs[:PLANE],
        refs[PLANE : PLANE + 4],
        refs[PLANE + 4 :],
    )
    grads = jnp.concatenate([block[...] for block in blocks], axis=0)
    result = jnp.zeros((SLOTS, D), F32)
    for half, ref in enumerate((own_ref, other_ref)):
        for chunk in range(FFH // CHUNK):
            cut = slice(chunk * CHUNK, (chunk + 1) * CHUNK)
            columns = slice(half * FFH + chunk * CHUNK, half * FFH + (chunk + 1) * CHUNK)
            grad_pre = (mm(grads, ref[1, :, cut]) * slope_ref[:, columns].astype(F32)).astype(BF16)
            grad_pre_ref[:, columns] = grad_pre
            result = result + mm_t(grad_pre, ref[0, :, cut])
    for k in range(PLANE):
        outs[k][...] = result[k * CAP : (k + 1) * CAP].astype(BF16)


EXPERT_BACK = [shape((SLOTS, 2 * FFH), BF16)] + [shape((CAP, D), BF16)] * PLANE


def expert_grads_kernel(pair, *refs):
    if pair:
        blocks, (hidden_ref, grad_pre_ref, keep_ref, send_ref) = refs[:PLANE], refs[PLANE:]
        inputs = jnp.concatenate([block[0] for block in blocks], axis=0)
        grads = jnp.concatenate([block[1] for block in blocks], axis=0)
    else:
        blocks, (hidden_ref, grad_pre_ref, keep_ref, send_ref) = refs[: 2 * PLANE], refs[2 * PLANE :]
        inputs = jnp.concatenate([block[...] for block in blocks[:PLANE]], axis=0)
        grads = jnp.concatenate([block[...] for block in blocks[PLANE:]], axis=0)
    out_shift = jnp.sum(grads.astype(F32), axis=0, keepdims=True)
    out_shift = jnp.concatenate([out_shift, jnp.zeros((1, FFH - D), F32)], axis=1)
    inputs_t, grads_t = inputs.T, grads.T
    for half, ref in enumerate((keep_ref, send_ref)):
        shifts = []
        for chunk in range(FFH // CHUNK):
            cut = slice(chunk * CHUNK, (chunk + 1) * CHUNK)
            columns = slice(half * FFH + chunk * CHUNK, half * FFH + (chunk + 1) * CHUNK)
            grad_pre = grad_pre_ref[:, columns]
            ref[0:D, cut] = mm(inputs_t, grad_pre).astype(ref.dtype)
            ref[D : 2 * D, cut] = mm(grads_t, hidden_ref[:, columns]).astype(ref.dtype)
            shifts.append(jnp.sum(grad_pre.astype(F32), axis=0, keepdims=True))
        tail = [out_shift, jnp.concatenate(shifts, axis=1), jnp.zeros((SMALL - 2, FFH), F32)]
        ref[2 * D : 2 * D + SMALL, :] = jnp.concatenate(tail, axis=0).astype(ref.dtype)


def expert_grads_pair_kernel(*refs):
    expert_grads_kernel(True, *refs)


def expert_grads_owned_kernel(levels, place_ref, *refs):
    blocks, (hidden_ref, grad_pre_ref, out_ref) = refs[:PLANE], refs[PLANE:]
    inputs = jnp.concatenate([block[0] for block in blocks], axis=0)
    grads = jnp.concatenate([block[1] for block in blocks], axis=0)
    out_shift = jnp.sum(grads.astype(F32), axis=0, keepdims=True)
    out_shift = jnp.concatenate([out_shift, jnp.zeros((1, FFH - D), F32)], axis=1)
    size = D // levels
    inputs_t, grads_t = inputs.T, grads.T
    for half in range(2):
        shifts = []
        for chunk in range(FFH // CHUNK):
            cut = slice(chunk * CHUNK, (chunk + 1) * CHUNK)
            columns = slice(half * FFH + chunk * CHUNK, half * FFH + (chunk + 1) * CHUNK)
            grad_pre = grad_pre_ref[:, columns]
            sums = (mm(inputs_t, grad_pre), mm(grads_t, hidden_ref[:, columns]))
            for part in range(2):
                values = sums[part].astype(BF16)
                for level in range(levels):
                    out_ref[
                        2 * level + (place_ref[5] ^ half), part * size : (part + 1) * size, cut
                    ] = values[level * size : (level + 1) * size]
            shifts.append(jnp.sum(grad_pre.astype(F32), axis=0, keepdims=True))
        tail = [out_shift, jnp.concatenate(shifts, axis=1), jnp.zeros((SMALL - 2, FFH), F32)]
        tail = jnp.concatenate(tail, axis=0).astype(BF16)
        for level in range(levels):
            out_ref[2 * level + (place_ref[5] ^ half), 2 * size : 2 * size + SMALL, :] = tail


def expert_grads_single_kernel(*refs):
    expert_grads_kernel(False, *refs)


EXPERT_SUMS = [shape((2 * D + SMALL, FFH), BF16), shape((2 * D + SMALL, FFH), BF16)]


def spot_of(level, role):
    return role + PLANE * level


def rows_at(index, size, base=0):
    return pl.ds(base + pl.multiple_of(index * size, size), size)


def one_hot(me, extent, width, dtype=BF16):
    row = lax.broadcasted_iota(jnp.int32, (extent, width), 0)
    column = lax.broadcasted_iota(jnp.int32, (extent, width), 1)
    return jnp.where(row + me * extent == column, 1.0, 0.0).astype(dtype)


def pack_shard(layer, rows, me, refs, shard_ref):
    (gain1, bias1, shift, gain2, bias2, router, out_bias, qv, in_bias, qkv, output) = refs
    vectors = [ref[layer : layer + 1, :].astype(F32) for ref in (gain1, bias1, shift, gain2, bias2)]
    vectors = jnp.concatenate(vectors + [out_bias[layer].astype(F32)], axis=0)
    place = one_hot(me, rows, D)
    wide = mm(vectors.astype(BF16), place)
    router = mm(router[layer], place)
    shifts = mm(qv[layer], one_hot(me, qv.shape[2], HALF))
    shifts = jnp.concatenate([shifts[0:1], shifts[1:2]], axis=1)
    inner = mm(in_bias[layer], one_hot(me, in_bias.shape[2], FFH))
    left = [wide[0:1], wide[2:3], wide[4:5], router[0:1], router[2:3], wide[5:6], wide[7:8]]
    right = [wide[1:2], wide[3:4], shifts, router[1:2], router[3:4], wide[6:7], wide[8:9]]
    small = jnp.concatenate(
        [jnp.concatenate(left, axis=0), jnp.concatenate(right, axis=0)], axis=1
    )
    small = jnp.concatenate([small, inner, jnp.zeros((SMALL - 11, 2 * D), F32)], axis=0)
    shard_ref[rows : rows + SMALL, :] = small.astype(BF16)
    for part in range(3):
        shard_ref[0:rows, part * HALF : (part + 1) * HALF] = qkv[layer, part]
    shard_ref[0:rows, 3 * HALF : 4 * HALF] = output[layer]


def pack_kernel(rows, place_ref, *refs):
    first_ref, last_ref = refs[13:15]
    role = place_ref[1]
    expert_in, expert_out = refs[11:13]
    for layer in range(2):
        for k, ref in enumerate(refs[15 + layer * PLANE : 15 + (layer + 1) * PLANE]):
            ref[0:rows, :] = expert_in[layer, role ^ k]
            ref[rows : 2 * rows, :] = expert_out[layer, role ^ k]
    pack_shard(0, rows, place_ref[0], refs[:11], first_ref)
    pack_shard(1, rows, place_ref[0], refs[:11], last_ref)
    last_ref[rows + SMALL : rows + 2 * SMALL, :] = jnp.zeros((SMALL, 2 * D), BF16)


def stack_attention_kernel(rows, place_ref, *refs):
    pieces, out_ref = refs[:-1], refs[-1]
    high = place_ref[3]
    tail = jnp.zeros((SMALL, 2 * D), F32)
    for j, piece in enumerate(pieces):
        out_ref[rows_at(high ^ j, rows), :] = piece[0:rows, :]
        tail = tail + piece[rows : rows + SMALL, :].astype(F32)
    out_ref[len(pieces) * rows : len(pieces) * rows + SMALL, :] = tail.astype(BF16)


def join_attention_kernel(rows, depth, place_ref, *refs):
    pieces, out_ref = refs[:-1], refs[-1]
    low = place_ref[4]
    tail = jnp.zeros((SMALL, 2 * D), F32)
    for k, piece in enumerate(pieces):
        for high in range(depth):
            out_ref[rows_at(high * 4 + (low ^ k), rows), :] = piece[
                high * rows : (high + 1) * rows, :
            ]
        tail = tail + piece[depth * rows : depth * rows + SMALL, :].astype(F32)
    out_ref[D : D + SMALL, :] = tail.astype(BF16)


def join_gathered_kernel(rows, pieces_ref, out_ref, *sends):
    tail = jnp.zeros((SMALL, 2 * D), F32)
    for at in range(D // rows):
        piece = pieces_ref[at, 0:rows, :]
        out_ref[at * rows : (at + 1) * rows, :] = piece
        for half, ref in enumerate(sends):
            ref[at * rows : (at + 1) * rows, :] = piece[:, half * D : (half + 1) * D]
        tail = tail + pieces_ref[at, rows : rows + SMALL, :].astype(F32)
    out_ref[D : D + SMALL, :] = tail.astype(BF16)
    for half, ref in enumerate(sends):
        ref[D : D + SMALL, :] = tail[:, half * D : (half + 1) * D].astype(BF16)


def join_plane_kernel(rows, place_ref, *refs):
    pieces, outs = refs[:PLANE], refs[PLANE:]
    count = 2 * PLANE * rows
    for out_ref in outs:
        for k, piece in enumerate(pieces):
            out_ref[rows_at(place_ref[1] ^ k, 2 * rows), :] = piece[...]
        if out_ref.shape[0] > count:
            out_ref[count : count + SMALL, :] = jnp.zeros((SMALL, FFH), BF16)


def join_levels_kernel(rows, place_ref, *refs):
    pieces, outs = refs[:-2], refs[-2:]
    for j, piece in enumerate(pieces):
        for role in range(PLANE):
            at = rows_at(spot_of(place_ref[2] ^ j, role), rows)
            for part in range(2):
                first = (2 * role + part) * rows
                for out_ref in outs:
                    out_ref[part, at, :] = piece[first : first + rows, :]


def split_roles_kernel(rows, depth, keep_ref, got_ref, out_ref):
    for role in range(PLANE):
        for level in range(depth):
            first = spot_of(level, role) * rows
            at = slice(first, first + rows)
            out_ref[role, level * rows : (level + 1) * rows, :] = (
                keep_ref[at, :].astype(F32) + got_ref[at, :].astype(F32)
            ).astype(BF16)


def split_expert_kernel(rows, place_ref, keep_ref, got_ref, own_ref, far_ref, near_ref, next_ref):
    block = PLANE * rows
    low = slice(2 * D, 2 * D + SMALL)
    tail = keep_ref[low, :].astype(F32) + got_ref[low, :].astype(F32)
    for j, ref in ((3, far_ref), (1, near_ref), (2, next_ref), (0, own_ref)):
        for part in range(2):
            for role in range(PLANE):
                at = rows_at(spot_of(place_ref[2] ^ j, role), rows, part * D)
                first = part * block + role * rows
                ref[first : first + rows, :] = (
                    keep_ref[at, :].astype(F32) + got_ref[at, :].astype(F32)
                ).astype(ref.dtype)
        if j != 1:
            ref[2 * block : 2 * block + SMALL, :] = tail.astype(ref.dtype)


def add_kernel(own_ref, got_ref, out_ref):
    out_ref[...] = (own_ref[...].astype(F32) + got_ref[...].astype(F32)).astype(BF16)


def spread_expert_kernel(
    rows, place_ref, own_ref, far_ref, near_ref, next_ref, last_ref, *outs
):
    block = PLANE * rows
    base = 2 * block
    each = 2 * rows + SMALL
    tail = own_ref[base : base + SMALL, :].astype(F32) + far_ref[base : base + SMALL, :].astype(F32)
    tail = tail + next_ref[base : base + SMALL, :].astype(F32)
    for k, out in enumerate(outs):
        for part in range(2):
            at = rows_at(place_ref[1] ^ k, rows, part * block)
            first = part * rows
            out[first : first + rows, :] = (
                own_ref[at, :].astype(F32)
                + near_ref[at, :].astype(F32)
                + next_ref[at, :].astype(F32)
            ).astype(BF16)
            out[each + first : each + first + rows, :] = last_ref[at, :]
        out[2 * rows : each, :] = tail.astype(BF16)
        out[each + 2 * rows : 2 * each, :] = last_ref[base : base + SMALL, :]


def split_attention_kernel(rows, depth, place_ref, keep_ref, *refs):
    gots, outs = refs[: len(PARTS)], refs[len(PARTS) :]
    low = place_ref[4]
    for got_ref, cut in zip(gots, PARTS):
        tail = keep_ref[D : D + SMALL, cut].astype(F32) + got_ref[D : D + SMALL, :].astype(F32)
        for k, out in enumerate(outs):
            for high in range(depth):
                at = rows_at(high * 4 + (low ^ k), rows)
                out[high * rows : (high + 1) * rows, cut] = (
                    keep_ref[at, cut].astype(F32) + got_ref[at, :].astype(F32)
                ).astype(out.dtype)
            out[depth * rows : depth * rows + SMALL, cut] = tail.astype(out.dtype)


def spread_attention_kernel(rows, depth, place_ref, *refs):
    pieces, last_ref, (keep_ref, send_ref) = refs[:PLANE], refs[PLANE], refs[PLANE + 1 :]
    high = place_ref[3]
    base = depth * rows

    def summed(at):
        total = pieces[0][at, :]
        for piece in pieces[1:]:
            total = total + piece[at, :].astype(F32)
        return total

    tail = summed(slice(base, base + SMALL))
    for ref, flip in ((keep_ref, 0), (send_ref, 1)):
        for at in range(2):
            index = rows_at(high ^ (flip + 2 * at), rows)
            first = 2 * at * rows
            ref[first : first + rows, :] = summed(index).astype(ref.dtype)
            ref[first + rows : first + 2 * rows, :] = last_ref[index, :].astype(ref.dtype)
        ref[4 * rows : 4 * rows + SMALL, :] = tail.astype(ref.dtype)


def halve_attention_kernel(rows, own_ref, got_ref, keep_ref, send_ref):
    total = own_ref[...] + got_ref[...].astype(F32)
    tail = total[4 * rows : 4 * rows + SMALL]
    for ref, at in ((keep_ref, 0), (send_ref, 2 * rows)):
        ref[0 : 2 * rows, :] = total[at : at + 2 * rows].astype(ref.dtype)
        ref[2 * rows : 2 * rows + SMALL, :] = tail.astype(ref.dtype)


def exact(a, b):
    return lax.dot_general(
        a, b, (((1,), (1,)), ((), ())), precision=lax.Precision.HIGHEST, preferred_element_type=F32
    )


def own_attention(rows, me, first, tail, last, outs):
    gain1, bias1, qkv, qv, output, shift, gain2, bias2, router = outs
    for layer, body in enumerate((first, last)):
        for part in range(3):
            qkv[layer, part] = body[:, part * HALF : (part + 1) * HALF]
        output[layer] = body[:, 3 * HALF : 4 * HALF]
        small = tail[8 * layer : 8 * layer + 8]
        left = exact(small[:, 0:D], one_hot(me, rows, D, F32))
        right = exact(small[:, D : 2 * D], one_hot(me, rows, D, F32))
        for ref, values, row in (
            (gain1, left, 0),
            (bias1, right, 0),
            (shift, left, 1),
            (gain2, right, 1),
            (bias2, left, 2),
        ):
            ref[layer : layer + 1, :] = values[row : row + 1]
        for e in range(EXPERTS):
            values = (left, right)[e % 2]
            router[layer, e : e + 1, :] = values[3 + e // 2 : 4 + e // 2]
        width = qv.shape[2]
        for part in range(2):
            values = exact(
                small[:, D + part * HALF : D + (part + 1) * HALF], one_hot(me, width, HALF, F32)
            )
            qv[layer, part : part + 1, :] = values[2:3]


def own_attention_kernel(rows, place_ref, own_ref, got_ref, *outs):
    total = own_ref[...] + got_ref[...].astype(F32)
    tail = total[2 * rows : 2 * rows + SMALL]
    own_attention(rows, place_ref[0], total[0:rows], tail, total[rows : 2 * rows], outs)


def own_experts_kernel(rows, place_ref, *refs):
    pieces = refs[:PLANE]
    inner_ref, in_bias_ref, outer_ref, out_bias_ref = refs[PLANE:]
    each = 2 * rows + SMALL
    me, role = place_ref[0], place_ref[1]
    in_place = one_hot(me, in_bias_ref.shape[2], FFH)
    out_place = one_hot(me, rows, D)
    for layer in range(2):
        for k in range(PLANE):
            piece = pieces[k].at[layer * each : (layer + 1) * each]
            expert = role ^ k
            inner_ref[layer, expert] = piece[0:rows, :].astype(F32)
            outer_ref[layer, expert] = piece[rows : 2 * rows, :].astype(F32)
            tail = piece[2 * rows : 2 * rows + SMALL, :]
            out_bias_ref[layer, pl.ds(expert, 1), :] = mm_t(tail[:, 0:D], out_place)[0:1]
            in_bias_ref[layer, pl.ds(expert, 1), :] = mm_t(tail, in_place)[1:2]


class Order:
    def __init__(self, place):
        self.last = ()
        self.place = place

    def run(self, kernel, out_shape, operands, name, fixed=(), place=True, through=()):
        count = len(out_shape)
        fars = [at for at in range(count) if not isinstance(out_shape[at], jax.ShapeDtypeStruct)]
        if not fars:
            out_shape = [*out_shape, shape((8, 128), F32)]

        def body(*refs):
            if fars:
                kernel(*fixed, *refs)
            else:
                kernel(*fixed, *refs[:-1])
                refs[-1][...] = jnp.zeros((8, 128), F32)

        if place:
            operands = (self.place, *operands)
        outs = list(call(body, out_shape, operands, name, self.last, through, int(place)))
        if fars:
            sized = [outs[at] for at in fars]
            token = far(min(sized, key=lambda out: out.size * out.dtype.itemsize))
        else:
            token = outs.pop(count)
        self.last = (token,)
        return outs

    def gate(self, through):
        def kernel(place_ref, out_ref):
            out_ref[...] = jnp.zeros_like(out_ref)

        return self.run(kernel, [shape((8, 128), F32)], (), "gate", through=through)[1:]

    def main(self, kernel, out_shape, operands, name, through=(), place=False):
        outs = self.run(kernel, out_shape, operands, name, (), place, through)
        count = len(out_shape)
        return outs[:count], outs[count:]


class Moves:
    def __init__(self, dp, order, me, role, level):
        self.dp, self.order = dp, order
        self.me, self.role, self.level = me, role, level
        self.depth, self.rows = dp // PLANE, D // dp

    def swap(self, x, mask):
        return lax.ppermute(x, "dp", [(i, i ^ mask) for i in range(self.dp)])

    def swap_core(self, x):
        return lax.ppermute(x, "tensor", [(0, 1), (1, 0)])

    def kept(self, x):
        return far(x)

    def to_role(self, x, k):
        return self.swap(x, spot_of(0, k))

    def to_level(self, x, j):
        return self.swap(x, spot_of(j, 0))

    def exchange(self, blocks):
        return [blocks[0]] + [self.to_role(blocks[k], k) for k in range(1, PLANE)]


class FastMoves(Moves):
    def one(self, *args, **kwargs):
        return self.order.run(*args, **kwargs)[0]

    def begin(self, weights):
        rows = self.rows
        outs = [shape((rows + SMALL, 2 * D), BF16), shape((rows + 2 * SMALL, 2 * D), BF16)]
        outs += [shape((2 * rows, FFH), BF16)] * (2 * PLANE)
        first, last, *sends = self.order.run(
            pack_kernel, outs, all_far(weights), "pack", (rows,)
        )
        exp0 = self.exchange(sends[:PLANE])
        att0 = [first] + [self.swap(first, 4 * j) for j in range(1, self.depth)]
        return att0, exp0, lax.all_gather(last, "dp"), sends[PLANE:]

    def groups(self, index):
        firsts = {}
        for level in range(self.depth):
            for role in range(PLANE):
                key = level if index == 0 else role
                firsts.setdefault(key, []).append(spot_of(level, role))
        return list(firsts.values())

    def plane0(self, pieces):
        out = [shape((2 * PLANE * self.rows, FFH), BF16)]
        own = self.one(join_plane_kernel, out, pieces, "join_plane", (self.rows,))
        return [own, self.to_level(own, 1), self.to_level(own, 2)]

    def stack0(self, pieces):
        out = [shape((self.depth * self.rows + SMALL, 2 * D), BF16)]
        message = self.one(stack_attention_kernel, out, pieces, "stack_attention", (self.rows,))
        return [message] + [self.swap(message, k) for k in range(1, 4)]

    def join0(self, pieces, exp0, exp1, given):
        out = [far_shape((D + SMALL, 2 * D), BF16)]
        fixed = (self.rows, self.depth)
        own, near, next_, *rest = self.order.run(
            join_attention_kernel,
            out,
            pieces,
            "join_attention",
            fixed,
            through=[*exp0[1:3], *exp1[1:], *given],
        )
        sends, given = rest[: PLANE - 1], rest[PLANE - 1 :]
        exp0 = [exp0[0], near, next_, self.to_level(next_, 1)]
        return (own, self.swap_core(own)), exp0, self.exchange([exp1[0], *sends]), given

    def plane1(self, pieces):
        count = 2 * PLANE * self.rows
        out = [shape((count + SMALL, FFH), BF16), shape((count, FFH), BF16)]
        return self.order.run(join_plane_kernel, out, pieces, "join_plane", (self.rows,))

    def forward(self, piece):
        return self.to_level(piece, 1)

    def join_last(self, gathered):
        out = [far_shape((D + SMALL, 2 * D), BF16)] + [shape((D + SMALL, D), BF16)] * 2
        own, left, right = self.order.run(
            join_gathered_kernel, out, (far(gathered),), "join_gathered", (self.rows,), False
        )
        return own, self.swap_core(left), self.swap_core(right)

    def join_levels(self, pieces, through=()):
        out = [far_shape((2, D, FFH), BF16), shape((2, D, FFH), BF16)]
        own, send, *through = self.order.run(
            join_levels_kernel, out, all_far(pieces), "join_levels", (self.rows,), through=through
        )
        return (own, self.swap_core(send)), through

    def last_attention_1(self, operands):
        (keep, send), _ = self.order.main(
            attention_grads_kernel,
            [shape((D, 2 * D), BF16)] * 2,
            operands,
            "attention_grads1",
        )
        return keep, self.swap_core(send)

    def last_expert(self, operands):
        out = [far_shape((2 * self.depth, 2 * PLANE * self.rows + SMALL, FFH), BF16)]
        sums = self.one(
            expert_grads_owned_kernel, out, operands, "expert_grads1", (self.depth,)
        )
        groups = [
            [2 * member + core for member in group for core in range(2)]
            for group in self.groups(1)
        ]
        return lax.psum_scatter(
            sums, ("dp", "tensor"), scatter_dimension=0, axis_index_groups=groups
        )

    def last_attention_2(self, keep, got):
        out = [far_shape((PLANE, self.depth * self.rows, 2 * D), BF16)]
        fixed = (self.rows, self.depth)
        sums = self.one(split_roles_kernel, out, (keep, got), "split_roles", fixed, False)
        return lax.psum_scatter(
            sums, "dp", scatter_dimension=0, axis_index_groups=self.groups(0)
        )

    def expert_sum_2(self, keep, got, through=()):
        count = 2 * PLANE * self.rows
        outs = [
            far_shape((count + SMALL, FFH), BF16),
            shape((count + SMALL, FFH), BF16),
            shape((count, FFH), BF16),
            far_shape((count + SMALL, FFH), BF16),
        ]
        own, third, near, next_, *through = self.order.run(
            split_expert_kernel, outs, (keep, got), "split_expert", (self.rows,), through=through
        )
        return [own, self.to_level(third, 1), self.to_level(near, 1), next_], through

    def expert_sum_3(self, state):
        own, third, near, next_ = state
        message = self.one(
            add_kernel,
            [shape(third.shape, BF16)],
            (far(next_), third),
            "add_expert",
            place=False,
        )
        return [own, third, near, self.to_level(message, 2)]

    def expert_sum_4(self, state, last, through=()):
        outs = [shape((2 * (2 * self.rows + SMALL), FFH), BF16)] * PLANE
        state = (*state, last.reshape(2 * PLANE * self.rows + SMALL, FFH))
        blocks = self.order.run(
            spread_expert_kernel,
            outs,
            all_far(state),
            "spread_expert",
            (self.rows,),
            through=through,
        )
        return self.exchange(blocks[:PLANE]), blocks[PLANE:]

    def attention_sum_1(self, keep, sends):
        return keep, [self.swap_core(send) for send in sends]

    def attention_sum_2(self, state, through):
        dims = (self.depth * self.rows + SMALL, 2 * D)
        outs = [far_shape(dims, F32)] + [shape(dims, BF16)] * 3
        fixed = (self.rows, self.depth)
        operands = (far(state[0]), *state[1])
        blocks = self.order.run(
            split_attention_kernel, outs, operands, "split_attention", fixed, through=through
        )
        return [blocks[0]] + [self.swap(blocks[k], k) for k in range(1, 4)], blocks[4:]

    def attention_sum_3(self, pieces, last, through=()):
        outs = [
            shape((4 * self.rows + SMALL, 2 * D), F32),
            shape((4 * self.rows + SMALL, 2 * D), BF16),
        ]
        fixed = (self.rows, self.depth)
        operands = all_far((*pieces, last.reshape(self.depth * self.rows, 2 * D)))
        keep, send, *through = self.order.run(
            spread_attention_kernel, outs, operands, "spread_attention", fixed, through=through
        )
        return (keep, self.swap(send, 4)), through

    def attention_sum_4(self, state):
        outs = [
            shape((2 * self.rows + SMALL, 2 * D), F32),
            shape((2 * self.rows + SMALL, 2 * D), BF16),
        ]
        keep, send = self.order.run(
            halve_attention_kernel, outs, state, "halve_attention", (self.rows,), False
        )
        return keep, self.swap(send, 8)

    def own_attention(self, pieces):
        rows, dp = self.rows, self.dp
        outs = [
            shape((2, rows), F32),
            shape((2, rows), F32),
            shape((2, 3, rows, HALF), F32),
            shape((2, 2, HALF // dp), F32),
            shape((2, rows, HALF), F32),
            shape((2, rows), F32),
            shape((2, rows), F32),
            shape((2, rows), F32),
            shape((2, EXPERTS, rows), F32),
        ]
        return self.order.run(
            own_attention_kernel, outs, pieces, "own_attention", (rows,)
        )

    def own_experts(self, pieces):
        rows = self.rows
        outs = [
            shape((2, EXPERTS, rows, FFH), F32),
            shape((2, EXPERTS, FFH // self.dp), F32),
            shape((2, EXPERTS, rows, FFH), F32),
            shape((2, EXPERTS, rows), F32),
        ]
        return self.order.run(own_experts_kernel, outs, pieces, "own_experts", (rows,))


class PlainMoves(Moves):
    def kept(self, x):
        return x

    def by_index(self, pieces, me):
        return jnp.take(jnp.stack(pieces), me ^ jnp.arange(len(pieces)), axis=0)

    def relative(self, array, me, axis):
        return jnp.take(array, me ^ jnp.arange(array.shape[axis]), axis=axis)

    def spots(self):
        return [spot_of(j, k) for j in range(self.depth) for k in range(PLANE)]

    def total(self, pieces):
        return sum(piece.astype(F32) for piece in pieces)

    def pack(self, layer, weights):
        (
            norm1_gain,
            norm1_bias,
            output_bias,
            norm2_gain,
            norm2_bias,
            router_weight,
            expert_out_bias,
            qv_bias,
            expert_in_bias,
            qkv_weight,
            output_weight,
            expert_in,
            expert_out,
        ) = [weight[layer] for weight in weights]
        vectors = (norm1_gain, norm1_bias, output_bias, norm2_gain, norm2_bias)

        def placed(values, width):
            extent = values.shape[-1]
            column = jnp.arange(extent)[:, None] + self.me * extent
            spot = (column == jnp.arange(width)[None, :]).astype(BF16)
            return jnp.dot(values, spot, preferred_element_type=F32).astype(BF16)

        wide = placed(jnp.stack(vectors), D)
        router = placed(router_weight, D)
        shifts = placed(qv_bias, HALF).reshape(1, D)
        outer = placed(expert_out_bias, D)
        small = jnp.concatenate([wide, shifts, router, outer], axis=0).reshape(7, 2 * D)
        inner = placed(expert_in_bias, FFH)
        body = jnp.concatenate([*qkv_weight, output_weight], axis=1)
        blank = jnp.zeros((SMALL - 11, 2 * D), BF16)
        shard = jnp.concatenate([body, small, inner, blank], axis=0)
        experts = jnp.stack([expert_in, expert_out], axis=1)
        return shard, list(self.relative(experts, self.role, 0))

    def begin(self, weights):
        shard0, sends0 = self.pack(0, weights)
        shard1, sends1 = self.pack(1, weights)
        return shard0, [jnp.stack(sends0)], shard1, [jnp.stack(sends1)]

    def plane0(self, pieces):
        return pieces * 3

    def plane1(self, pieces):
        return pieces * 2

    def stack0(self, shard):
        return shard

    def join0(self, shard, exp0, exp1, given):
        own, left, right = self.join_last(shard)
        return (own, jnp.concatenate([left, right], axis=1)), exp0, exp1, given

    def forward(self, piece):
        return piece

    def join_last(self, shard):
        gathered = lax.all_gather(shard, "dp")
        body = gathered[:, : self.rows].reshape(D, 2 * D)
        tail = jnp.sum(gathered[:, self.rows :].astype(F32), axis=0).astype(BF16)
        own = jnp.concatenate([body, tail], axis=0)
        other = self.swap_core(own)
        return own, other[:, :D], other[:, D:]

    def join_levels(self, pieces, through=()):
        body = self.by_index(self.exchange(list(pieces[0])), self.role)
        pieces = [body] + [self.to_level(body, j) for j in range(1, self.depth)]
        stacked = self.by_index(pieces, self.level).reshape(self.dp, 2, self.rows, FFH)
        order = sorted(range(self.dp), key=lambda at: self.spots()[at])
        own = stacked[jnp.array(order)].transpose(1, 0, 2, 3).reshape(2, D, FFH)
        return (own, self.swap_core(own)), through

    def expert_sum_2(self, keep, got, through=()):
        return [keep, got, got, got], through

    def expert_sum_3(self, state):
        return state

    def expert_sum_4(self, state, last, through=()):
        return (self.sum_expert(*state[:2]), self.sum_expert(*last)), through

    def sum_expert(self, keep, got):
        rows, depth = self.rows, self.depth
        whole = keep.astype(F32) + got.astype(F32)
        tail = whole[2 * D :]
        body = whole[: 2 * D].reshape(2, self.dp, rows, FFH)[:, jnp.array(self.spots())]
        body = self.relative(body.reshape(2, depth, PLANE * rows, FFH), self.level, 1)
        low, low_tail = body.astype(BF16), tail.astype(BF16)
        count = 2 * PLANE * rows
        pieces = []
        for j in range(1, depth):
            message = jnp.concatenate([low[:, j].reshape(count, FFH), low_tail], axis=0)
            pieces.append(self.to_level(message, j))
        body = body[:, 0].reshape(count, FFH) + self.total([piece[:count] for piece in pieces])
        tail = tail + self.total([piece[count:] for piece in pieces])
        body = self.relative(body.reshape(2, PLANE, rows, FFH), self.role, 1).astype(BF16)
        tail = tail.astype(BF16)
        count = 2 * rows
        blocks = [
            jnp.concatenate([body[:, k].reshape(count, FFH), tail], axis=0) for k in range(PLANE)
        ]
        return self.exchange(blocks)

    def attention_sum_1(self, keep, sends):
        return keep, jnp.concatenate(sends, axis=1)

    def attention_sum_2(self, state, through):
        return state, through

    def attention_sum_3(self, state, last, through=()):
        return (state, last), through

    def attention_sum_4(self, state):
        (keep, send), last = state
        whole = keep + self.swap_core(send).astype(F32)
        body = lax.psum_scatter(whole[:D], "dp", scatter_dimension=0, tiled=True)
        return jnp.concatenate([body, lax.psum(whole[D:], "dp")], axis=0), last

    def last_attention_1(self, operands):
        (keep, send), _ = self.order.main(
            attention_grads_kernel,
            [shape((D, 2 * D), F32), shape((D, 2 * D), BF16)],
            operands,
            "attention_grads1",
        )
        return keep, self.swap_core(send)

    def last_expert(self, operands):
        (keep, send), _ = self.order.main(
            expert_grads_pair_kernel, EXPERT_SUMS, operands, "expert_grads1"
        )
        return keep, self.swap_core(send)

    def last_attention_2(self, keep, got):
        whole = keep + got.astype(F32)
        return lax.psum_scatter(whole, "dp", scatter_dimension=0, tiled=True)

    def own_attention(self, state):
        total, last = state
        rows = self.rows
        body = jnp.stack([total[:rows], last])
        tail = total[rows:].reshape(2, 16, D)

        def owned(values, width):
            return lax.dynamic_slice_in_dim(
                values, self.me * width, width, axis=values.ndim - 1
            )

        wide = owned(tail, rows)
        qkv = body[:, :, : 3 * HALF].reshape(2, rows, 3, HALF).transpose(0, 2, 1, 3)
        qv = owned(tail[:, 5].reshape(2, 2, HALF), HALF // self.dp)
        vectors = [wide[:, row] for row in range(5)]
        return (
            *vectors[:2],
            qkv,
            qv,
            body[:, :, 3 * HALF :],
            *vectors[2:],
            wide[:, 6:10],
        )

    def own_experts(self, state):
        first, last = state
        rows = self.rows
        owned = jnp.stack([self.by_index(first, self.role), self.by_index(last, self.role)])
        owned = owned.astype(F32)
        tail = owned[:, :, 2 * rows :]
        width = FFH // self.dp
        in_bias = lax.dynamic_slice_in_dim(tail[:, :, 1], self.me * width, width, axis=2)
        out_bias = lax.dynamic_slice_in_dim(tail[:, :, 0], self.me * rows, rows, axis=2)
        return owned[:, :, :rows], in_bias, owned[:, :, rows : 2 * rows], out_bias


def build(dp):
    def local(
        tokens,
        routes,
        norm1_gain,
        norm1_bias,
        qkv_weight,
        qv_bias,
        output_weight,
        output_bias,
        norm2_gain,
        norm2_bias,
        router_weight,
        expert_in,
        expert_in_bias,
        expert_out,
        expert_out_bias,
        grad_out,
    ):
        me = lax.axis_index("dp").astype(jnp.int32)
        core = lax.axis_index("tensor")
        role, level = me % PLANE, me // PLANE
        order = Order(
            jnp.stack([me, role, level, me // 4, me % 4, core.astype(jnp.int32)])
        )
        moves = (FastMoves if dp == 16 else PlainMoves)(dp, order, me, role, level)
        weights = (
            norm1_gain,
            norm1_bias,
            output_bias,
            norm2_gain,
            norm2_bias,
            router_weight.transpose(0, 2, 1),
            expert_out_bias,
            qv_bias,
            expert_in_bias,
            qkv_weight.transpose(0, 2, 1, 3),
            output_weight.transpose(0, 2, 1),
            expert_in,
            expert_out.transpose(0, 1, 3, 2),
        )

        att0, exp0, gathered1, exp1 = moves.begin(weights)

        choice = lax.dynamic_index_in_dim(routes, core, axis=1, keepdims=False)
        hot = (choice[..., None] == jnp.arange(EXPERTS)).astype(BF16)
        any_hot = hot[:, :, 0] + hot[:, :, 1]
        below = jnp.tril(jnp.ones((SEQ, SEQ), BF16), -1)
        slot = jnp.einsum("ts,lse->lte", below, any_hot, preferred_element_type=F32)
        slot = jnp.sum(hot.astype(F32) * slot[:, :, None], axis=-1).astype(jnp.int32)
        target = (choice ^ role) * CAP + slot
        columns = jnp.pad(
            jnp.concatenate([target, choice], axis=-1),
            ((0, 0), (0, SP - SEQ), (0, 0)),
            constant_values=-1,
        )
        target_rows = columns[:, :, 0:2].transpose(0, 2, 1)

        def image(values):
            values = lax.dynamic_index_in_dim(values, core, axis=0, keepdims=False)
            return jnp.pad(values, ((0, SP - SEQ), (0, 0)))

        rows, grad = image(tokens), image(grad_out)

        exp0 = moves.plane0(exp0)
        att0 = moves.stack0(att0)
        given = [rows, grad, columns[0], columns[1], target_rows[0], target_rows[1]]
        attention0, exp0, exp1, given = moves.join0(att0, exp0, exp1, given)
        rows, grad, columns, target_rows = given[0], given[1], given[2:4], given[4:6]

        kept0, _ = order.main(
            first_forward_kernel,
            forward_outs(False),
            (rows, far(attention0[0]), attention0[1], columns[0], target_rows[0]),
            "attention_first",
        )
        middle0, normed0, normed2_0, qkv0, mixed0, log0, probs0, small0 = kept0[:8]
        blocks0 = moves.exchange(kept0[8:])
        expert0, exp1[1:] = moves.join_levels(exp0, exp1[1:])
        exp1, early1 = moves.plane1(exp1)
        next1 = moves.to_level(early1, 2)
        (hidden0, slope0, *results), (exp1,) = order.main(
            expert_forward_kernel,
            expert_outs(False),
            (*blocks0, *all_far(expert0), small0),
            "expert_forward",
            [exp1],
            place=True,
        )
        slots0 = moves.exchange(results)
        near1 = moves.to_level(exp1, 1)
        next1, gathered1, *slots0[1:] = order.gate([next1, moves.kept(gathered1), *slots0[1:]])
        exp1 = [exp1, near1, next1, moves.forward(next1)]
        attention1 = moves.join_last(gathered1)

        (rows1, *kept1), _ = order.main(
            last_forward_kernel,
            [far_shape((SP, D), F32)] + forward_outs(True),
            (
                *all_far((middle0, probs0)),
                columns[0],
                *all_far(slots0),
                grad,
                *all_far(attention1),
                columns[1],
                target_rows[1],
            ),
            "attention_last",
        )
        middle1, normed1, normed2_1, qkv1, mixed1, log1, probs1, small1 = kept1[:8]
        blocks1 = moves.exchange(kept1[8:])
        expert1, _ = moves.join_levels(exp1)
        (hidden1, grad_pre1, *results), _ = order.main(
            expert_both_kernel,
            expert_outs(True),
            (*blocks1, *expert1, small1),
            "expert_both",
            place=True,
        )
        pairs1 = moves.exchange(results)
        sums1 = moves.last_expert((*all_far(blocks1), hidden1, grad_pre1))
        back1, _ = order.main(
            backward_last_kernel,
            backward_outs(True),
            (
                grad,
                *pairs1,
                *all_far((rows1, middle1, normed2_1, qkv1, mixed1, log1, probs1)),
                columns[1],
                *all_far(attention1),
                far(probs0),
                columns[0],
                target_rows[0],
            ),
            "attention_back_last",
        )
        grad_rows1, grad_qkv1, grad_att1, keep1, send1, output = back1[:6]
        grads0 = moves.exchange(back1[6:])
        output_got = moves.swap_core(output)
        att_owned1 = moves.last_attention_1((far(normed1), grad_qkv1, grad_att1, far(mixed1)))

        att_owned1 = moves.last_attention_2(*att_owned1)
        (grad_pre0, *results), (output_got,) = order.main(
            expert_back_kernel,
            EXPERT_BACK,
            all_far((*grads0, slope0, *expert0)),
            "expert_back",
            [output_got],
        )
        slot_grads0 = moves.exchange(results)
        sums0, _ = order.main(
            expert_grads_single_kernel,
            EXPERT_SUMS,
            all_far((*blocks0, *grads0, hidden0)) + [grad_pre0],
            "expert_grads0",
        )
        sums0, slot_grads0[1:] = moves.expert_sum_2(
            sums0[0], moves.swap_core(sums0[1]), slot_grads0[1:]
        )
        (grad_rows0, grad_qkv0, grad_att0, keep0, send0), _ = order.main(
            backward_first_kernel,
            backward_outs(False),
            (
                far(grad_rows1),
                *all_far(slots0),
                *slot_grads0,
                rows,
                *all_far((middle0, normed2_0, qkv0, mixed0, log0, probs0)),
                columns[0],
                *all_far(attention0),
            ),
            "attention_back_first",
        )
        att_sums0, _ = order.main(
            attention_grads_small_kernel,
            ATTENTION_SUMS,
            (
                far(normed0),
                grad_qkv0,
                grad_att0,
                far(mixed0),
                keep0,
                send0,
                far(keep1),
                far(send1),
            ),
            "attention_grads0",
        )

        att_sums0 = moves.attention_sum_1(att_sums0[0], att_sums0[1:])
        sums0 = moves.expert_sum_3(sums0)
        att_sums0, (sums1,) = moves.attention_sum_2(att_sums0, [moves.kept(sums1)])
        att_sums0, _ = moves.attention_sum_3(att_sums0, att_owned1)
        sums0, (grad_rows0,) = moves.expert_sum_4(sums0, sums1, [grad_rows0])
        att_sums0 = moves.attention_sum_4(att_sums0)
        rows_got = moves.swap_core(grad_rows0)
        gain1, bias1, qkv, qv, out, shift, gain2, bias2, router = moves.own_attention(att_sums0)
        inner, in_bias, outer, out_bias = moves.own_experts(sums0)

        def both(values, others):
            first = jnp.where(core == 0, values, others)[:SEQ]
            second = jnp.where(core == 0, others, values)[:SEQ]
            return jnp.stack([first, second], axis=1).transpose(1, 0, 2)

        return (
            both(output, output_got),
            both(grad_rows0, rows_got),
            gain1,
            bias1,
            qkv.transpose(0, 2, 1, 3),
            qv,
            out.transpose(0, 2, 1),
            shift,
            gain2,
            bias2,
            router.transpose(0, 2, 1),
            inner,
            in_bias,
            outer.transpose(0, 1, 3, 2),
            out_bias,
        )

    return local


def solution(mesh):
    weights = (
        P(None, "dp"),
        P(None, "dp"),
        P(None, "dp", None, "tensor"),
        P(None, None, ("tensor", "dp")),
        P(None, "tensor", "dp"),
        P(None, "dp"),
        P(None, "dp"),
        P(None, "dp"),
        P(None, "dp", None),
        P(None, None, "dp", "tensor"),
        P(None, None, ("tensor", "dp")),
        P(None, None, "tensor", "dp"),
        P(None, None, "dp"),
    )
    images = P("dp", None, None)
    return jax.shard_map(
        build(mesh.shape["dp"]),
        mesh=mesh,
        in_specs=(images, P(None, "dp", None, None)) + weights + (images,),
        out_specs=(images, images) + weights,
        check_vma=False,
    )
```
